32 devices in a mesh: dp: 4 (over x, core), row: 2 (over y), col: 4 (over z).
Axes of the slice: x: 2, y: 2, z: 4, core: 2. Of those that a mesh axis runs over, the one named last changes fastest.
Arguments:
- tokens: bfloat16 [16384, 1024], P(('dp', 'col'), 'row'), may hold values from -6 to 6
- segment_ids: int32 [16384], P(('dp', 'row')), may hold values from 0 to 302, as said below
- cotangent: bfloat16 [16384, 1024], P(('dp', 'col'), 'row'), may hold values from -6 to 6
- norm1_gain: bfloat16 [1024], P('row'), may hold values from 0.5 to 1.5
- in_weight: bfloat16 [1024, 3, 1024], P('row', None, 'col'), may hold values from -0.1875 to 0.1875
- conv_weight: bfloat16 [3, 1024], P(None, 'col'), may hold values from -3.5 to 3.5
- out_weight: bfloat16 [1024, 1024], P('col', 'row'), may hold values from -0.1875 to 0.1875
- norm2_gain: bfloat16 [1024], P('row'), may hold values from 0.5 to 1.5
- gate_weight: bfloat16 [1024, 4608], P('row', 'col'), may hold values from -0.1875 to 0.1875
- up_weight: bfloat16 [1024, 4608], P('row', 'col'), may hold values from -0.1875 to 0.1875
- down_weight: bfloat16 [4608, 1024], P('col', 'row'), may hold values from -0.09375 to 0.09375
Outputs:
- output: bfloat16 [16384, 1024], P(('dp', 'col'), 'row')
- input_grad: float32 [16384, 1024], P(('dp', 'col'), 'row')
- norm1_grad: float32 [1024], P('row')
- in_grad: float32 [1024, 3, 1024], P('row', None, 'col')
- conv_grad: float32 [3, 1024], P(None, 'col')
- out_grad: float32 [1024, 1024], P('col', 'row')
- norm2_grad: float32 [1024], P('row')
- gate_grad: float32 [1024, 4608], P('row', 'col')
- up_grad: float32 [1024, 4608], P('row', 'col')
- down_grad: float32 [4608, 1024], P('col', 'row')
The draws below stay inside these ranges and needn't reach their ends.
Inputs may be any that keep to these rules, and one draw needn't show every extreme that they name: `segment_ids`: segment numbers never fall along the tokens; a run of one number never crosses a boundary between the sequences of 1024 tokens, and every run but a sequence's last has 60 to 800 tokens.
All inputs are finite; a program needn't handle non-finite values.
Results may differ from the reference program's by a relative error of at most 0.012.
Values may be sent and summed in bfloat16 or wider, within the bound.
No kernel may reach another device: no remote copies, remote signals or barrier semaphores. Data moves between devices by JAX's collectives and lax.ppermute only.
A program may use at most 256 MiB of HBM per device.

```python
from functools import partial
import jax
import jax.numpy as jnp
from jax import lax

D = 1024
FF = 4608
SEQ = 1024
DOC_LO = 60
DOC_HI = 800
TOK_DP = 4096
TOKENS = 16384
N_DP = 4


def draw_segment_ids(key, part):
    key = jax.random.fold_in(key, 11)
    sequences = TOKENS // SEQ
    columns = SEQ // DOC_LO + 1
    lengths = jax.random.randint(key, (sequences, columns), DOC_LO, DOC_HI + 1)
    bounds = jnp.cumsum(lengths, axis=1)
    places = jnp.arange(SEQ)
    document = jnp.sum((places[None, :, None] >= bounds[:, None, :]).astype(jnp.int32), axis=2)
    last_doc = document[:, -1:]
    later = (jnp.arange(sequences) > 0).astype(jnp.int32)[:, None]
    document = document + (columns - 1 - last_doc) * later
    starts = jnp.arange(sequences)[:, None] * (columns + 1)
    return (document + starts).reshape(TOKENS).astype(jnp.int32)


def levels(rng, shape, shards, low, largest):
    gain = 1.0
    for axis_at, blocks in shards:
        steps = jax.random.uniform(jax.random.fold_in(jax.random.fold_in(rng, 6), axis_at), (blocks,), jnp.float32, low / len(shards), largest / len(shards))
        gain = gain * jnp.repeat(jnp.exp(steps), shape[axis_at] // blocks).reshape((-1,) + (1,) * (len(shape) - 1 - axis_at))
    return gain


def scatter_about(key, dims, width, bound, pieces=(), kind=jnp.bfloat16):
    array = width * jax.random.normal(key, dims, jnp.float32)
    if pieces:
        array = array * levels(key, dims, pieces, -0.22, 0.18)
    return jnp.clip(array, -bound, bound).astype(kind)


def setup_inputs(seed: int = 0) -> dict:
    splits = jax.random.split(jax.random.key(seed), 12)
    return {
        "tokens": scatter_about(splits[0], (TOKENS, D), 1.0, 6.0, ((0, 16), (1, 2))),
        "segment_ids": draw_segment_ids(jax.random.fold_in(splits[11], 71), 0),
        "cotangent": scatter_about(splits[2], (TOKENS, D), 1.0, 6.0, ((0, 16), (1, 2))),
        "norm1_gain": jnp.clip(1.0 + 0.1 * jax.random.normal(splits[3], (D,), jnp.float32), 0.5, 1.5).astype(jnp.bfloat16),
        "in_weight": scatter_about(splits[4], (D, 3, D), D ** -0.5, 0.1875, ((0, 2), (2, 4))),
        "conv_weight": scatter_about(splits[5], (3, D), 3 ** -0.5, 3.5, ((1, 4),)),
        "out_weight": scatter_about(splits[6], (D, D), D ** -0.5, 0.1875, ((0, 4), (1, 2))),
        "norm2_gain": jnp.clip(1.0 + 0.1 * jax.random.normal(splits[7], (D,), jnp.float32), 0.5, 1.5).astype(jnp.bfloat16),
        "gate_weight": scatter_about(splits[8], (D, FF), D ** -0.5, 0.1875, ((0, 2), (1, 4))),
        "up_weight": scatter_about(splits[9], (D, FF), D ** -0.5, 0.1875, ((0, 2), (1, 4))),
        "down_weight": scatter_about(splits[10], (FF, D), FF ** -0.5, 0.09375, ((0, 4), (1, 2))),
    }


@jax.custom_vjp
def low(v):
    return lax.optimization_barrier(v.astype(jnp.bfloat16)).astype(jnp.float32)

@jax.custom_vjp
def low_back(v):
    return v

def low_keep(v):
    return (low(v), None)

def low_pass(kept, grad):
    return (grad,)

def back_keep(v):
    return (v, None)

def back_low(kept, grad):
    return (low(grad),)
low.defvjp(low_keep, low_pass)
low_back.defvjp(back_keep, back_low)
EPSILON = 1e-05

def matmul(left, right):
    return jnp.dot(left, right, precision=lax.Precision.HIGHEST)

def shifted(values, offset):
    filler = jnp.zeros((offset,) + values.shape[1:], values.dtype)
    return jnp.concatenate([filler, values[:-offset]], axis=0)

def same_segment(segments, offset):
    equal = (segments[offset:] == segments[:-offset]).astype(jnp.float32)
    return jnp.concatenate([jnp.zeros((offset,), jnp.float32), equal])[:, None]

def forward(segments, inputs, gain_one, mixer_in, conv_taps, mixer_out, gain_two, gate_proj, up_proj, down_proj):
    model_width = inputs.shape[1]
    scale_one = lax.rsqrt(lax.optimization_barrier(jnp.mean(inputs * inputs, axis=1, keepdims=True)) + EPSILON)
    normed_one = low(inputs * scale_one * gain_one)
    projected = low_back(matmul(normed_one, mixer_in.reshape(model_width, 3 * model_width)))
    input_gate = projected[:, :model_width]
    output_gate = projected[:, model_width:2 * model_width]
    values_part = projected[:, 2 * model_width:]
    mix_input = input_gate * values_part
    keep_one = same_segment(segments, 1)
    keep_two = same_segment(segments, 2)
    convolved = conv_taps[2] * mix_input + conv_taps[1] * keep_one * shifted(mix_input, 1) + conv_taps[0] * keep_two * shifted(mix_input, 2)
    mixed_value = low(output_gate * convolved)
    hidden_one = inputs + low_back(matmul(mixed_value, mixer_out))
    scale_two = lax.rsqrt(lax.optimization_barrier(jnp.mean(hidden_one * hidden_one, axis=1, keepdims=True)) + EPSILON)
    normed_two = low(hidden_one * scale_two * gain_two)
    gate_value = low_back(matmul(normed_two, gate_proj))
    up_value = low_back(matmul(normed_two, up_proj))
    activated = low(jax.nn.silu(gate_value) * up_value)
    return hidden_one + matmul(activated, down_proj)

def reference(tokens, segment_ids, cotangent, norm1_gain, in_weight, conv_weight, out_weight, norm2_gain, gate_weight, up_weight, down_weight):
    params = tuple((weight_item.astype(jnp.float32) for weight_item in (norm1_gain, in_weight, conv_weight, out_weight, norm2_gain, gate_weight, up_weight, down_weight)))
    inputs = tokens.astype(jnp.float32).reshape(N_DP, TOK_DP, D)
    segments = segment_ids.reshape(N_DP, TOK_DP)
    cotangents = cotangent.astype(jnp.float32).reshape(N_DP, TOK_DP, D)

    def block_step(totals, block_item):
        block_inputs, block_segments, block_cotangent = block_item
        result, pullback = jax.vjp(partial(forward, block_segments), block_inputs, *params)
        gradients = pullback(block_cotangent)
        totals = tuple((total_item + grad_item for total_item, grad_item in zip(totals, gradients[1:])))
        return (totals, (result.astype(jnp.bfloat16), gradients[0]))
    initial = tuple((jnp.zeros(weight_item.shape, jnp.float32) for weight_item in params))
    totals, (outputs, input_grads) = lax.scan(block_step, initial, (inputs, segments, cotangents))
    return (outputs.reshape(TOKENS, D), input_grads.reshape(TOKENS, D), totals[0], totals[1], totals[2], totals[3], totals[4], totals[5], totals[6], totals[7])
```

```python
import jax
import jax.numpy as jnp
from jax import lax
from jax.sharding import PartitionSpec as P

EPSILON = 1e-05
TEAM = 4


def dot_nt(left, right):
    return lax.dot_general(left, right, (((1,), (1,)), ((), ())), preferred_element_type=jnp.float32)


def dot_nn(left, right):
    return lax.dot_general(left, right, (((1,), (0,)), ((), ())), preferred_element_type=jnp.float32)


def dot_tn(left, right):
    return lax.dot_general(left, right, (((0,), (0,)), ((), ())), preferred_element_type=jnp.float32)


def over_dp(values, distance):
    size = lax.axis_size("dp")
    return lax.ppermute(values, "dp", [(i, i ^ distance) for i in range(size)])


def over_core(values):
    return over_dp(values, 1)


def over_x(values):
    return over_dp(values, 2)


def over_row(values):
    return lax.ppermute(values, "row", [(0, 1), (1, 0)])


def over_col(values, shift):
    size = lax.axis_size("col")
    return lax.ppermute(values, "col", [(i, (i + shift) % size) for i in range(size)])


def col_swap(values, distance):
    size = lax.axis_size("col")
    return lax.ppermute(values, "col", [(i, i ^ distance) for i in range(size)])


def narrow(values):
    return values.astype(jnp.bfloat16)


def wide(values):
    return values.astype(jnp.float32)


def halves(values):
    size = values.shape[0] // 2
    return values[:size], values[size:]


def other_teams(values):
    distance = TEAM
    while distance < lax.axis_size("dp"):
        values = values + over_dp(values, distance)
        distance *= 2
    return values


def gather_pieces(piece, parts):
    cols = lax.axis_size("col")
    pieces = [piece] + [over_col(piece, shift) for shift in range(1, cols)]
    rows = piece.shape[0] // parts
    stacked = jnp.concatenate(
        [one[part * rows : (part + 1) * rows] for part in range(parts) for one in pieces], axis=0
    )
    return jnp.concatenate([stacked, over_row(stacked)], axis=1)


def scatter_pieces(partial, parts):
    cols = lax.axis_size("col")
    half = partial.shape[1] // 2
    mine = partial[:, :half] + wide(over_row(narrow(partial[:, half:])))
    rows = partial.shape[0] // (parts * cols)
    grid = mine.reshape(parts, cols, rows, half)
    total = grid[:, 0].reshape(parts * rows, half)
    for shift in range(1, cols):
        total = total + wide(over_col(narrow(grid[:, shift].reshape(parts * rows, half)), -shift))
    return total


def team_rows(piece, parts):
    rows, half = piece.shape[0] // parts, piece.shape[1]
    own = narrow(other_teams(piece)).reshape(parts, rows, half)
    far = over_x(own)
    pair = over_core(jnp.stack([own, far]))
    place = lax.axis_index("dp") % TEAM
    blocks = [own, pair[0], far, pair[1]]
    result = jnp.zeros((parts, TEAM * rows, half), jnp.bfloat16)
    for distance, block in enumerate(blocks):
        result = lax.dynamic_update_slice(result, block, (0, (place ^ distance) * rows, 0))
    return result


def norm_scale(hidden):
    return lax.rsqrt(jnp.mean(hidden * hidden, axis=1, keepdims=True) + EPSILON)


def norm_backward(grad_normed, hidden, row_scale, gain_vector):
    inner_sum = jnp.sum(grad_normed * gain_vector * hidden, axis=1, keepdims=True)
    cubed = row_scale * row_scale * row_scale
    return grad_normed * gain_vector * row_scale - hidden * (cubed / hidden.shape[1]) * inner_sum


def to_own_tokens(block):
    size = block.shape[0] // 2
    row = lax.axis_index("row")
    own = lax.dynamic_slice_in_dim(block, row * size, size, 0)
    other = lax.dynamic_slice_in_dim(block, (1 - row) * size, size, 0)
    received = over_row(other)
    far_own, far_received = over_x(own), over_x(received)
    near = jnp.concatenate([own, received], axis=1)
    far = jnp.concatenate([far_own, far_received], axis=1)
    both = over_core(jnp.stack([near, far]))
    return (near, both[0]), (far, both[1])


def to_blocks(values, dtype):
    half = values.shape[1] // 2
    size = values.shape[0]
    row = lax.axis_index("row")
    received = over_row(narrow(values[:, half:])).astype(dtype)
    result = jnp.zeros((2 * size, half), dtype)
    result = lax.dynamic_update_slice(result, values[:, :half].astype(dtype), (row * size, 0))
    return lax.dynamic_update_slice(result, received, ((1 - row) * size, 0))


def body(
    tokens,
    segment_ids,
    cotangent,
    norm1_gain,
    in_weight,
    conv_weight,
    out_weight,
    norm2_gain,
    gate_weight,
    up_weight,
    down_weight,
):
    place = lax.axis_index("dp") % TEAM
    row = lax.axis_index("row")
    col = lax.axis_index("col")
    cols = lax.axis_size("col")
    sequence = tokens.shape[0]
    size = sequence // 2
    half = tokens.shape[1]

    channels = in_weight.shape[2] // TEAM
    hidden = gate_weight.shape[1] // TEAM
    in_part = lax.dynamic_slice_in_dim(in_weight, place * channels, channels, 2)
    in_part = in_part.transpose(1, 2, 0).reshape(3 * channels, half)
    out_part = lax.dynamic_slice_in_dim(out_weight, place * channels, channels, 0)
    gate_part = lax.dynamic_slice_in_dim(gate_weight, place * hidden, hidden, 1).T
    up_part = lax.dynamic_slice_in_dim(up_weight, place * hidden, hidden, 1).T
    down_part = lax.dynamic_slice_in_dim(down_weight, place * hidden, hidden, 0)
    taps_part = lax.dynamic_slice_in_dim(conv_weight, place * channels, channels, 1)

    near_tokens, far_tokens = to_own_tokens(tokens)
    mixer = gather_pieces(jnp.concatenate([in_part, out_part], axis=0), 4)
    in_rows, out_rows = mixer[: 3 * cols * channels], mixer[3 * cols * channels :]
    taps = jnp.concatenate([taps_part] + [over_col(taps_part, shift) for shift in range(1, cols)], axis=1)
    taps = wide(taps)
    gains = jnp.stack([norm1_gain, norm2_gain])
    gains = wide(jnp.concatenate([gains, over_row(gains)], axis=1))
    gain_one, gain_two = gains[0], gains[1]

    ids = jnp.stack([segment_ids, over_row(segment_ids)])
    ids = lax.dynamic_index_in_dim(ids, (col // 2) ^ row, 0, keepdims=False)
    ids = lax.dynamic_slice_in_dim(ids, (col % 2) * sequence, sequence, 0)
    ids_far = over_x(ids)
    ids_pair = over_core(jnp.stack([ids, ids_far]))
    ids = jnp.stack([ids, ids_pair[0], ids_far, ids_pair[1]])
    keeps = []
    for offset in (1, 2):
        equal = (ids[:, offset:] == ids[:, :-offset]).astype(jnp.float32)
        keeps.append(jnp.pad(equal, ((0, 0), (offset, offset))))
    keep_one = lax.dynamic_slice_in_dim(keeps[0], row * size, size, 1)[:, :, None]
    keep_two = lax.dynamic_slice_in_dim(keeps[1], row * size, size, 1)[:, :, None]
    next_one = lax.dynamic_slice_in_dim(keeps[0], row * size + 1, size, 1)[:, :, None]
    next_two = lax.dynamic_slice_in_dim(keeps[1], row * size + 2, size, 1)[:, :, None]
    keep_one, keep_two, next_one, next_two = (
        (flags[:2], flags[2:]) for flags in (keep_one, keep_two, next_one, next_two)
    )

    gate_rows = gather_pieces(gate_part, 1)
    up_rows = gather_pieces(up_part, 1)
    down_rows = gather_pieces(down_part, 1)
    near_grads, far_grads = to_own_tokens(cotangent)

    width = cols * channels
    inputs = [jnp.concatenate(pair, axis=0) for pair in (near_tokens, far_tokens)]
    normed_one, scale_one, mixed, saved = [], [], [], []
    for pair in (0, 1):
        values = wide(inputs[pair])
        scale = norm_scale(values)
        scale_one.append(scale)
        normed_one.append(narrow(values * scale * gain_one))
    for pair in (0, 1):
        projected = dot_nt(normed_one[pair], in_rows).reshape(2, size, 3 * width)
        input_gate, output_gate, values_part = (
            projected[:, :, :width],
            projected[:, :, width : 2 * width],
            projected[:, :, 2 * width :],
        )
        mix_input = input_gate * values_part
        before = over_row(mix_input[:, size - 2 :])
        extended = jnp.concatenate([before, mix_input], axis=1)
        prior_one = keep_one[pair] * extended[:, 1 : size + 1]
        prior_two = keep_two[pair] * extended[:, :size]
        convolved = taps[2] * mix_input + taps[1] * prior_one + taps[0] * prior_two
        mixed.append(narrow(output_gate * convolved).reshape(2 * size, width))
        saved.append((input_gate, output_gate, values_part, mix_input, prior_one, prior_two, convolved))

    far_sum = dot_nn(mixed[1], out_rows)
    far_sum = far_sum[:size] + wide(over_core(narrow(far_sum[size:])))
    from_far = over_x(narrow(far_sum))
    near_sum = dot_nn(mixed[0], out_rows)
    near_sum = near_sum[:size] + wide(over_core(narrow(near_sum[size:])))
    to_far = over_x(narrow(near_sum))
    hidden_near = wide(near_tokens[0]) + (near_sum + wide(from_far))
    hidden_far = wide(far_tokens[0]) + (far_sum + wide(to_far))

    hiddens, scale_two, normed_two = (hidden_near, hidden_far), [], []
    for values in hiddens:
        scale = norm_scale(values)
        scale_two.append(scale)
        normed = narrow(values * scale * gain_two)
        normed_two.append(jnp.concatenate([normed, over_core(normed)], axis=0))

    cotangents = [jnp.concatenate(pair, axis=0) for pair in (near_grads, far_grads)]
    act, grad_gate, grad_up, back = [], [], [], []
    for pair in (0, 1):
        gate_value = dot_nt(normed_two[pair], gate_rows)
        up_value = dot_nt(normed_two[pair], up_rows)
        grad_act = dot_nt(cotangents[pair], down_rows)
        sigmoid_gate = jax.nn.sigmoid(gate_value)
        silu = gate_value * sigmoid_gate
        act.append(narrow(silu * up_value))
        grad_gate.append(narrow(grad_act * up_value * sigmoid_gate * (1.0 + gate_value * (1.0 - sigmoid_gate))))
        grad_up.append(narrow(grad_act * silu))
        back.append(dot_nn(grad_gate[pair], gate_rows) + dot_nn(grad_up[pair], up_rows))
        if pair == 0:
            near_back = back[0][:size] + wide(over_core(narrow(back[0][size:])))
            back_to_far = over_x(narrow(near_back))
    far_back = back[1][:size] + wide(over_core(narrow(back[1][size:])))
    back_from_far = over_x(narrow(far_back))

    down_total = scatter_pieces(dot_tn(act[0], cotangents[0]) + dot_tn(act[1], cotangents[1]), 1)
    gate_total = scatter_pieces(
        dot_tn(grad_gate[0], normed_two[0]) + dot_tn(grad_gate[1], normed_two[1]), 1
    )
    up_total = scatter_pieces(dot_tn(grad_up[0], normed_two[0]) + dot_tn(grad_up[1], normed_two[1]), 1)

    far_out = dot_nn(act[1], down_rows)
    far_out = far_out[:size] + wide(over_core(narrow(far_out[size:])))
    out_from_far = over_x(narrow(far_out))
    near_out = dot_nn(act[0], down_rows)
    near_out = near_out[:size] + wide(over_core(narrow(near_out[size:])))
    result = narrow(hidden_near + (near_out + wide(out_from_far)))

    back_sums = (near_back + wide(back_from_far), far_back + wide(back_to_far))
    grad_hidden, grad_mixed = [], []
    for which, cotangent_rows in ((0, near_grads[0]), (1, far_grads[0])):
        grads = wide(cotangent_rows) + norm_backward(
            back_sums[which], hiddens[which], scale_two[which], gain_two
        )
        grad_hidden.append(grads)
        low = narrow(grads)
        grad_mixed.append(jnp.concatenate([low, over_core(low)], axis=0))
    gain_two_grad = jnp.sum(back_sums[0] * hidden_near * scale_two[0], axis=0)

    grad_projected, conv_local = [None, None], 0.0
    sums = [None, None]
    for pair in (1, 0):
        input_gate, output_gate, values_part, mix_input, prior_one, prior_two, convolved = saved[pair]
        grad_y = dot_nt(grad_mixed[pair], out_rows).reshape(2, size, width)
        grad_conv = grad_y * output_gate
        conv_local = conv_local + jnp.stack(
            [
                jnp.sum(grad_conv * prior_two, axis=(0, 1)),
                jnp.sum(grad_conv * prior_one, axis=(0, 1)),
                jnp.sum(grad_conv * mix_input, axis=(0, 1)),
            ]
        )
        after = over_row(grad_conv[:, :2])
        extended = jnp.concatenate([grad_conv, after], axis=1)
        grad_mix = (
            taps[2] * grad_conv
            + taps[1] * (next_one[pair] * extended[:, 1 : size + 1])
            + taps[0] * (next_two[pair] * extended[:, 2:])
        )
        grad_projected[pair] = narrow(
            jnp.concatenate([grad_mix * values_part, grad_y * convolved, grad_mix * input_gate], axis=2)
        ).reshape(2 * size, 3 * width)
        sums[pair] = dot_nn(grad_projected[pair], in_rows)
        if pair == 1:
            far_one = sums[1][:size] + wide(over_core(narrow(sums[1][size:])))
            one_from_far = over_x(narrow(far_one))
    near_one = sums[0][:size] + wide(over_core(narrow(sums[0][size:])))
    grad_normed_one = near_one + wide(one_from_far)

    mixer_total = scatter_pieces(
        jnp.concatenate(
            [
                dot_tn(grad_projected[0], normed_one[0]) + dot_tn(grad_projected[1], normed_one[1]),
                dot_tn(mixed[0], grad_mixed[0]) + dot_tn(mixed[1], grad_mixed[1]),
            ],
            axis=0,
        ),
        4,
    )

    own_inputs = wide(near_tokens[0])
    own_scale = scale_one[0][:size]
    input_grad = grad_hidden[0] + norm_backward(grad_normed_one, own_inputs, own_scale, gain_one)
    gain_one_grad = jnp.sum(grad_normed_one * own_inputs * own_scale, axis=0)

    gain_local = jnp.stack([gain_one_grad, gain_two_grad])
    conv_flat = conv_local.reshape(3, cols, channels).transpose(1, 0, 2).reshape(cols, 3 * channels)
    conv_flat = jnp.take(conv_flat, (col - jnp.arange(cols)) % cols, axis=0).reshape(-1)
    sent = jnp.concatenate([gain_local[:, half:].reshape(-1), conv_flat])
    small = jnp.concatenate([gain_local[:, :half].reshape(-1), conv_flat]) + over_row(sent)
    for distance in (1, 2):
        small = small + col_swap(small, distance)
    conv_own = lax.dynamic_slice_in_dim(small[2 * half :], col * 3 * channels, 3 * channels, 0)
    conv_wide = lax.dynamic_update_slice(
        jnp.zeros((TEAM * 3 * channels,), jnp.float32), conv_own, (place * 3 * channels,)
    )
    small = jnp.concatenate([small[: 2 * half], conv_wide])
    small = small + over_x(small)
    small = small + over_core(small)
    small = other_teams(small)
    conv_grad = small[2 * half :].reshape(TEAM, 3, channels).transpose(1, 0, 2).reshape(3, TEAM * channels)

    down_grad = wide(team_rows(down_total, 1)[0])
    gate_grad = wide(team_rows(gate_total, 1)[0].T)
    up_grad = wide(team_rows(up_total, 1)[0].T)
    mixer_grads = team_rows(mixer_total, 4)
    in_grad = wide(mixer_grads[:3].transpose(2, 0, 1))
    out_grad = wide(mixer_grads[3])
    return (
        to_blocks(result, jnp.bfloat16),
        to_blocks(input_grad, jnp.float32),
        small[:half],
        in_grad,
        conv_grad,
        out_grad,
        small[half : 2 * half],
        gate_grad,
        up_grad,
        down_grad,
    )


def solution(mesh):
    return jax.shard_map(
        body,
        mesh=mesh,
        in_specs=(
            P(("dp", "col"), "row"),
            P(("dp", "row")),
            P(("dp", "col"), "row"),
            P("row"),
            P("row", None, "col"),
            P(None, "col"),
            P("col", "row"),
            P("row"),
            P("row", "col"),
            P("row", "col"),
            P("col", "row"),
        ),
        out_specs=(
            P(("dp", "col"), "row"),
            P(("dp", "col"), "row"),
            P("row"),
            P("row", None, "col"),
            P(None, "col"),
            P("col", "row"),
            P("row"),
            P("row", "col"),
            P("row", "col"),
            P("col", "row"),
        ),
        check_vma=False,
    )
```

```python
import jax
import jax.numpy as jnp
from jax import lax
from jax.experimental import pallas as pl
from jax.experimental.pallas import tpu as pltpu
from jax.sharding import PartitionSpec as P

EPSILON = 1e-05
TEAM = 4


def dot_nt(left, right):
    return lax.dot_general(left, right, (((1,), (1,)), ((), ())), preferred_element_type=jnp.float32)


def dot_nn(left, right):
    return lax.dot_general(left, right, (((1,), (0,)), ((), ())), preferred_element_type=jnp.float32)


def dot_tn(left, right):
    return lax.dot_general(left, right, (((0,), (0,)), ((), ())), preferred_element_type=jnp.float32)


def over_dp(values, distance):
    size = lax.axis_size("dp")
    return lax.ppermute(values, "dp", [(i, i ^ distance) for i in range(size)])


def over_core(values):
    return over_dp(values, 1)


def over_x(values):
    return over_dp(values, 2)


def over_row(values):
    return lax.ppermute(values, "row", [(0, 1), (1, 0)])


def col_swap(values, distance):
    size = lax.axis_size("col")
    return lax.ppermute(values, "col", [(i, i ^ distance) for i in range(size)])


def narrow(values):
    return values.astype(jnp.bfloat16)


def wide(values):
    return values.astype(jnp.float32)


def halves(values):
    size = values.shape[0] // 2
    return values[:size], values[size:]


def other_teams(values):
    distance = TEAM
    while distance < lax.axis_size("dp"):
        values = values + over_dp(values, distance)
        distance *= 2
    return values


def after(value, *events):
    return lax.optimization_barrier((value, *events))[0]


def meet(*values):
    return lax.optimization_barrier(values)


def hop(move, value, *waiting):
    return meet(move(value), *waiting)


def stacked(pair, other, parts):
    pieces = jnp.concatenate([pair, other], axis=0)
    if parts > 1:
        pieces = pieces.reshape(4, parts, -1, pair.shape[2]).transpose(1, 0, 2, 3)
    return pieces.reshape(-1, pair.shape[2])


def col_first(piece):
    return jnp.stack([piece, col_swap(piece, 2)])


def col_send(values, parts):
    rows = values.shape[0] // (parts * 4)
    grid = values.reshape(parts, 2, 2 * rows, values.shape[1])
    return narrow(grid[:, 1]), grid[:, 0]


def col_add(kept, received):
    total = kept + wide(received)
    rows = total.shape[1] // 2
    return narrow(total[:, rows:]), total[:, :rows]


def col_last(kept, received):
    return (kept + wide(received)).reshape(-1, kept.shape[2])


def team_rows(piece, parts):
    rows, half = piece.shape[0] // parts, piece.shape[1]
    own = narrow(other_teams(piece)).reshape(parts, rows, half)
    far = over_x(own)
    pair = over_core(jnp.stack([own, far]))
    place = lax.axis_index("dp") % TEAM
    blocks = [own, pair[0], far, pair[1]]
    result = jnp.zeros((parts, TEAM * rows, half), jnp.bfloat16)
    for distance, block in enumerate(blocks):
        result = lax.dynamic_update_slice(result, block, (0, (place ^ distance) * rows, 0))
    return result


def norm_scale(hidden):
    return lax.rsqrt(jnp.mean(hidden * hidden, axis=1, keepdims=True) + EPSILON)


def norm_backward(grad_normed, hidden, row_scale, gain_vector):
    inner_sum = jnp.sum(grad_normed * gain_vector * hidden, axis=1, keepdims=True)
    cubed = row_scale * row_scale * row_scale
    return grad_normed * gain_vector * row_scale - hidden * (cubed / hidden.shape[1]) * inner_sum


def to_blocks(values, dtype):
    half = values.shape[1] // 2
    size = values.shape[0]
    row = lax.axis_index("row")
    received = over_row(narrow(values[:, half:])).astype(dtype)
    result = jnp.zeros((2 * size, half), dtype)
    result = lax.dynamic_update_slice(result, values[:, :half].astype(dtype), (row * size, 0))
    return lax.dynamic_update_slice(result, received, ((1 - row) * size, 0))


ROWS = 256
VMEM_BYTES = 48 * 2**20


def whole(array):
    return pl.BlockSpec(array.shape, lambda i: (0,) * array.ndim)


def row_tiles(array):
    return pl.BlockSpec((ROWS, array.shape[1]), lambda i: (i, 0))


def token_call(kernel, tiled, resident, outs):
    tokens = tiled[0].shape[0]
    shapes = [jax.ShapeDtypeStruct((tokens, columns), dtype) for columns, dtype in outs]
    return pl.pallas_call(
        kernel,
        grid=(tokens // ROWS,),
        in_specs=[row_tiles(one) for one in tiled] + [whole(one) for one in resident],
        out_specs=[row_tiles(one) for one in shapes],
        out_shape=shapes,
        compiler_params=pltpu.CompilerParams(vmem_limit_bytes=VMEM_BYTES),
    )(*tiled, *resident)


def split_nt(left, near, row):
    half = near.shape[1]
    return dot_nt(left[:, :half], near[...]) + dot_nt(left[:, half:], row[...])


def forward_kernel(normed, gate_near, gate_row, up_near, up_row, gate, up, act):
    gate_value = split_nt(normed, gate_near, gate_row)
    up_value = split_nt(normed, up_near, up_row)
    gate[...] = narrow(gate_value)
    up[...] = narrow(up_value)
    act[...] = narrow(gate_value * jax.nn.sigmoid(gate_value) * up_value)


def backward_kernel(
    gate, up, cotangent, down_near, down_row, gate_near, gate_row, up_near, up_row, grad_gate, grad_up, back
):
    half = gate_near.shape[1]
    grad_act = split_nt(cotangent, down_near, down_row)
    gate_value, up_value = wide(gate[...]), wide(up[...])
    sigmoid_gate = jax.nn.sigmoid(gate_value)
    gated = grad_act * sigmoid_gate
    low_gate = narrow(gated * up_value * (1.0 + gate_value * (1.0 - sigmoid_gate)))
    low_up = narrow(gated * gate_value)
    grad_gate[...] = low_gate
    grad_up[...] = low_up
    back[:, :half] = narrow(dot_nn(low_gate, gate_near[...]) + dot_nn(low_up, up_near[...]))
    back[:, half:] = narrow(dot_nn(low_gate, gate_row[...]) + dot_nn(low_up, up_row[...]))


def out_kernel(act, down_near, down_row, out):
    half = down_near.shape[1]
    out[:, :half] = narrow(dot_nn(act[...], down_near[...]))
    out[:, half:] = narrow(dot_nn(act[...], down_row[...]))


def weight_kernel(left_near, left_far, right_near, right_far, own, sent):
    total = dot_tn(left_near[...], right_near[...]) + dot_tn(left_far[...], right_far[...])
    half = own.shape[1]
    own[...] = total[:, :half]
    sent[...] = narrow(total[:, half:])


def weight_grads(lefts, rights, tile):
    tokens, columns = lefts[0].shape
    half = rights[0].shape[1] // 2
    left_spec = pl.BlockSpec((tokens, tile), lambda i: (0, i))
    out_spec = pl.BlockSpec((tile, half), lambda i: (i, 0))
    return pl.pallas_call(
        weight_kernel,
        grid=(columns // tile,),
        in_specs=[left_spec, left_spec, whole(rights[0]), whole(rights[1])],
        out_specs=[out_spec, out_spec],
        out_shape=[
            jax.ShapeDtypeStruct((columns, half), jnp.float32),
            jax.ShapeDtypeStruct((columns, half), jnp.bfloat16),
        ],
        compiler_params=pltpu.CompilerParams(vmem_limit_bytes=VMEM_BYTES),
    )(*lefts, *rights)


def body(
    tokens,
    segment_ids,
    cotangent,
    norm1_gain,
    in_weight,
    conv_weight,
    out_weight,
    norm2_gain,
    gate_weight,
    up_weight,
    down_weight,
):
    place = lax.axis_index("dp") % TEAM
    row = lax.axis_index("row")
    col = lax.axis_index("col")
    cols = lax.axis_size("col")
    sequence = tokens.shape[0]
    size = sequence // 2
    half = tokens.shape[1]

    tokens_other = lax.dynamic_slice_in_dim(tokens, (1 - row) * size, size, 0)
    tokens_own = lax.dynamic_slice_in_dim(tokens, row * size, size, 0)
    tokens_row = over_row(tokens_other)
    tokens_x0 = over_x(tokens_own)
    channels = in_weight.shape[2] // TEAM
    hidden = gate_weight.shape[1] // TEAM
    in_part = lax.dynamic_slice_in_dim(in_weight, place * channels, channels, 2)
    in_part = in_part.transpose(1, 2, 0).reshape(3 * channels, half)
    out_part = lax.dynamic_slice_in_dim(out_weight, place * channels, channels, 0)
    taps_part = lax.dynamic_slice_in_dim(conv_weight, place * channels, channels, 1)
    taps_part = jnp.pad(taps_part, ((0, 13), (0, half - channels)))
    mixer_pair = col_first(jnp.concatenate([in_part, out_part, taps_part], axis=0))
    grads_other = lax.dynamic_slice_in_dim(cotangent, (1 - row) * size, size, 0)
    grads_own = lax.dynamic_slice_in_dim(cotangent, row * size, size, 0)
    gate_part = lax.dynamic_slice_in_dim(gate_weight, place * hidden, hidden, 1).T
    gains = jnp.stack([norm1_gain, norm2_gain])
    gains_row = over_row(gains)
    ids_row = over_row(segment_ids)
    tokens_row, tokens_x0, gains_row, ids_row, mixer_pair, grads_other, gate_part = meet(
        tokens_row, tokens_x0, gains_row, ids_row, mixer_pair, grads_other, gate_part
    )

    tokens_x1 = over_x(tokens_row)
    grads_row = over_row(grads_other)
    mixer_other = col_swap(mixer_pair, 1)
    up_part = lax.dynamic_slice_in_dim(up_weight, place * hidden, hidden, 1).T
    down_part = lax.dynamic_slice_in_dim(down_weight, place * hidden, hidden, 0)
    ids = jnp.stack([segment_ids, ids_row])
    ids = lax.dynamic_index_in_dim(ids, (col // 2) ^ row, 0, keepdims=False)
    ids = lax.dynamic_slice_in_dim(ids, (col % 2) * sequence, sequence, 0)
    ids_far = over_x(ids)
    tokens_x1, grads_row, ids_far, mixer_other, gate_part, grads_own, ids, up_part = meet(
        tokens_x1, grads_row, ids_far, mixer_other, gate_part, grads_own, ids, up_part
    )

    mixer_near = stacked(mixer_pair[:, : 4 * channels], mixer_other[:, : 4 * channels], 4)
    mixer_row = over_row(mixer_near)
    grads_x0, grads_x1 = over_x(grads_own), over_x(grads_row)
    gate_pair = col_first(gate_part)
    near = jnp.concatenate([tokens_own, tokens_row], axis=1)
    far = jnp.concatenate([tokens_x0, tokens_x1], axis=1)
    pair, ids, ids_far = hop(over_core, jnp.stack([near, far]), ids, ids_far)
    near_tokens, far_tokens = (near, pair[0]), (far, pair[1])
    ids_pair, pair = hop(over_core, jnp.stack([ids, ids_far]), pair)
    ids = jnp.stack([ids, ids_pair[0], ids_far, ids_pair[1]])
    keeps = []
    for offset in (1, 2):
        equal = (ids[:, offset:] == ids[:, :-offset]).astype(jnp.float32)
        keeps.append(jnp.pad(equal, ((0, 0), (offset, offset))))
    keep_one = lax.dynamic_slice_in_dim(keeps[0], row * size, size, 1)[:, :, None]
    keep_two = lax.dynamic_slice_in_dim(keeps[1], row * size, size, 1)[:, :, None]
    next_one = lax.dynamic_slice_in_dim(keeps[0], row * size + 1, size, 1)[:, :, None]
    next_two = lax.dynamic_slice_in_dim(keeps[1], row * size + 2, size, 1)[:, :, None]
    keep_one, keep_two, next_one, next_two = (
        (flags[:2], flags[2:]) for flags in (keep_one, keep_two, next_one, next_two)
    )
    near_tokens, far_tokens = (near, pair[0]), (far, pair[1])
    gains = wide(jnp.concatenate([gains, gains_row], axis=1))
    gain_one, gain_two = gains[0], gains[1]
    inputs = [jnp.concatenate(both, axis=0) for both in (near_tokens, far_tokens)]
    normed_one, scale_one = [], []
    for which in (0, 1):
        values = wide(inputs[which])
        scale = norm_scale(values)
        scale_one.append(scale)
        normed_one.append(narrow(values * scale * gain_one))
    gate_pair, up_part = meet(gate_pair, up_part)
    gate_other = col_swap(gate_pair, 1)
    taps = jnp.concatenate(
        [both[which, 4 * channels : 4 * channels + 3, :channels] for both in (mixer_pair, mixer_other) for which in (0, 1)],
        axis=1,
    )
    taps = wide(taps)
    mixer_row, grads_x0, grads_x1, gate_other, normed_one, up_part, down_part = meet(
        mixer_row, grads_x0, grads_x1, gate_other, normed_one, up_part, down_part
    )

    gate_near = stacked(gate_pair, gate_other, 1)
    gate_row = over_row(gate_near)
    up_pair = col_first(up_part)
    mixer = jnp.concatenate([mixer_near, mixer_row], axis=1)
    in_rows, out_rows = mixer[: 3 * cols * channels], mixer[3 * cols * channels :]
    width = cols * channels
    saved, mixed, sums = [None, None], [None, None], [None, None]

    def project(which):
        projected = dot_nt(normed_one[which], in_rows).reshape(2, size, 3 * width)
        mix_input = projected[:, :, :width] * projected[:, :, 2 * width :]
        return projected, mix_input, mix_input[:, size - 2 :]

    def mix(which, projected, mix_input, before):
        input_gate, output_gate, values_part = (
            projected[:, :, :width],
            projected[:, :, width : 2 * width],
            projected[:, :, 2 * width :],
        )
        extended = jnp.concatenate([before, mix_input], axis=1)
        prior_one = keep_one[which] * extended[:, 1 : size + 1]
        prior_two = keep_two[which] * extended[:, :size]
        convolved = taps[2] * mix_input + taps[1] * prior_one + taps[0] * prior_two
        mixed[which] = narrow(output_gate * convolved).reshape(2 * size, width)
        saved[which] = (input_gate, output_gate, values_part, mix_input, prior_one, prior_two, convolved)
        return dot_nn(mixed[which], out_rows)

    def core_sum(partial, *waiting):
        received, *waiting = hop(over_core, narrow(partial[size:]), *waiting)
        return (wide(partial[:size]) + wide(received), *waiting)

    far_projected, far_mix, far_end = project(1)
    near_projected, near_mix, near_end = project(0)
    ends, far_mix, near_mix = hop(over_row, jnp.stack([near_end, far_end]), far_mix, near_mix)
    far_sum, near_mix = core_sum(mix(1, far_projected, far_mix, ends[1]), near_mix)
    from_far = over_x(narrow(far_sum))
    up_pair, near_mix = meet(up_pair, near_mix)
    up_other = col_swap(up_pair, 1)
    (near_sum,) = core_sum(mix(0, near_projected, near_mix, ends[0]))
    to_far = over_x(narrow(near_sum))
    from_far, gate_row, up_other, down_part = meet(from_far, gate_row, up_other, down_part)

    up_near = stacked(up_pair, up_other, 1)
    up_row = over_row(up_near)
    down_pair = col_first(down_part)

    def second_norm(hidden_sum, *waiting):
        scale = norm_scale(hidden_sum)
        normed = narrow(hidden_sum * scale * gain_two)
        received, *waiting = hop(over_core, normed, *waiting)
        return (scale, jnp.concatenate([normed, received], axis=0), *waiting)

    hidden_near = wide(near_tokens[0]) + (near_sum + wide(from_far))
    scale_near, normed_near, gate_near = second_norm(hidden_near, gate_near)
    near = jnp.concatenate([grads_own, grads_row], axis=1)
    far = jnp.concatenate([grads_x0, grads_x1], axis=1)
    pair, down_pair = hop(over_core, jnp.stack([near, far]), down_pair)
    near_grads, far_grads = (near, pair[0]), (far, pair[1])
    down_other = col_swap(down_pair, 1)
    up_row, down_other, to_far = meet(up_row, down_other, to_far)

    down_near = stacked(down_pair, down_other, 1)
    down_row = over_row(down_near)
    hidden_far = wide(far_tokens[0]) + (far_sum + wide(to_far))
    scale_far, normed_far, up_near = second_norm(hidden_far, up_near)
    hiddens, scale_two, normed_two = (hidden_near, hidden_far), (scale_near, scale_far), (normed_near, normed_far)
    cotangents = [jnp.concatenate(both, axis=0) for both in (near_grads, far_grads)]
    units = gate_near.shape[0]
    weights = (gate_near, gate_row, up_near, up_row)
    outs = ((units, jnp.bfloat16),) * 3
    gates, ups, act = zip(*[token_call(forward_kernel, [normed], weights, outs) for normed in normed_two])
    gates, ups, act = list(gates), list(ups), list(act)
    down_own, down_sent = weight_grads(act, cotangents, units // 3)
    down_sent, down_kept = col_send(jnp.concatenate([down_own, wide(down_sent)], axis=1), 1)
    down_moved = col_swap(down_sent, 1)
    down_row, act, gates, ups, down_sent = meet(down_row, act, gates, ups, down_sent)

    grad_gate, grad_up = [None, None], [None, None]

    def hidden_back(which, gate_value, up_value):
        grad_gate[which], grad_up[which], back = token_call(
            backward_kernel,
            [gate_value, up_value, cotangents[which]],
            (down_near, down_row, *weights),
            ((units, jnp.bfloat16), (units, jnp.bfloat16), (2 * half, jnp.bfloat16)),
        )
        return back

    def exchange(partial):
        return partial[:, :half], narrow(partial[:, half:])

    near_back, gates[1], ups[1] = core_sum(hidden_back(0, gates[0], ups[0]), gates[1], ups[1])
    back_to_far = over_x(narrow(near_back))
    far_back, grad_gate, grad_up, act, down_moved = core_sum(
        hidden_back(1, gates[1], ups[1]), grad_gate, grad_up, act, down_moved
    )
    back_from_far = over_x(narrow(far_back))
    down_sent, down_kept = col_add(down_kept, down_moved)
    down_moved = col_swap(down_sent, 2)
    gate_own, gate_sent = weight_grads(grad_gate, normed_two, units // 3)
    gate_moved = over_row(gate_sent)
    grad_up, act, gate_sent = meet(grad_up, act, gate_sent)
    up_own, up_sent = weight_grads(grad_up, normed_two, units // 3)
    outs = [token_call(out_kernel, [one], (down_near, down_row), ((2 * half, jnp.bfloat16),))[0] for one in act]
    received, outs, up_sent = hop(over_core, jnp.stack([outs[0][size:], outs[1][size:]]), outs, up_sent)
    near_out, far_out = (wide(out[:size]) + wide(received[which]) for which, out in enumerate(outs))
    back_to_far, back_from_far, gate_moved, up_sent, down_moved, far_out, near_out = meet(
        back_to_far, back_from_far, gate_moved, up_sent, down_moved, far_out, near_out
    )

    up_moved = over_row(up_sent)
    out_from_far = over_x(narrow(far_out))
    gate_sent, gate_kept = col_send(gate_own + wide(gate_moved), 1)
    gate_moved = col_swap(gate_sent, 1)
    down_own, down_sent = exchange(col_last(down_kept, down_moved))
    back_sums = (near_back + wide(back_from_far), far_back + wide(back_to_far))
    grad_hidden, low = [], []
    for which, cotangent_rows in ((0, near_grads[0]), (1, far_grads[0])):
        grads = wide(cotangent_rows) + norm_backward(
            back_sums[which], hiddens[which], scale_two[which], gain_two
        )
        grad_hidden.append(grads)
        low.append(narrow(grads))
    received, low = hop(over_core, jnp.stack(low), low)
    grad_mixed = [jnp.concatenate([low[which], received[which]], axis=0) for which in (0, 1)]
    gain_two_grad = jnp.sum(back_sums[0] * hidden_near * scale_two[0], axis=0)

    grad_projected = [None, None]

    def mix_back(which):
        grad_y = dot_nt(grad_mixed[which], out_rows).reshape(2, size, width)
        grad_conv = grad_y * saved[which][1]
        return grad_y, grad_conv, grad_conv[:, :2]

    def project_back(which, grad_y, grad_conv, following):
        input_gate, output_gate, values_part, mix_input, prior_one, prior_two, convolved = saved[which]
        conv_local = jnp.stack(
            [
                jnp.sum(grad_conv * prior_two, axis=(0, 1)),
                jnp.sum(grad_conv * prior_one, axis=(0, 1)),
                jnp.sum(grad_conv * mix_input, axis=(0, 1)),
            ]
        )
        extended = jnp.concatenate([grad_conv, following], axis=1)
        grad_mix = (
            taps[2] * grad_conv
            + taps[1] * (next_one[which] * extended[:, 1 : size + 1])
            + taps[0] * (next_two[which] * extended[:, 2:])
        )
        grad_projected[which] = narrow(
            jnp.concatenate([grad_mix * values_part, grad_y * convolved, grad_mix * input_gate], axis=2)
        ).reshape(2 * size, 3 * width)
        return dot_nn(grad_projected[which], in_rows), conv_local

    far_y, far_conv, far_start = mix_back(1)
    near_y, near_conv, near_start = mix_back(0)
    starts, far_conv, near_conv = hop(over_row, jnp.stack([near_start, far_start]), far_conv, near_conv)
    far_one, far_taps = project_back(1, far_y, far_conv, starts[1])
    far_one, near_conv = core_sum(far_one, near_conv)
    one_from_far = over_x(narrow(far_one))
    near_one, near_taps = project_back(0, near_y, near_conv, starts[0])
    near_one, grad_projected, normed_one, mixed, gate_moved = core_sum(
        near_one, grad_projected, normed_one, mixed, gate_moved
    )
    conv_local = near_taps + far_taps
    gate_sent, gate_kept = col_add(gate_kept, gate_moved)
    gate_moved = col_swap(gate_sent, 2)
    mixer_own, mixer_sent = exchange(
        jnp.concatenate(
            [
                dot_tn(grad_projected[0], normed_one[0]) + dot_tn(grad_projected[1], normed_one[1]),
                dot_tn(mixed[0], grad_mixed[0]) + dot_tn(mixed[1], grad_mixed[1]),
            ],
            axis=0,
        )
    )
    up_moved, mixer_sent, gate_moved, down_sent = meet(up_moved, mixer_sent, gate_moved, down_sent)
    mixer_moved = over_row(mixer_sent)
    up_sent, up_kept = col_send(up_own + wide(up_moved), 1)
    up_moved = col_swap(up_sent, 1)
    out_from_far, one_from_far, mixer_sent, up_sent = meet(out_from_far, one_from_far, mixer_sent, up_sent)
    result = narrow(hidden_near + (near_out + wide(out_from_far)))
    grad_normed_one = near_one + wide(one_from_far)
    own_inputs = wide(near_tokens[0])
    own_scale = scale_one[0][:size]
    input_grad = grad_hidden[0] + norm_backward(grad_normed_one, own_inputs, own_scale, gain_one)
    gain_one_grad = jnp.sum(grad_normed_one * own_inputs * own_scale, axis=0)
    down_total = down_own + wide(over_row(down_sent))
    gate_total = col_last(gate_kept, gate_moved)
    up_moved, mixer_moved = meet(up_moved, mixer_moved)
    up_sent, up_kept = col_add(up_kept, up_moved)
    up_moved = col_swap(up_sent, 2)
    mixer_sent, mixer_kept = col_send(mixer_own + wide(mixer_moved), 4)
    mixer_moved = col_swap(mixer_sent, 1)
    up_total = col_last(up_kept, up_moved)
    mixer_sent, mixer_kept = col_add(mixer_kept, mixer_moved)
    mixer_total = col_last(mixer_kept, col_swap(mixer_sent, 2))

    gain_local = jnp.stack([gain_one_grad, gain_two_grad])
    conv_flat = conv_local.reshape(3, cols, channels).transpose(1, 0, 2).reshape(cols, 3 * channels)
    apart = jnp.arange(cols) ^ col
    conv_flat = jnp.take(conv_flat, apart // 2 + apart % 2 * 2, axis=0).reshape(-1)
    sent = jnp.concatenate([gain_local[:, half:].reshape(-1), conv_flat])
    small = jnp.concatenate([gain_local[:, :half].reshape(-1), conv_flat]) + over_row(sent)
    for distance in (1, 2):
        small = small + col_swap(small, distance)
    conv_own = lax.dynamic_slice_in_dim(small[2 * half :], col * 3 * channels, 3 * channels, 0)
    conv_wide = lax.dynamic_update_slice(
        jnp.zeros((TEAM * 3 * channels,), jnp.float32), conv_own, (place * 3 * channels,)
    )
    small = jnp.concatenate([small[: 2 * half], conv_wide])
    small = small + over_x(small)
    small = small + over_core(small)
    small = other_teams(small)
    conv_grad = small[2 * half :].reshape(TEAM, 3, channels).transpose(1, 0, 2).reshape(3, TEAM * channels)

    down_grad = wide(team_rows(down_total, 1)[0])
    gate_grad = wide(team_rows(gate_total, 1)[0].T)
    up_grad = wide(team_rows(up_total, 1)[0].T)
    mixer_grads = team_rows(mixer_total, 4)
    in_grad = wide(mixer_grads[:3].transpose(2, 0, 1))
    out_grad = wide(mixer_grads[3])
    return (
        to_blocks(result, jnp.bfloat16),
        to_blocks(input_grad, jnp.float32),
        small[:half],
        in_grad,
        conv_grad,
        out_grad,
        small[half : 2 * half],
        gate_grad,
        up_grad,
        down_grad,
    )


def solution(mesh):
    return jax.shard_map(
        body,
        mesh=mesh,
        in_specs=(
            P(("dp", "col"), "row"),
            P(("dp", "row")),
            P(("dp", "col"), "row"),
            P("row"),
            P("row", None, "col"),
            P(None, "col"),
            P("col", "row"),
            P("row"),
            P("row", "col"),
            P("row", "col"),
            P("col", "row"),
        ),
        out_specs=(
            P(("dp", "col"), "row"),
            P(("dp", "col"), "row"),
            P("row"),
            P("row", None, "col"),
            P(None, "col"),
            P("col", "row"),
            P("row"),
            P("row", "col"),
            P("row", "col"),
            P("col", "row"),
        ),
        check_vma=False,
    )
```

```python
import jax
import jax.numpy as jnp
from jax import lax
from jax.experimental import pallas as pl
from jax.experimental.pallas import tpu as pltpu
from jax.sharding import PartitionSpec as P

EPSILON = 1e-05
TEAM = 4


def dot_nt(left, right):
    return lax.dot_general(left, right, (((1,), (1,)), ((), ())), preferred_element_type=jnp.float32)


def dot_nn(left, right):
    return lax.dot_general(left, right, (((1,), (0,)), ((), ())), preferred_element_type=jnp.float32)


def dot_tn(left, right):
    return lax.dot_general(left, right, (((0,), (0,)), ((), ())), preferred_element_type=jnp.float32)


def over_dp(values, distance):
    size = lax.axis_size("dp")
    return lax.ppermute(values, "dp", [(i, i ^ distance) for i in range(size)])


def over_core(values):
    return over_dp(values, 1)


def over_x(values):
    return over_dp(values, 2)


def over_row(values):
    return lax.ppermute(values, "row", [(0, 1), (1, 0)])


def col_swap(values, distance):
    size = lax.axis_size("col")
    return lax.ppermute(values, "col", [(i, i ^ distance) for i in range(size)])


def narrow(values):
    return values.astype(jnp.bfloat16)


def wide(values):
    return values.astype(jnp.float32)


def halves(values):
    size = values.shape[0] // 2
    return values[:size], values[size:]


def other_teams(values):
    distance = TEAM
    while distance < lax.axis_size("dp"):
        values = values + over_dp(values, distance)
        distance *= 2
    return values


def after(value, *events):
    return lax.optimization_barrier((value, *events))[0]


def meet(*values):
    return lax.optimization_barrier(values)


def hop(move, value, *waiting):
    return meet(move(value), *waiting)


def stacked(pair, other, parts):
    pieces = jnp.concatenate([pair, other], axis=0)
    if parts > 1:
        pieces = pieces.reshape(4, parts, -1, pair.shape[2]).transpose(1, 0, 2, 3)
    return pieces.reshape(-1, pair.shape[2])


def col_first(piece):
    return jnp.stack([piece, col_swap(piece, 2)])


def col_send(values, parts):
    rows = values.shape[0] // (parts * 4)
    grid = values.reshape(parts, 2, 2 * rows, values.shape[1])
    return narrow(grid[:, 1]), grid[:, 0]


def col_add(kept, received):
    total = kept + wide(received)
    rows = total.shape[1] // 2
    return narrow(total[:, rows:]), total[:, :rows]


def col_last(kept, received):
    return (kept + wide(received)).reshape(-1, kept.shape[2])


def team_first(piece):
    return narrow(other_teams(piece))


def team_rows(own, far, pair, parts):
    rows, half = own.shape[0] // parts, own.shape[1]
    place = lax.axis_index("dp") % TEAM
    result = jnp.zeros((parts, TEAM * rows, half), jnp.bfloat16)
    for distance, block in enumerate((own, pair[0], far, pair[1])):
        block = block.reshape(parts, rows, half)
        result = lax.dynamic_update_slice(result, block, (0, (place ^ distance) * rows, 0))
    return result


def norm_scale(hidden):
    return lax.rsqrt(jnp.mean(hidden * hidden, axis=1, keepdims=True) + EPSILON)


def norm_backward(grad_normed, hidden, row_scale, gain_vector):
    inner_sum = jnp.sum(grad_normed * gain_vector * hidden, axis=1, keepdims=True)
    cubed = row_scale * row_scale * row_scale
    return grad_normed * gain_vector * row_scale - hidden * (cubed / hidden.shape[1]) * inner_sum


def to_blocks(values, received):
    size, half = values.shape
    row = lax.axis_index("row")
    result = jnp.zeros((2 * size, half), values.dtype)
    result = lax.dynamic_update_slice(result, values, (row * size, 0))
    return lax.dynamic_update_slice(result, received.astype(values.dtype), ((1 - row) * size, 0))


ROWS = 256
VMEM_BYTES = 48 * 2**20
COST = pl.CostEstimate(flops=1, bytes_accessed=1, transcendentals=0)


def whole(array):
    return pl.BlockSpec(array.shape, lambda i: (0,) * array.ndim)


def row_tiles(array):
    return pl.BlockSpec((ROWS, array.shape[1]), lambda i: (i, 0))


def token_call(kernel, tiled, resident, outs):
    tokens = tiled[0].shape[0]
    shapes = [jax.ShapeDtypeStruct((tokens, columns), dtype) for columns, dtype in outs]
    return pl.pallas_call(
        kernel,
        grid=(tokens // ROWS,),
        in_specs=[row_tiles(one) for one in tiled] + [whole(one) for one in resident],
        out_specs=[row_tiles(one) for one in shapes],
        out_shape=shapes,
        compiler_params=pltpu.CompilerParams(vmem_limit_bytes=VMEM_BYTES),
        cost_estimate=COST,
    )(*tiled, *resident)


def split_nt(left, near, row):
    half = near.shape[1]
    return dot_nt(left[:, :half], near[...]) + dot_nt(left[:, half:], row[...])


def forward_kernel(normed, gate_near, gate_row, up_near, up_row, gate, up, act):
    gate_value = split_nt(normed, gate_near, gate_row)
    up_value = split_nt(normed, up_near, up_row)
    gate[...] = narrow(gate_value)
    up[...] = narrow(up_value)
    act[...] = narrow(gate_value * jax.nn.sigmoid(gate_value) * up_value)


def backward_kernel(
    gate, up, cotangent, down_near, down_row, gate_near, gate_row, up_near, up_row, grad_gate, grad_up, back
):
    half = gate_near.shape[1]
    grad_act = split_nt(cotangent, down_near, down_row)
    gate_value, up_value = wide(gate[...]), wide(up[...])
    sigmoid_gate = jax.nn.sigmoid(gate_value)
    gated = grad_act * sigmoid_gate
    low_gate = narrow(gated * up_value * (1.0 + gate_value * (1.0 - sigmoid_gate)))
    low_up = narrow(gated * gate_value)
    grad_gate[...] = low_gate
    grad_up[...] = low_up
    back[:, :half] = narrow(dot_nn(low_gate, gate_near[...]) + dot_nn(low_up, up_near[...]))
    back[:, half:] = narrow(dot_nn(low_gate, gate_row[...]) + dot_nn(low_up, up_row[...]))


def out_kernel(act, down_near, down_row, out):
    half = down_near.shape[1]
    out[:, :half] = narrow(dot_nn(act[...], down_near[...]))
    out[:, half:] = narrow(dot_nn(act[...], down_row[...]))


def project_kernel(inputs, gain, in_near, in_row, normed, projected):
    values = wide(inputs[...])
    scale = lax.rsqrt(jnp.mean(values * values, axis=1, keepdims=True) + EPSILON)
    low = narrow(values * scale * gain[...])
    normed[...] = low
    projected[...] = split_nt(low, in_near, in_row)


def mixer_values(projected, flags, before, taps):
    width = taps.shape[1]
    input_gate, output_gate, values_part = (projected[:, part * width : (part + 1) * width] for part in range(3))
    mix_input = input_gate * values_part
    place = lax.broadcasted_iota(jnp.int32, mix_input.shape, 0)
    one, two = before[0, 1:2], before[0, 0:1]
    prior_one = flags[:, 0:1] * jnp.where(place == 0, one, pltpu.roll(mix_input, 1, 0))
    prior_two = jnp.where(place == 0, two, jnp.where(place == 1, one, pltpu.roll(mix_input, 2, 0)))
    prior_two = flags[:, 1:2] * prior_two
    convolved = taps[2:3] * mix_input + taps[1:2] * prior_one + taps[0:1] * prior_two
    return input_gate, output_gate, values_part, mix_input, prior_one, prior_two, convolved


def mix_kernel(projected, flags, before, taps, out_near, out_row, mixed, partial):
    half = out_near.shape[1]
    _, output_gate, _, _, _, _, convolved = mixer_values(projected, flags, before, taps)
    low = narrow(output_gate * convolved)
    mixed[...] = low
    partial[:, :half] = narrow(dot_nn(low, out_near[...]))
    partial[:, half:] = narrow(dot_nn(low, out_row[...]))


def mix_back_kernel(
    grad_mixed, projected, flags, before, behind, taps, out_near, out_row, in_near, in_row, grad_projected, partial, sums
):
    half = out_near.shape[1]
    width = taps.shape[1]
    input_gate, output_gate, values_part, mix_input, prior_one, prior_two, convolved = mixer_values(
        projected, flags, before, taps
    )
    grad_y = split_nt(grad_mixed, out_near, out_row)
    grad_conv = grad_y * output_gate
    for tap, values in enumerate((prior_two, prior_one, mix_input)):
        sums[0, tap : tap + 1] = jnp.sum(grad_conv * values, axis=0, keepdims=True)
    size = grad_conv.shape[0]
    place = lax.broadcasted_iota(jnp.int32, grad_conv.shape, 0)
    one, two = behind[0, 0:1], behind[0, 1:2]
    next_one = jnp.where(place == size - 1, one, pltpu.roll(grad_conv, size - 1, 0))
    next_two = jnp.where(place == size - 2, one, pltpu.roll(grad_conv, size - 2, 0))
    next_two = jnp.where(place == size - 1, two, next_two)
    grad_mix = (
        taps[2:3] * grad_conv
        + taps[1:2] * (flags[:, 2:3] * next_one)
        + taps[0:1] * (flags[:, 3:4] * next_two)
    )
    low = narrow(jnp.concatenate([grad_mix * values_part, grad_y * convolved, grad_mix * input_gate], axis=1))
    grad_projected[...] = low
    partial[:, :half] = narrow(dot_nn(low, in_near[...]))
    partial[:, half:] = narrow(dot_nn(low, in_row[...]))


def sequence_call(kernel, tiled, small, resident, outs, small_outs=()):
    size = tiled[0].shape[0] // 2

    def by_rows(array):
        return pl.BlockSpec((size, array.shape[1]), lambda i: (i, 0))

    def by_first(array):
        return pl.BlockSpec((1, *array.shape[1:]), lambda i: (i, 0, 0))

    shapes = [jax.ShapeDtypeStruct((2 * size, columns), dtype) for columns, dtype in outs]
    small_shapes = [jax.ShapeDtypeStruct((2, *shape), jnp.float32) for shape in small_outs]
    return pl.pallas_call(
        kernel,
        grid=(2,),
        in_specs=[by_rows(one) for one in tiled] + [by_first(one) for one in small] + [whole(one) for one in resident],
        out_specs=[by_rows(one) for one in shapes] + [by_first(one) for one in small_shapes],
        out_shape=shapes + small_shapes,
        compiler_params=pltpu.CompilerParams(vmem_limit_bytes=VMEM_BYTES),
        cost_estimate=COST,
    )(*tiled, *small, *resident)


def weight_kernel(left_near, left_far, right_near, right_far, own, sent):
    total = dot_tn(left_near[...], right_near[...]) + dot_tn(left_far[...], right_far[...])
    half = own.shape[1]
    own[...] = total[:, :half]
    sent[...] = narrow(total[:, half:])


def weight_grads(lefts, rights, tile):
    tokens, columns = lefts[0].shape
    half = rights[0].shape[1] // 2
    left_spec = pl.BlockSpec((tokens, tile), lambda i: (0, i))
    out_spec = pl.BlockSpec((tile, half), lambda i: (i, 0))
    return pl.pallas_call(
        weight_kernel,
        grid=(columns // tile,),
        in_specs=[left_spec, left_spec, whole(rights[0]), whole(rights[1])],
        out_specs=[out_spec, out_spec],
        out_shape=[
            jax.ShapeDtypeStruct((columns, half), jnp.float32),
            jax.ShapeDtypeStruct((columns, half), jnp.bfloat16),
        ],
        compiler_params=pltpu.CompilerParams(vmem_limit_bytes=VMEM_BYTES),
        cost_estimate=COST,
    )(*lefts, *rights)


def body(
    tokens,
    segment_ids,
    cotangent,
    norm1_gain,
    in_weight,
    conv_weight,
    out_weight,
    norm2_gain,
    gate_weight,
    up_weight,
    down_weight,
):
    place = lax.axis_index("dp") % TEAM
    row = lax.axis_index("row")
    col = lax.axis_index("col")
    cols = lax.axis_size("col")
    sequence = tokens.shape[0]
    size = sequence // 2
    half = tokens.shape[1]

    tokens_other = lax.dynamic_slice_in_dim(tokens, (1 - row) * size, size, 0)
    tokens_own = lax.dynamic_slice_in_dim(tokens, row * size, size, 0)
    tokens_row = over_row(tokens_other)
    tokens_x0 = over_x(tokens_own)
    channels = in_weight.shape[2] // TEAM
    hidden = gate_weight.shape[1] // TEAM
    in_part = lax.dynamic_slice_in_dim(in_weight, place * channels, channels, 2)
    in_part = in_part.transpose(1, 2, 0).reshape(3 * channels, half)
    out_part = lax.dynamic_slice_in_dim(out_weight, place * channels, channels, 0)
    taps_part = lax.dynamic_slice_in_dim(conv_weight, place * channels, channels, 1)
    taps_part = jnp.pad(taps_part, ((0, 0), (0, half - channels)))
    gains_part = jnp.pad(jnp.stack([norm1_gain, norm2_gain]), ((0, 11), (0, 0)))
    in_pair = col_first(jnp.concatenate([in_part, taps_part, gains_part, out_part], axis=0))
    grads_other = lax.dynamic_slice_in_dim(cotangent, (1 - row) * size, size, 0)
    grads_own = lax.dynamic_slice_in_dim(cotangent, row * size, size, 0)
    gate_part = lax.dynamic_slice_in_dim(gate_weight, place * hidden, hidden, 1).T
    ids_row = over_row(segment_ids)
    in_pair, tokens_row, tokens_x0, ids_row, grads_other, gate_part = meet(
        in_pair, tokens_row, tokens_x0, ids_row, grads_other, gate_part
    )

    in_other = col_swap(in_pair, 1)
    tokens_x1 = over_x(tokens_row)
    grads_row = over_row(grads_other)
    gate_pair = col_first(gate_part)
    up_part = lax.dynamic_slice_in_dim(up_weight, place * hidden, hidden, 1).T
    down_part = lax.dynamic_slice_in_dim(down_weight, place * hidden, hidden, 0)
    ids = jnp.stack([segment_ids, ids_row])
    ids = lax.dynamic_index_in_dim(ids, (col // 2) ^ row, 0, keepdims=False)
    ids = lax.dynamic_slice_in_dim(ids, (col % 2) * sequence, sequence, 0)
    ids_far = over_x(ids)
    in_other, tokens_x1, grads_row, ids_far, gate_pair, grads_own, ids, up_part, down_part = meet(
        in_other, tokens_x1, grads_row, ids_far, gate_pair, grads_own, ids, up_part, down_part
    )
    in_rows = 3 * channels
    in_near = stacked(in_pair[:, :in_rows], in_other[:, :in_rows], 3)
    in_near = jnp.concatenate([in_near, in_pair[0, in_rows : in_rows + 16]], axis=0)
    out_near = stacked(in_pair[:, in_rows + 16 :], in_other[:, in_rows + 16 :], 1)
    grads_near = jnp.concatenate([grads_own, grads_row], axis=1)
    in_near, out_near, grads_near, up_part, tokens_x1, gate_pair, ids = meet(
        in_near, out_near, grads_near, up_part, tokens_x1, gate_pair, ids
    )

    near = jnp.concatenate([tokens_own, tokens_row], axis=1)
    far = jnp.concatenate([tokens_x0, tokens_x1], axis=1)
    pair, ids_pair = over_core(jnp.stack([near, far])), over_core(jnp.stack([ids, ids_far]))
    pair, ids_pair, in_near, out_near, in_other, grads_near, gate_pair, up_part = meet(
        pair, ids_pair, in_near, out_near, in_other, grads_near, gate_pair, up_part
    )
    in_row = over_row(in_near)
    out_row = over_row(out_near)
    gate_other = col_swap(gate_pair, 1)
    up_pair = col_first(up_part)
    grads_far = over_x(grads_near)
    ids = jnp.stack([ids, ids_pair[0], ids_far, ids_pair[1]])
    keeps = []
    for offset in (1, 2):
        equal = (ids[:, offset:] == ids[:, :-offset]).astype(jnp.float32)
        keeps.append(jnp.pad(equal, ((0, 0), (offset, offset))))
    flags = jnp.stack(
        [
            lax.dynamic_slice_in_dim(keeps[which], row * size + offset, size, 1)
            for which, offset in ((0, 0), (1, 0), (0, 1), (1, 2))
        ],
        axis=2,
    )
    flags = [flags[:2].reshape(2 * size, 4), flags[2:].reshape(2 * size, 4)]
    near_tokens, far_tokens = (near, pair[0]), (far, pair[1])
    inputs = [jnp.concatenate(both, axis=0) for both in (near_tokens, far_tokens)]
    taps = jnp.concatenate(
        [both[which, in_rows : in_rows + 3, :channels] for both in (in_pair, in_other) for which in (0, 1)], axis=1
    )
    taps = wide(taps)
    in_row, out_row, gate_other, up_pair, inputs, taps, flags, down_part = meet(
        in_row, out_row, gate_other, up_pair, inputs, taps, flags, down_part
    )

    width = cols * channels
    gains = jnp.stack([norm1_gain, norm2_gain])
    gains = wide(jnp.concatenate([gains, in_row[4 * in_rows + 3 : 4 * in_rows + 5]], axis=1))
    gain_one, gain_two = gains[0], gains[1]
    in_near, in_row = in_near[: 4 * in_rows], in_row[: 4 * in_rows]
    ends = wide(jnp.concatenate([one[at + size - 8 : at + size] for one in inputs for at in (0, size)], axis=0))
    ends = narrow(ends * norm_scale(ends) * gain_one)
    ends = dot_nt(ends[:, :half], in_near) + dot_nt(ends[:, half:], in_row)
    ends = (ends[:, :width] * ends[:, 2 * width :]).reshape(2, 2, 8, width)[:, :, 6:]
    gate_near = stacked(gate_pair, gate_other, 1)
    before, gate_near, up_pair, down_part, inputs = hop(over_row, ends, gate_near, up_pair, down_part, inputs)
    gate_row = over_row(gate_near)
    up_other = col_swap(up_pair, 1)
    down_pair = col_first(down_part)
    grads_pair = over_core(jnp.stack([grads_near, grads_far]))
    normed_one, projected = zip(
        *[
            token_call(
                project_kernel,
                [one],
                (gain_one[None], in_near, in_row),
                ((2 * half, jnp.bfloat16), (3 * width, jnp.float32)),
            )
            for one in inputs
        ]
    )

    def mix(which):
        return sequence_call(
            mix_kernel,
            [projected[which], flags[which]],
            [before[which]],
            (taps, out_near, out_row),
            ((width, jnp.bfloat16), (2 * half, jnp.bfloat16)),
        )

    def core_sum(partial, *waiting):
        received, *waiting = hop(over_core, narrow(partial[size:]), *waiting)
        return (wide(partial[:size]) + wide(received), *waiting)

    mixed = [None, None]
    mixed[1], far_partial = mix(1)
    mixed[0], near_partial = mix(0)
    up_other, down_pair, gate_row, grads_pair, far_partial, near_partial = meet(
        up_other, down_pair, gate_row, grads_pair, far_partial, near_partial
    )
    up_near = stacked(up_pair, up_other, 1)
    near_grads, far_grads = (grads_near, grads_pair[0]), (grads_far, grads_pair[1])
    cotangents = [jnp.concatenate(both, axis=0) for both in (near_grads, far_grads)]
    received, far_partial, near_partial, up_near, down_pair, cotangents = hop(
        over_core,
        jnp.stack([near_partial[size:], far_partial[size:]]),
        far_partial,
        near_partial,
        up_near,
        down_pair,
        cotangents,
    )
    far_sum = wide(far_partial[:size]) + wide(received[1])
    near_sum = wide(near_partial[:size]) + wide(received[0])
    from_far, to_far = over_x(narrow(far_sum)), over_x(narrow(near_sum))
    up_row = over_row(up_near)
    down_other = col_swap(down_pair, 1)
    from_far, down_other, up_row = meet(from_far, down_other, up_row)
    down_near = stacked(down_pair, down_other, 1)
    from_far, down_near = meet(from_far, down_near)
    down_row = over_row(down_near)
    hidden_near = wide(near_tokens[0]) + (near_sum + wide(from_far))
    scale_near = norm_scale(hidden_near)
    normed_own = narrow(hidden_near * scale_near * gain_two)
    to_far, normed_own = meet(to_far, normed_own)
    hidden_far = wide(far_tokens[0]) + (far_sum + wide(to_far))
    scale_far = norm_scale(hidden_far)
    normed_x = narrow(hidden_far * scale_far * gain_two)
    down_row, normed_own, normed_x = meet(down_row, normed_own, normed_x)
    (pair,) = hop(over_core, jnp.stack([normed_own, normed_x]))
    normed_near = jnp.concatenate([normed_own, pair[0]], axis=0)
    normed_far = jnp.concatenate([normed_x, pair[1]], axis=0)
    hiddens, scale_two, normed_two = (hidden_near, hidden_far), (scale_near, scale_far), (normed_near, normed_far)
    units = gate_near.shape[0]
    weights = (gate_near, gate_row, up_near, up_row)
    wide_outs = ((units, jnp.bfloat16),) * 3

    grad_gate, grad_up = [None, None], [None, None]

    def hidden_back(which, gate_value, up_value):
        grad_gate[which], grad_up[which], back = token_call(
            backward_kernel,
            [gate_value, up_value, cotangents[which]],
            (down_near, down_row, *weights),
            ((units, jnp.bfloat16), (units, jnp.bfloat16), (2 * half, jnp.bfloat16)),
        )
        return back

    def exchange(partial):
        return partial[:, :half], narrow(partial[:, half:])

    gate_value, up_value, act_near = token_call(forward_kernel, [normed_near], weights, wide_outs)
    near_back, normed_far = core_sum(hidden_back(0, gate_value, up_value), normed_far)
    near_send, normed_far = meet(narrow(near_back), normed_far)
    back_to_far = over_x(near_send)
    gate_value, up_value, act_far = token_call(forward_kernel, [normed_far], weights, wide_outs)
    far_partial = hidden_back(1, gate_value, up_value)
    act, normed_two = [act_near, act_far], [normed_near, normed_far]
    back_to_far, far_partial, grad_gate, grad_up, act = meet(back_to_far, far_partial, grad_gate, grad_up, act)
    far_back, grad_gate, grad_up, act = core_sum(far_partial, grad_gate, grad_up, act)
    far_send, grad_gate, grad_up, act = meet(narrow(far_back), grad_gate, grad_up, act)
    back_from_far = over_x(far_send)
    gate_own, gate_sent = weight_grads(grad_gate, normed_two, units // 3)
    gate_moved = over_row(gate_sent)
    gate_sent, grad_up, act = meet(gate_sent, grad_up, act)
    down_own, down_sent = weight_grads(act, cotangents, units // 3)
    down_sent, down_kept = col_send(jnp.concatenate([down_own, wide(down_sent)], axis=1), 1)
    down_moved = col_swap(down_sent, 1)
    down_sent, grad_up, act = meet(down_sent, grad_up, act)
    up_own, up_sent = weight_grads(grad_up, normed_two, units // 3)
    outs = [token_call(out_kernel, [one], (down_near, down_row), ((2 * half, jnp.bfloat16),))[0] for one in act]
    back_from_far, outs, up_sent = meet(back_from_far, outs, up_sent)

    back_sums = (near_back + wide(back_from_far), far_back + wide(back_to_far))
    grad_hidden, low = [], []
    for which, cotangent_rows in ((0, near_grads[0]), (1, far_grads[0])):
        grads = wide(cotangent_rows) + norm_backward(
            back_sums[which], hiddens[which], scale_two[which], gain_two
        )
        grad_hidden.append(grads)
        low.append(narrow(grads))
    gain_two_grad = jnp.sum(back_sums[0] * hidden_near * scale_two[0], axis=0)
    gate_moved, down_moved, low = meet(gate_moved, down_moved, low)
    gate_sent, gate_kept = col_send(gate_own + wide(gate_moved), 1)
    down_sent, down_kept = col_add(down_kept, down_moved)
    low_moved, out_moved = over_core(jnp.stack(low)), over_core(jnp.stack([outs[0][size:], outs[1][size:]]))
    low_moved, out_moved, low, outs, up_sent, gate_sent, down_sent = meet(
        low_moved, out_moved, low, outs, up_sent, gate_sent, down_sent
    )
    grad_mixed = [jnp.concatenate([low[which], low_moved[which]], axis=0) for which in (0, 1)]
    near_out, far_out = (wide(out[:size]) + wide(out_moved[which]) for which, out in enumerate(outs))
    far_out = narrow(far_out)

    starts = jnp.concatenate([one[at : at + 8] for one in grad_mixed for at in (0, size)], axis=0)
    starts = dot_nt(starts[:, :half], out_near) + dot_nt(starts[:, half:], out_row)
    opened = jnp.concatenate([one[at : at + 8, width : 2 * width] for one in projected for at in (0, size)], axis=0)
    starts = (starts * opened).reshape(2, 2, 8, width)[:, :, :2]
    behind, grad_mixed, up_sent, gate_sent, down_sent, far_out, near_out = hop(
        over_row, starts, grad_mixed, up_sent, gate_sent, down_sent, far_out, near_out
    )
    up_moved = over_row(up_sent)
    gate_moved = col_swap(gate_sent, 1)
    down_moved = col_swap(down_sent, 2)
    out_from_far = over_x(far_out)

    def mix_back(which):
        return sequence_call(
            mix_back_kernel,
            [grad_mixed[which], projected[which], flags[which]],
            [before[which], behind[which]],
            (taps, out_near, out_row, in_near, in_row),
            ((3 * width, jnp.bfloat16), (2 * half, jnp.bfloat16)),
            ((3, width),),
        )

    grad_projected = [None, None]
    grad_projected[1], far_one, far_taps = mix_back(1)
    far_one, grad_mixed = meet(far_one, grad_mixed)
    grad_projected[0], near_one, near_taps = mix_back(0)
    in_own, in_sent = weight_grads(grad_projected, normed_one, width)
    out_own, out_sent = weight_grads(mixed, grad_mixed, width)
    mixer_own = jnp.concatenate([in_own, out_own], axis=0)
    mixer_sent = jnp.concatenate([in_sent, out_sent], axis=0)
    out_from_far, up_moved, gate_moved, down_moved, far_one, near_one, mixer_sent = meet(
        out_from_far, up_moved, gate_moved, down_moved, far_one, near_one, mixer_sent
    )
    gate_sent, gate_kept = col_add(gate_kept, gate_moved)
    up_sent, up_kept = col_send(up_own + wide(up_moved), 1)
    down_own, down_sent = exchange(col_last(down_kept, down_moved))
    received, far_one, near_one, mixer_sent, up_sent, gate_sent, down_sent = hop(
        over_core,
        jnp.stack([near_one[size:], far_one[size:]]),
        far_one,
        near_one,
        mixer_sent,
        up_sent,
        gate_sent,
        down_sent,
    )
    mixer_moved = over_row(mixer_sent)
    up_moved = col_swap(up_sent, 1)
    gate_moved = col_swap(gate_sent, 2)
    far_one = narrow(wide(far_one[:size]) + wide(received[1]))
    one_from_far = over_x(far_one)
    near_one = wide(near_one[:size]) + wide(received[0])
    result = narrow(hidden_near + (near_out + wide(out_from_far)))
    conv_local = jnp.sum(near_taps + far_taps, axis=0)
    one_from_far, mixer_moved, up_moved, gate_moved, near_one, result, down_sent = meet(
        one_from_far, mixer_moved, up_moved, gate_moved, near_one, result, down_sent
    )
    mixer_sent, mixer_kept = col_send(mixer_own + wide(mixer_moved), 4)
    up_sent, up_kept = col_add(up_kept, up_moved)
    gate_total = team_first(col_last(gate_kept, gate_moved))
    mixer_sent, up_sent, gate_total, one_from_far, near_one, down_sent = meet(
        mixer_sent, up_sent, gate_total, one_from_far, near_one, down_sent
    )
    mixer_moved = col_swap(mixer_sent, 1)
    up_moved = col_swap(up_sent, 2)
    gate_far = over_x(gate_total)
    down_from_row = over_row(down_sent)
    grad_normed_one = near_one + wide(one_from_far)
    own_inputs = wide(near_tokens[0])
    own_scale = norm_scale(own_inputs)
    input_grad = grad_hidden[0] + norm_backward(grad_normed_one, own_inputs, own_scale, gain_one)
    gain_one_grad = jnp.sum(grad_normed_one * own_inputs * own_scale, axis=0)
    mixer_moved, up_moved, gate_far, down_from_row, input_grad, gain_one_grad = meet(
        mixer_moved, up_moved, gate_far, down_from_row, input_grad, gain_one_grad
    )
    mixer_sent, mixer_kept = col_add(mixer_kept, mixer_moved)
    mixer_sent, up_moved, down_from_row, gate_far, input_grad, result, gain_one_grad = meet(
        mixer_sent, up_moved, down_from_row, gate_far, input_grad, result, gain_one_grad
    )
    mixer_moved = col_swap(mixer_sent, 2)
    up_total = team_first(col_last(up_kept, up_moved))
    down_total = team_first(down_own + wide(down_from_row))
    both = jnp.stack([up_total, down_total])
    both_far = over_x(both)
    input_row = over_row(narrow(input_grad[:, half:]))
    gate_pair = over_core(jnp.stack([gate_total, gate_far]))
    mixer_moved, both_far, gate_pair, result, input_row = meet(mixer_moved, both_far, gate_pair, result, input_row)
    mixer_total = team_first(col_last(mixer_kept, mixer_moved))
    mixer_total, both_far, gate_pair, result, gain_one_grad = meet(
        mixer_total, both_far, gate_pair, result, gain_one_grad
    )
    mixer_far = over_x(mixer_total)
    result_row = over_row(result[:, half:])
    both_pair = over_core(jnp.stack([both, both_far]))
    gate_grad = wide(team_rows(gate_total, gate_far, gate_pair, 1)[0].T)
    mixer_far, both_pair = meet(mixer_far, both_pair)
    up_grad = wide(team_rows(up_total, both_far[0], both_pair[:, 0], 1)[0].T)
    down_grad = wide(team_rows(down_total, both_far[1], both_pair[:, 1], 1)[0])
    mixer_pair = over_core(jnp.stack([mixer_total, mixer_far]))
    mixer_grads = team_rows(mixer_total, mixer_far, mixer_pair, 4)
    in_grad = wide(mixer_grads[:3].transpose(2, 0, 1))
    out_grad = wide(mixer_grads[3])

    gain_local = jnp.stack([gain_one_grad, gain_two_grad])
    conv_flat = conv_local.reshape(3, cols, channels).transpose(1, 0, 2).reshape(cols, 3 * channels)
    apart = jnp.arange(cols) ^ col
    conv_flat = jnp.take(conv_flat, apart // 2 + apart % 2 * 2, axis=0).reshape(-1)
    sent = jnp.concatenate([gain_local[:, half:].reshape(-1), conv_flat])
    small = jnp.concatenate([gain_local[:, :half].reshape(-1), conv_flat]) + over_row(sent)
    for distance in (1, 2):
        small = small + col_swap(small, distance)
    conv_own = lax.dynamic_slice_in_dim(small[2 * half :], col * 3 * channels, 3 * channels, 0)
    conv_wide = lax.dynamic_update_slice(
        jnp.zeros((TEAM * 3 * channels,), jnp.float32), conv_own, (place * 3 * channels,)
    )
    small = jnp.concatenate([small[: 2 * half], conv_wide])
    small = small + over_x(small)
    small = small + over_core(small)
    small = other_teams(small)
    conv_grad = small[2 * half :].reshape(TEAM, 3, channels).transpose(1, 0, 2).reshape(3, TEAM * channels)

    return (
        to_blocks(result[:, :half], result_row),
        to_blocks(input_grad[:, :half], input_row),
        small[:half],
        in_grad,
        conv_grad,
        out_grad,
        small[half : 2 * half],
        gate_grad,
        up_grad,
        down_grad,
    )


def solution(mesh):
    return jax.shard_map(
        body,
        mesh=mesh,
        in_specs=(
            P(("dp", "col"), "row"),
            P(("dp", "row")),
            P(("dp", "col"), "row"),
            P("row"),
            P("row", None, "col"),
            P(None, "col"),
            P("col", "row"),
            P("row"),
            P("row", "col"),
            P("row", "col"),
            P("col", "row"),
        ),
        out_specs=(
            P(("dp", "col"), "row"),
            P(("dp", "col"), "row"),
            P("row"),
            P("row", None, "col"),
            P(None, "col"),
            P("col", "row"),
            P("row"),
            P("row", "col"),
            P("row", "col"),
            P("col", "row"),
        ),
        check_vma=False,
    )
```

```python
import jax
import jax.numpy as jnp
from jax import lax
from jax.experimental import pallas as pl
from jax.experimental.pallas import tpu as pltpu
from jax.sharding import PartitionSpec as P

EPSILON = 1e-05
TEAM = 4


def dot_nt(left, right):
    return lax.dot_general(left, right, (((1,), (1,)), ((), ())), preferred_element_type=jnp.float32)


def dot_nn(left, right):
    return lax.dot_general(left, right, (((1,), (0,)), ((), ())), preferred_element_type=jnp.float32)


def dot_tn(left, right):
    return lax.dot_general(left, right, (((0,), (0,)), ((), ())), preferred_element_type=jnp.float32)


def over_dp(values, distance):
    size = lax.axis_size("dp")
    return lax.ppermute(values, "dp", [(i, i ^ distance) for i in range(size)])


def over_core(values):
    return over_dp(values, 1)


def over_x(values):
    return over_dp(values, 2)


def over_row(values):
    return lax.ppermute(values, "row", [(0, 1), (1, 0)])


def col_swap(values, distance):
    size = lax.axis_size("col")
    return lax.ppermute(values, "col", [(i, i ^ distance) for i in range(size)])


def narrow(values):
    return values.astype(jnp.bfloat16)


def wide(values):
    return values.astype(jnp.float32)


def halves(values):
    size = values.shape[0] // 2
    return values[:size], values[size:]


def other_teams(values):
    distance = TEAM
    while distance < lax.axis_size("dp"):
        values = values + over_dp(values, distance)
        distance *= 2
    return values


def after(value, *events):
    return lax.optimization_barrier((value, *events))[0]


def meet(*values):
    return lax.optimization_barrier(values)


def hop(move, value, *waiting):
    return meet(move(value), *waiting)


def stacked(pair, other, parts):
    pieces = jnp.concatenate([pair, other], axis=0)
    if parts > 1:
        pieces = pieces.reshape(4, parts, -1, pair.shape[2]).transpose(1, 0, 2, 3)
    return pieces.reshape(-1, pair.shape[2])


def col_first(piece):
    return jnp.stack([piece, col_swap(piece, 2)])


def col_send(values, parts):
    rows = values.shape[0] // (parts * 4)
    grid = values.reshape(parts, 2, 2 * rows, values.shape[1])
    return narrow(grid[:, 1]), grid[:, 0]


def col_add(kept, received):
    total = kept + wide(received)
    rows = total.shape[1] // 2
    return narrow(total[:, rows:]), total[:, :rows]


def col_last(kept, received):
    return (kept + wide(received)).reshape(-1, kept.shape[2])


def team_first(piece):
    return narrow(other_teams(piece))


def team_rows(own, far, pair, parts):
    rows, half = own.shape[0] // parts, own.shape[1]
    place = lax.axis_index("dp") % TEAM
    result = jnp.zeros((parts, TEAM * rows, half), jnp.bfloat16)
    for distance, block in enumerate((own, pair[0], far, pair[1])):
        block = block.reshape(parts, rows, half)
        result = lax.dynamic_update_slice(result, block, (0, (place ^ distance) * rows, 0))
    return result


def norm_scale(hidden):
    return lax.rsqrt(jnp.mean(hidden * hidden, axis=1, keepdims=True) + EPSILON)


def norm_backward(grad_normed, hidden, row_scale, gain_vector):
    inner_sum = jnp.sum(grad_normed * gain_vector * hidden, axis=1, keepdims=True)
    cubed = row_scale * row_scale * row_scale
    return grad_normed * gain_vector * row_scale - hidden * (cubed / hidden.shape[1]) * inner_sum


def to_blocks(values, received):
    size, half = values.shape
    row = lax.axis_index("row")
    result = jnp.zeros((2 * size, half), values.dtype)
    result = lax.dynamic_update_slice(result, values, (row * size, 0))
    return lax.dynamic_update_slice(result, received.astype(values.dtype), ((1 - row) * size, 0))


ROWS = 256
COST = pl.CostEstimate(flops=1, bytes_accessed=1, transcendentals=0)


def whole(array):
    return pl.BlockSpec(array.shape, lambda i: (0,) * array.ndim)


def row_tiles(array):
    return pl.BlockSpec((ROWS, array.shape[1]), lambda i: (i, 0))


def token_call(kernel, tiled, resident, outs):
    tokens = tiled[0].shape[0]
    shapes = [jax.ShapeDtypeStruct((tokens, columns), dtype) for columns, dtype in outs]
    return pl.pallas_call(
        kernel,
        grid=(tokens // ROWS,),
        in_specs=[row_tiles(one) for one in tiled] + [whole(one) for one in resident],
        out_specs=[row_tiles(one) for one in shapes],
        out_shape=shapes,
        compiler_params=pltpu.CompilerParams(vmem_limit_bytes=20 * 2**20),
        cost_estimate=COST,
    )(*tiled, *resident)


def split_nt(left, near, row):
    half = near.shape[1]
    return dot_nt(left[:, :half], near[...]) + dot_nt(left[:, half:], row[...])


def gated_kernel(
    normed, cotangent, gate_near, gate_row, up_near, up_row, down_near, down_row,
    act, grad_gate, grad_up, back_own, back_sent, out_own, out_sent,
):
    gate_value = split_nt(normed, gate_near, gate_row)
    up_value = split_nt(normed, up_near, up_row)
    grad_act = split_nt(cotangent, down_near, down_row)
    sigmoid_gate = jax.nn.sigmoid(gate_value)
    silu = gate_value * sigmoid_gate
    low_act = narrow(silu * up_value)
    low_gate = narrow(grad_act * up_value * (sigmoid_gate * (1.0 + gate_value * (1.0 - sigmoid_gate))))
    low_up = narrow(grad_act * silu)
    act[...] = low_act
    grad_gate[...] = low_gate
    grad_up[...] = low_up
    back = jnp.concatenate(
        [
            narrow(dot_nn(low_gate, gate_near[...]) + dot_nn(low_up, up_near[...])),
            narrow(dot_nn(low_gate, gate_row[...]) + dot_nn(low_up, up_row[...])),
        ],
        axis=1,
    )
    out = jnp.concatenate(
        [narrow(dot_nn(low_act, down_near[...])), narrow(dot_nn(low_act, down_row[...]))], axis=1
    )
    own_or_sent(back, back_own, back_sent)
    own_or_sent(out, out_own, out_sent)


def gated_call(normed, cotangent, weights):
    tokens, width = normed.shape
    units = weights[0].shape[0]
    steps = tokens // ROWS
    wide_out = jax.ShapeDtypeStruct((tokens, units), jnp.bfloat16)
    part_out = jax.ShapeDtypeStruct((tokens // 2, width), jnp.bfloat16)
    own = pl.BlockSpec((ROWS, width), lambda i: (jnp.minimum(i, steps // 2 - 1), 0))
    sent = pl.BlockSpec((ROWS, width), lambda i: (jnp.maximum(i - steps // 2, 0), 0))
    return pl.pallas_call(
        gated_kernel,
        grid=(steps,),
        in_specs=[row_tiles(normed), row_tiles(cotangent)] + [whole(one) for one in weights],
        out_specs=[row_tiles(wide_out)] * 3 + [own, sent] * 2,
        out_shape=[wide_out] * 3 + [part_out] * 4,
        compiler_params=pltpu.CompilerParams(vmem_limit_bytes=36 * 2**20),
        cost_estimate=COST,
    )(normed, cotangent, *weights)


def project_kernel(inputs, gain, in_near, in_row, normed, projected):
    values = wide(inputs[...])
    scale = lax.rsqrt(jnp.mean(values * values, axis=1, keepdims=True) + EPSILON)
    low = narrow(values * scale * gain[...])
    normed[...] = low
    projected[...] = split_nt(low, in_near, in_row)


def mixer_values(projected, flags, before, taps):
    width = taps.shape[1]
    input_gate, output_gate, values_part = (projected[:, part * width : (part + 1) * width] for part in range(3))
    mix_input = input_gate * values_part
    place = lax.broadcasted_iota(jnp.int32, mix_input.shape, 0)
    one, two = before[0, 1:2], before[0, 0:1]
    prior_one = flags[:, 0:1] * jnp.where(place == 0, one, pltpu.roll(mix_input, 1, 0))
    prior_two = jnp.where(place == 0, two, jnp.where(place == 1, one, pltpu.roll(mix_input, 2, 0)))
    prior_two = flags[:, 1:2] * prior_two
    convolved = taps[2:3] * mix_input + taps[1:2] * prior_one + taps[0:1] * prior_two
    return input_gate, output_gate, values_part, mix_input, prior_one, prior_two, convolved


def own_or_sent(partial, own, sent):
    first = pl.program_id(0) < pl.num_programs(0) // 2

    @pl.when(first)
    def _():
        own[...] = partial

    @pl.when(jnp.logical_not(first))
    def _():
        sent[...] = partial


def mix_kernel(projected, flags, before, taps, out_near, out_row, mixed, own, sent):
    _, output_gate, _, _, _, _, convolved = mixer_values(projected, flags, before, taps)
    low = narrow(output_gate * convolved)
    mixed[...] = low
    partial = narrow(jnp.concatenate([dot_nn(low, out_near[...]), dot_nn(low, out_row[...])], axis=1))
    own_or_sent(partial, own, sent)


def mix_back_kernel(
    grad_mixed, projected, flags, before, behind, taps, out_near, out_row, in_near, in_row,
    grad_projected, sums, own, sent,
):
    width = taps.shape[1]
    input_gate, output_gate, values_part, mix_input, prior_one, prior_two, convolved = mixer_values(
        projected, flags, before, taps
    )
    grad_y = split_nt(grad_mixed, out_near, out_row)
    grad_conv = grad_y * output_gate
    for tap, values in enumerate((prior_two, prior_one, mix_input)):
        sums[0, tap : tap + 1] = jnp.sum(grad_conv * values, axis=0, keepdims=True)
    size = grad_conv.shape[0]
    place = lax.broadcasted_iota(jnp.int32, grad_conv.shape, 0)
    one, two = behind[0, 0:1], behind[0, 1:2]
    next_one = jnp.where(place == size - 1, one, pltpu.roll(grad_conv, size - 1, 0))
    next_two = jnp.where(place == size - 2, one, pltpu.roll(grad_conv, size - 2, 0))
    next_two = jnp.where(place == size - 1, two, next_two)
    grad_mix = (
        taps[2:3] * grad_conv
        + taps[1:2] * (flags[:, 2:3] * next_one)
        + taps[0:1] * (flags[:, 3:4] * next_two)
    )
    low = narrow(jnp.concatenate([grad_mix * values_part, grad_y * convolved, grad_mix * input_gate], axis=1))
    grad_projected[...] = low
    partial = narrow(jnp.concatenate([dot_nn(low, in_near[...]), dot_nn(low, in_row[...])], axis=1))
    own_or_sent(partial, own, sent)


def sequence_call(kernel, tiled, small, resident, outs, small_outs=()):
    size = tiled[0].shape[0] // 2

    def by_rows(array):
        return pl.BlockSpec((size, array.shape[1]), lambda i: (i, 0))

    def by_first(array):
        return pl.BlockSpec((1, *array.shape[1:]), lambda i: (i, 0, 0))

    shapes = [jax.ShapeDtypeStruct((2 * size, columns), dtype) for columns, dtype in outs]
    part = jax.ShapeDtypeStruct((size, 2 * resident[-1].shape[1]), jnp.bfloat16)
    small_shapes = [jax.ShapeDtypeStruct((2, *shape), jnp.float32) for shape in small_outs]
    return pl.pallas_call(
        kernel,
        grid=(2,),
        in_specs=[by_rows(one) for one in tiled] + [by_first(one) for one in small] + [whole(one) for one in resident],
        out_specs=[by_rows(one) for one in shapes] + [by_first(one) for one in small_shapes] + [whole(part)] * 2,
        out_shape=shapes + small_shapes + [part] * 2,
        compiler_params=pltpu.CompilerParams(vmem_limit_bytes=32 * 2**20),
        cost_estimate=COST,
    )(*tiled, *small, *resident)


def weight_kernel(left_near, left_far, right_near, right_far, own, sent):
    total = dot_tn(left_near[...], right_near[...]) + dot_tn(left_far[...], right_far[...])
    half = own.shape[1]
    own[...] = total[:, :half]
    sent[...] = narrow(total[:, half:])


def weight_grads(lefts, rights, tile):
    tokens, columns = lefts[0].shape
    half = rights[0].shape[1] // 2
    left_spec = pl.BlockSpec((tokens, tile), lambda i: (0, i))
    out_spec = pl.BlockSpec((tile, half), lambda i: (i, 0))
    return pl.pallas_call(
        weight_kernel,
        grid=(columns // tile,),
        in_specs=[left_spec, left_spec, whole(rights[0]), whole(rights[1])],
        out_specs=[out_spec, out_spec],
        out_shape=[
            jax.ShapeDtypeStruct((columns, half), jnp.float32),
            jax.ShapeDtypeStruct((columns, half), jnp.bfloat16),
        ],
        compiler_params=pltpu.CompilerParams(vmem_limit_bytes=28 * 2**20),
        cost_estimate=COST,
    )(*lefts, *rights)


def body(
    tokens,
    segment_ids,
    cotangent,
    norm1_gain,
    in_weight,
    conv_weight,
    out_weight,
    norm2_gain,
    gate_weight,
    up_weight,
    down_weight,
):
    place = lax.axis_index("dp") % TEAM
    row = lax.axis_index("row")
    col = lax.axis_index("col")
    cols = lax.axis_size("col")
    sequence = tokens.shape[0]
    size = sequence // 2
    half = tokens.shape[1]

    tokens_other = lax.dynamic_slice_in_dim(tokens, (1 - row) * size, size, 0)
    tokens_own = lax.dynamic_slice_in_dim(tokens, row * size, size, 0)
    tokens_row = over_row(tokens_other)
    tokens_x0 = over_x(tokens_own)
    channels = in_weight.shape[2] // TEAM
    hidden = gate_weight.shape[1] // TEAM
    in_part = lax.dynamic_slice_in_dim(in_weight, place * channels, channels, 2)
    in_part = in_part.transpose(1, 2, 0).reshape(3 * channels, half)
    out_part = lax.dynamic_slice_in_dim(out_weight, place * channels, channels, 0)
    taps_part = lax.dynamic_slice_in_dim(conv_weight, place * channels, channels, 1)
    taps_part = jnp.pad(taps_part, ((0, 0), (0, half - channels)))
    gains_part = jnp.pad(jnp.stack([norm1_gain, norm2_gain]), ((0, 11), (0, 0)))
    in_pair = col_first(jnp.concatenate([in_part, taps_part, gains_part, out_part], axis=0))
    grads_other = lax.dynamic_slice_in_dim(cotangent, (1 - row) * size, size, 0)
    grads_own = lax.dynamic_slice_in_dim(cotangent, row * size, size, 0)
    gate_part = lax.dynamic_slice_in_dim(gate_weight, place * hidden, hidden, 1).T
    ids_row = over_row(segment_ids)
    in_pair, tokens_row, tokens_x0, ids_row, grads_other, gate_part = meet(
        in_pair, tokens_row, tokens_x0, ids_row, grads_other, gate_part
    )

    in_other = col_swap(in_pair, 1)
    tokens_x1 = over_x(tokens_row)
    grads_row = over_row(grads_other)
    gate_pair = col_first(gate_part)
    up_part = lax.dynamic_slice_in_dim(up_weight, place * hidden, hidden, 1).T
    down_part = lax.dynamic_slice_in_dim(down_weight, place * hidden, hidden, 0)
    ids = jnp.stack([segment_ids, ids_row])
    ids = lax.dynamic_index_in_dim(ids, (col // 2) ^ row, 0, keepdims=False)
    ids = lax.dynamic_slice_in_dim(ids, (col % 2) * sequence, sequence, 0)
    ids_far = over_x(ids)
    in_other, tokens_x1, grads_row, ids_far, gate_pair, grads_own, ids, up_part, down_part = meet(
        in_other, tokens_x1, grads_row, ids_far, gate_pair, grads_own, ids, up_part, down_part
    )
    in_rows = 3 * channels
    in_near = stacked(in_pair[:, :in_rows], in_other[:, :in_rows], 3)
    in_near = jnp.concatenate([in_near, in_pair[0, in_rows : in_rows + 16]], axis=0)
    out_near = stacked(in_pair[:, in_rows + 16 :], in_other[:, in_rows + 16 :], 1)
    grads_near = jnp.concatenate([grads_own, grads_row], axis=1)
    in_near, out_near, grads_near, up_part, tokens_x1, gate_pair, ids = meet(
        in_near, out_near, grads_near, up_part, tokens_x1, gate_pair, ids
    )

    near = jnp.concatenate([tokens_own, tokens_row], axis=1)
    far = jnp.concatenate([tokens_x0, tokens_x1], axis=1)
    pair, ids_pair = over_core(jnp.stack([near, far])), over_core(jnp.stack([ids, ids_far]))
    pair, ids_pair, in_near, out_near, in_other, grads_near, gate_pair, up_part = meet(
        pair, ids_pair, in_near, out_near, in_other, grads_near, gate_pair, up_part
    )
    in_row = over_row(in_near)
    out_row = over_row(out_near)
    gate_other = col_swap(gate_pair, 1)
    up_pair = col_first(up_part)
    grads_far = over_x(grads_near)
    ids = jnp.stack([ids, ids_pair[0], ids_far, ids_pair[1]])
    keeps = []
    for offset in (1, 2):
        equal = (ids[:, offset:] == ids[:, :-offset]).astype(jnp.float32)
        keeps.append(jnp.pad(equal, ((0, 0), (offset, offset))))
    flags = jnp.stack(
        [
            lax.dynamic_slice_in_dim(keeps[which], row * size + offset, size, 1)
            for which, offset in ((0, 0), (1, 0), (0, 1), (1, 2))
        ],
        axis=2,
    )
    flags = [flags[:2].reshape(2 * size, 4), flags[2:].reshape(2 * size, 4)]
    near_tokens, far_tokens = (near, pair[0]), (far, pair[1])
    inputs = [jnp.concatenate(both, axis=0) for both in (near_tokens, far_tokens)]
    taps = jnp.concatenate(
        [both[which, in_rows : in_rows + 3, :channels] for both in (in_pair, in_other) for which in (0, 1)], axis=1
    )
    taps = wide(taps)
    in_row, out_row, gate_other, up_pair, inputs, taps, flags, down_part = meet(
        in_row, out_row, gate_other, up_pair, inputs, taps, flags, down_part
    )

    width = cols * channels
    gains = jnp.stack([norm1_gain, norm2_gain])
    gains = wide(jnp.concatenate([gains, in_row[4 * in_rows + 3 : 4 * in_rows + 5]], axis=1))
    gain_one, gain_two = gains[0], gains[1]
    in_near, in_row = in_near[: 4 * in_rows], in_row[: 4 * in_rows]
    ends = wide(jnp.concatenate([one[at + size - 8 : at + size] for one in inputs for at in (0, size)], axis=0))
    ends = narrow(ends * norm_scale(ends) * gain_one)
    ends = dot_nt(ends[:, :half], in_near) + dot_nt(ends[:, half:], in_row)
    ends = (ends[:, :width] * ends[:, 2 * width :]).reshape(2, 2, 8, width)[:, :, 6:]
    gate_near = stacked(gate_pair, gate_other, 1)
    before, gate_near, up_pair, down_part, inputs, grads_own_x = hop(
        over_row, ends, gate_near, up_pair, down_part, inputs, grads_near
    )
    gate_row = over_row(gate_near)
    up_other = col_swap(up_pair, 1)
    down_pair = col_first(down_part)
    grads_pair = over_core(jnp.stack([grads_own_x, grads_far]))
    normed_one, projected = zip(
        *[
            token_call(
                project_kernel,
                [one],
                (gain_one[None], in_near, in_row),
                ((2 * half, jnp.bfloat16), (3 * width, jnp.float32)),
            )
            for one in inputs
        ]
    )

    def mix(which):
        return sequence_call(
            mix_kernel,
            [projected[which], flags[which]],
            [before[which]],
            (taps, out_near, out_row),
            ((width, jnp.bfloat16),),
        )

    mixed = [None, None]
    mixed[1], far_own, far_sent = mix(1)
    mixed[0], near_own, near_sent = mix(0)
    up_other, down_pair, gate_row, grads_pair, far_own, far_sent, near_own, near_sent = meet(
        up_other, down_pair, gate_row, grads_pair, far_own, far_sent, near_own, near_sent
    )
    up_near = stacked(up_pair, up_other, 1)
    near_grads, far_grads = (grads_near, grads_pair[0]), (grads_far, grads_pair[1])
    cotangents = [jnp.concatenate(both, axis=0) for both in (near_grads, far_grads)]
    far_moved, near_moved, far_own, near_own, up_near, down_pair, cotangents = meet(
        over_core(far_sent), over_core(near_sent), far_own, near_own, up_near, down_pair, cotangents
    )
    far_send = narrow(wide(far_own) + wide(far_moved))
    near_send = narrow(wide(near_own) + wide(near_moved))
    from_far, to_far = over_x(far_send), over_x(near_send)
    up_row = over_row(up_near)
    down_other = col_swap(down_pair, 1)
    from_far, down_other, up_row = meet(from_far, down_other, up_row)
    down_near = stacked(down_pair, down_other, 1)
    from_far, down_near = meet(from_far, down_near)
    down_row = over_row(down_near)
    hidden_near = wide(near_tokens[0]) + (wide(near_own) + wide(near_moved) + wide(from_far))
    scale_near = norm_scale(hidden_near)
    normed_own = narrow(hidden_near * scale_near * gain_two)
    to_far, normed_own = meet(to_far, normed_own)
    hidden_far = wide(far_tokens[0]) + (wide(far_own) + wide(far_moved) + wide(to_far))
    scale_far = norm_scale(hidden_far)
    normed_x = narrow(hidden_far * scale_far * gain_two)
    down_row, normed_own, normed_x = meet(down_row, normed_own, normed_x)
    (pair,) = hop(over_core, jnp.stack([normed_own, normed_x]))
    normed_near = jnp.concatenate([normed_own, pair[0]], axis=0)
    normed_far = jnp.concatenate([normed_x, pair[1]], axis=0)
    hiddens, scale_two, normed_two = (hidden_near, hidden_far), (scale_near, scale_far), (normed_near, normed_far)
    units = gate_near.shape[0]
    weights = (gate_near, gate_row, up_near, up_row, down_near, down_row)

    def exchange(partial):
        return partial[:, :half], narrow(partial[:, half:])

    act, grad_gate, grad_up = [None, None], [None, None], [None, None]
    act[0], grad_gate[0], grad_up[0], near_own, near_sent, near_out_own, near_out_sent = gated_call(
        normed_near, cotangents[0], weights
    )
    near_moved, near_own, normed_far = hop(over_core, near_sent, near_own, normed_far)
    near_send, normed_far = meet(narrow(wide(near_own) + wide(near_moved)), normed_far)
    back_to_far = over_x(near_send)
    act[1], grad_gate[1], grad_up[1], far_own, far_sent, far_out_own, far_out_sent = gated_call(
        normed_far, cotangents[1], weights
    )
    normed_two = [normed_near, normed_far]
    back_to_far, far_own, far_sent, grad_gate, grad_up, act = meet(
        back_to_far, far_own, far_sent, grad_gate, grad_up, act
    )
    far_moved, far_own, grad_gate, grad_up, act = hop(over_core, far_sent, far_own, grad_gate, grad_up, act)
    far_send, grad_gate, grad_up, act = meet(narrow(wide(far_own) + wide(far_moved)), grad_gate, grad_up, act)
    back_from_far = over_x(far_send)
    gate_own, gate_sent = weight_grads(grad_gate, normed_two, units // 3)
    gate_moved = over_row(gate_sent)
    gate_sent, grad_up, act = meet(gate_sent, grad_up, act)
    down_own, down_sent = weight_grads(act, cotangents, units // 3)
    down_sent, down_kept = col_send(jnp.concatenate([down_own, wide(down_sent)], axis=1), 1)
    down_moved = col_swap(down_sent, 1)
    down_sent, grad_up, act = meet(down_sent, grad_up, act)
    up_own, up_sent = weight_grads(grad_up, normed_two, units // 3)
    back_from_far, up_sent = meet(back_from_far, up_sent)

    back_sums = (
        wide(near_own) + wide(near_moved) + wide(back_from_far),
        wide(far_own) + wide(far_moved) + wide(back_to_far),
    )
    grad_hidden, low = [], []
    for which, cotangent_rows in ((0, near_grads[0]), (1, far_grads[0])):
        grads = wide(cotangent_rows) + norm_backward(
            back_sums[which], hiddens[which], scale_two[which], gain_two
        )
        grad_hidden.append(grads)
        low.append(narrow(grads))
    gain_two_grad = jnp.sum(back_sums[0] * hidden_near * scale_two[0], axis=0)
    gate_moved, down_moved, low = meet(gate_moved, down_moved, low)
    gate_sent, gate_kept = col_send(gate_own + wide(gate_moved), 1)
    down_sent, down_kept = col_add(down_kept, down_moved)
    low_moved = over_core(jnp.stack(low))
    near_out_moved, far_out_moved = over_core(near_out_sent), over_core(far_out_sent)
    low_moved, near_out_moved, far_out_moved, low, up_sent, gate_sent, down_sent = meet(
        low_moved, near_out_moved, far_out_moved, low, up_sent, gate_sent, down_sent
    )
    grad_mixed = [jnp.concatenate([low[which], low_moved[which]], axis=0) for which in (0, 1)]
    far_out = narrow(wide(far_out_own) + wide(far_out_moved))

    starts = jnp.concatenate([one[at : at + 8] for one in grad_mixed for at in (0, size)], axis=0)
    starts = dot_nt(starts[:, :half], out_near) + dot_nt(starts[:, half:], out_row)
    opened = jnp.concatenate([one[at : at + 8, width : 2 * width] for one in projected for at in (0, size)], axis=0)
    starts = (starts * opened).reshape(2, 2, 8, width)[:, :, :2]
    behind, grad_mixed, up_sent, gate_sent, down_sent, far_out = hop(
        over_row, starts, grad_mixed, up_sent, gate_sent, down_sent, far_out
    )
    up_moved = over_row(up_sent)
    gate_moved = col_swap(gate_sent, 1)
    down_moved = col_swap(down_sent, 2)
    out_from_far = over_x(far_out)

    def mix_back(which):
        return sequence_call(
            mix_back_kernel,
            [grad_mixed[which], projected[which], flags[which]],
            [before[which], behind[which]],
            (taps, out_near, out_row, in_near, in_row),
            ((3 * width, jnp.bfloat16),),
            ((3, width),),
        )

    grad_projected = [None, None]
    grad_projected[1], far_taps, far_one, far_one_sent = mix_back(1)
    far_one, grad_mixed = meet(far_one, grad_mixed)
    grad_projected[0], near_taps, near_one, near_one_sent = mix_back(0)
    in_own, in_sent = weight_grads(grad_projected, normed_one, width)
    out_own, out_sent = weight_grads(mixed, grad_mixed, width)
    mixer_own = jnp.concatenate([in_own, out_own], axis=0)
    mixer_sent = jnp.concatenate([in_sent, out_sent], axis=0)
    out_from_far, up_moved, gate_moved, down_moved, far_one, near_one, near_one_sent, mixer_sent = meet(
        out_from_far, up_moved, gate_moved, down_moved, far_one, near_one, near_one_sent, mixer_sent
    )
    gate_sent, gate_kept = col_add(gate_kept, gate_moved)
    up_sent, up_kept = col_send(up_own + wide(up_moved), 1)
    down_own, down_sent = exchange(col_last(down_kept, down_moved))
    far_one_moved, near_one_moved, far_one, near_one, mixer_sent, up_sent, gate_sent, down_sent = meet(
        over_core(far_one_sent), over_core(near_one_sent), far_one, near_one, mixer_sent, up_sent, gate_sent, down_sent
    )
    one_send = narrow(wide(far_one) + wide(far_one_moved))
    one_send, mixer_sent, far_one, near_one = meet(one_send, mixer_sent, far_one, near_one)
    mixer_moved = over_row(mixer_sent)
    up_moved = col_swap(up_sent, 1)
    gate_moved = col_swap(gate_sent, 2)
    one_from_far = over_x(one_send)
    result = narrow(hidden_near + (wide(near_out_own) + wide(near_out_moved) + wide(out_from_far)))
    gain_one_grad = 0.0
    for rows, one in (
        (near_tokens[0], near_one), (near_tokens[1], near_one_sent), (far_tokens[0], far_one), (far_tokens[1], far_one_sent)
    ):
        rows = wide(rows)
        gain_one_grad = gain_one_grad + jnp.sum(wide(one) * (rows * norm_scale(rows)), axis=0)
    conv_local = jnp.sum(near_taps + far_taps, axis=0)
    gain_local = jnp.stack([gain_one_grad, gain_two_grad])
    conv_flat = conv_local.reshape(3, cols, channels).transpose(1, 0, 2).reshape(cols, 3 * channels)
    apart = jnp.arange(cols) ^ col
    conv_flat = jnp.take(conv_flat, apart // 2 + apart % 2 * 2, axis=0).reshape(-1)
    small = jnp.concatenate([gain_local[:, :half].reshape(-1), conv_flat, gain_local[:, half:].reshape(-1)])
    small, up_moved, gate_moved = meet(small, up_moved, gate_moved)
    for distance in (1, 2):
        small = small + col_swap(small, distance)
    one_from_far, mixer_moved, up_moved, gate_moved, near_one, result, down_sent, small = meet(
        one_from_far, mixer_moved, up_moved, gate_moved, near_one, result, down_sent, small
    )
    mixer_sent, mixer_kept = col_send(mixer_own + wide(mixer_moved), 4)
    up_sent, up_kept = col_add(up_kept, up_moved)
    gate_total = team_first(col_last(gate_kept, gate_moved))
    mixer_sent, up_sent, gate_total, one_from_far, near_one, down_sent = meet(
        mixer_sent, up_sent, gate_total, one_from_far, near_one, down_sent
    )
    mixer_moved = col_swap(mixer_sent, 1)
    up_moved = col_swap(up_sent, 2)
    gate_far = over_x(gate_total)
    kept = 2 * half + 3 * width
    sent = jnp.concatenate([small[kept:], small[2 * half : kept]])
    small = small[:kept] + over_row(sent)
    small, down_sent = meet(small, down_sent)
    down_from_row = over_row(down_sent)
    conv_own = lax.dynamic_slice_in_dim(small[2 * half :], col * 3 * channels, 3 * channels, 0)
    conv_wide = lax.dynamic_update_slice(
        jnp.zeros((TEAM * 3 * channels,), jnp.float32), conv_own, (place * 3 * channels,)
    )
    small = jnp.concatenate([small[: 2 * half], conv_wide])
    small = small + over_x(small)
    grad_normed_one = wide(near_one) + wide(near_one_moved) + wide(one_from_far)
    own_inputs = wide(near_tokens[0])
    own_scale = norm_scale(own_inputs)
    input_grad = grad_hidden[0] + norm_backward(grad_normed_one, own_inputs, own_scale, gain_one)
    mixer_moved, up_moved, gate_far, down_from_row, input_grad, small = meet(
        mixer_moved, up_moved, gate_far, down_from_row, input_grad, small
    )
    mixer_sent, mixer_kept = col_add(mixer_kept, mixer_moved)
    mixer_sent, up_moved, down_from_row, gate_far, input_grad, result, small = meet(
        mixer_sent, up_moved, down_from_row, gate_far, input_grad, result, small
    )
    mixer_moved = col_swap(mixer_sent, 2)
    up_total = team_first(col_last(up_kept, up_moved))
    down_total = team_first(down_own + wide(down_from_row))
    both = jnp.stack([up_total, down_total])
    both_far = over_x(both)
    input_row = over_row(narrow(input_grad[:, half:]))
    small = other_teams(small + over_core(small))
    conv_grad = small[2 * half :].reshape(TEAM, 3, channels).transpose(1, 0, 2).reshape(3, TEAM * channels)
    gate_pair = over_core(jnp.stack([gate_total, gate_far]))
    mixer_moved, both_far, gate_pair, result, input_row = meet(mixer_moved, both_far, gate_pair, result, input_row)
    mixer_total = team_first(col_last(mixer_kept, mixer_moved))
    mixer_total, both_far, gate_pair, result = meet(mixer_total, both_far, gate_pair, result)
    mixer_far = over_x(mixer_total)
    result_row = over_row(result[:, half:])
    both_pair = over_core(jnp.stack([both, both_far]))
    gate_grad = wide(team_rows(gate_total, gate_far, gate_pair, 1)[0].T)
    mixer_far, both_pair = meet(mixer_far, both_pair)
    up_grad = wide(team_rows(up_total, both_far[0], both_pair[:, 0], 1)[0].T)
    down_grad = wide(team_rows(down_total, both_far[1], both_pair[:, 1], 1)[0])
    mixer_pair = over_core(jnp.stack([mixer_total, mixer_far]))
    mixer_grads = team_rows(mixer_total, mixer_far, mixer_pair, 4)
    in_grad = wide(mixer_grads[:3].transpose(2, 0, 1))
    out_grad = wide(mixer_grads[3])

    return (
        to_blocks(result[:, :half], result_row),
        to_blocks(input_grad[:, :half], input_row),
        small[:half],
        in_grad,
        conv_grad,
        out_grad,
        small[half : 2 * half],
        gate_grad,
        up_grad,
        down_grad,
    )


def solution(mesh):
    return jax.shard_map(
        body,
        mesh=mesh,
        in_specs=(
            P(("dp", "col"), "row"),
            P(("dp", "row")),
            P(("dp", "col"), "row"),
            P("row"),
            P("row", None, "col"),
            P(None, "col"),
            P("col", "row"),
            P("row"),
            P("row", "col"),
            P("row", "col"),
            P("col", "row"),
        ),
        out_specs=(
            P(("dp", "col"), "row"),
            P(("dp", "col"), "row"),
            P("row"),
            P("row", None, "col"),
            P(None, "col"),
            P("col", "row"),
            P("row"),
            P("row", "col"),
            P("row", "col"),
            P("col", "row"),
        ),
        check_vma=False,
    )
```

```python
import functools

import jax
import jax.numpy as jnp
from jax import lax
from jax.experimental import pallas as pl
from jax.experimental.pallas import tpu as pltpu
from jax.sharding import PartitionSpec as P

EPSILON = 1e-05
TEAM = 4


def dot_nt(left, right):
    return lax.dot_general(left, right, (((1,), (1,)), ((), ())), preferred_element_type=jnp.float32)


def dot_nn(left, right):
    return lax.dot_general(left, right, (((1,), (0,)), ((), ())), preferred_element_type=jnp.float32)


def dot_tn(left, right):
    return lax.dot_general(left, right, (((0,), (0,)), ((), ())), preferred_element_type=jnp.float32)


def over_dp(values, distance):
    size = lax.axis_size("dp")
    return lax.ppermute(values, "dp", [(i, i ^ distance) for i in range(size)])


def over_core(values):
    return over_dp(values, 1)


def over_x(values):
    return over_dp(values, 2)


def over_row(values):
    return lax.ppermute(values, "row", [(0, 1), (1, 0)])


def col_swap(values, distance):
    size = lax.axis_size("col")
    return lax.ppermute(values, "col", [(i, i ^ distance) for i in range(size)])


def narrow(values):
    return values.astype(jnp.bfloat16)


def wide(values):
    return values.astype(jnp.float32)


def halves(values):
    size = values.shape[0] // 2
    return values[:size], values[size:]


def other_teams(values):
    distance = TEAM
    while distance < lax.axis_size("dp"):
        values = values + over_dp(values, distance)
        distance *= 2
    return values


def after(value, *events):
    return lax.optimization_barrier((value, *events))[0]


def meet(*values):
    return lax.optimization_barrier(values)


def hop(move, value, *waiting):
    return meet(move(value), *waiting)


def stacked(pair, other, parts):
    pieces = jnp.concatenate([pair, other], axis=0)
    if parts > 1:
        pieces = pieces.reshape(4, parts, -1, pair.shape[2]).transpose(1, 0, 2, 3)
    return pieces.reshape(-1, pair.shape[2])


def col_first(piece):
    return jnp.stack([piece, col_swap(piece, 2)])


def col_send(values, parts):
    rows = values.shape[0] // (parts * 4)
    grid = values.reshape(parts, 2, 2 * rows, values.shape[1])
    return narrow(grid[:, 1]), grid[:, 0]


def col_add(kept, received):
    total = kept + wide(received)
    rows = total.shape[1] // 2
    return narrow(total[:, rows:]), total[:, :rows]


def col_last(kept, received):
    return (kept + wide(received)).reshape(-1, kept.shape[2])


def team_first(piece):
    return narrow(other_teams(piece))


def team_rows(own, far, pair, parts):
    rows, half = own.shape[0] // parts, own.shape[1]
    place = lax.axis_index("dp") % TEAM
    result = jnp.zeros((parts, TEAM * rows, half), jnp.bfloat16)
    for distance, block in enumerate((own, pair[0], far, pair[1])):
        block = block.reshape(parts, rows, half)
        result = lax.dynamic_update_slice(result, block, (0, (place ^ distance) * rows, 0))
    return result


def norm_scale(hidden):
    return lax.rsqrt(jnp.mean(hidden * hidden, axis=1, keepdims=True) + EPSILON)


def norm_backward(grad_normed, hidden, row_scale, gain_vector):
    inner_sum = jnp.sum(grad_normed * gain_vector * hidden, axis=1, keepdims=True)
    cubed = row_scale * row_scale * row_scale
    return grad_normed * gain_vector * row_scale - hidden * (cubed / hidden.shape[1]) * inner_sum


def to_blocks(values, received):
    size, half = values.shape
    row = lax.axis_index("row")
    result = jnp.zeros((2 * size, half), values.dtype)
    result = lax.dynamic_update_slice(result, values, (row * size, 0))
    return lax.dynamic_update_slice(result, received.astype(values.dtype), ((1 - row) * size, 0))


ROWS = 256
COST = pl.CostEstimate(flops=1, bytes_accessed=1, transcendentals=0)


def whole(array):
    return pl.BlockSpec(array.shape, lambda i: (0,) * array.ndim)


def row_tiles(array):
    return pl.BlockSpec((ROWS, array.shape[1]), lambda i: (i, 0))


def token_call(kernel, tiled, resident, outs):
    tokens = tiled[0].shape[0]
    shapes = [jax.ShapeDtypeStruct((tokens, columns), dtype) for columns, dtype in outs]
    return pl.pallas_call(
        kernel,
        grid=(tokens // ROWS,),
        in_specs=[row_tiles(one) for one in tiled] + [whole(one) for one in resident],
        out_specs=[row_tiles(one) for one in shapes],
        out_shape=shapes,
        compiler_params=pltpu.CompilerParams(vmem_limit_bytes=20 * 2**20),
        cost_estimate=COST,
    )(*tiled, *resident)


def split_nt(left, near, row):
    half = near.shape[1]
    return dot_nt(left[:, :half], near[...]) + dot_nt(left[:, half:], row[...])


def gated_kernel(
    normed, cotangent, gate_near, gate_row, up_near, up_row, down_near, down_row,
    act, grad_gate, grad_up, back_own, back_sent, out_own, out_sent,
):
    gate_value = split_nt(normed, gate_near, gate_row)
    up_value = split_nt(normed, up_near, up_row)
    grad_act = split_nt(cotangent, down_near, down_row)
    sigmoid_gate = jax.nn.sigmoid(gate_value)
    silu = gate_value * sigmoid_gate
    low_act = narrow(silu * up_value)
    low_gate = narrow(grad_act * up_value * (sigmoid_gate * (1.0 + gate_value * (1.0 - sigmoid_gate))))
    low_up = narrow(grad_act * silu)
    act[...] = low_act
    grad_gate[...] = low_gate
    grad_up[...] = low_up
    back = jnp.concatenate(
        [
            narrow(dot_nn(low_gate, gate_near[...]) + dot_nn(low_up, up_near[...])),
            narrow(dot_nn(low_gate, gate_row[...]) + dot_nn(low_up, up_row[...])),
        ],
        axis=1,
    )
    out = jnp.concatenate(
        [narrow(dot_nn(low_act, down_near[...])), narrow(dot_nn(low_act, down_row[...]))], axis=1
    )
    own_or_sent(back, back_own, back_sent)
    own_or_sent(out, out_own, out_sent)


def gated_call(normed, cotangent, weights):
    tokens, width = normed.shape
    units = weights[0].shape[0]
    steps = tokens // ROWS
    wide_out = jax.ShapeDtypeStruct((tokens, units), jnp.bfloat16)
    part_out = jax.ShapeDtypeStruct((tokens // 2, width), jnp.bfloat16)
    own = pl.BlockSpec((ROWS, width), lambda i: (jnp.minimum(i, steps // 2 - 1), 0))
    sent = pl.BlockSpec((ROWS, width), lambda i: (jnp.maximum(i - steps // 2, 0), 0))
    return pl.pallas_call(
        gated_kernel,
        grid=(steps,),
        in_specs=[row_tiles(normed), row_tiles(cotangent)] + [whole(one) for one in weights],
        out_specs=[row_tiles(wide_out)] * 3 + [own, sent] * 2,
        out_shape=[wide_out] * 3 + [part_out] * 4,
        compiler_params=pltpu.CompilerParams(vmem_limit_bytes=36 * 2**20),
        cost_estimate=COST,
    )(normed, cotangent, *weights)


def project_kernel(inputs, gain, in_near, in_row, normed, projected):
    values = wide(inputs[...])
    scale = lax.rsqrt(jnp.mean(values * values, axis=1, keepdims=True) + EPSILON)
    low = narrow(values * scale * gain[...])
    normed[...] = low
    projected[...] = split_nt(low, in_near, in_row)


def mixer_values(projected, flags, before, taps):
    width = taps.shape[1]
    input_gate, output_gate, values_part = (projected[:, part * width : (part + 1) * width] for part in range(3))
    mix_input = input_gate * values_part
    place = lax.broadcasted_iota(jnp.int32, mix_input.shape, 0)
    one, two = before[0, 1:2], before[0, 0:1]
    prior_one = flags[:, 0:1] * jnp.where(place == 0, one, pltpu.roll(mix_input, 1, 0))
    prior_two = jnp.where(place == 0, two, jnp.where(place == 1, one, pltpu.roll(mix_input, 2, 0)))
    prior_two = flags[:, 1:2] * prior_two
    convolved = taps[2:3] * mix_input + taps[1:2] * prior_one + taps[0:1] * prior_two
    return input_gate, output_gate, values_part, mix_input, prior_one, prior_two, convolved


def own_or_sent(partial, own, sent):
    first = pl.program_id(0) < pl.num_programs(0) // 2

    @pl.when(first)
    def _():
        own[...] = partial

    @pl.when(jnp.logical_not(first))
    def _():
        sent[...] = partial


def mix_kernel(projected, flags, before, taps, out_near, out_row, mixed, own, sent):
    _, output_gate, _, _, _, _, convolved = mixer_values(projected, flags, before, taps)
    low = narrow(output_gate * convolved)
    mixed[...] = low
    partial = narrow(jnp.concatenate([dot_nn(low, out_near[...]), dot_nn(low, out_row[...])], axis=1))
    own_or_sent(partial, own, sent)


def mix_back_kernel(
    grad_mixed, projected, flags, before, behind, taps, out_near, out_row, in_near, in_row,
    grad_projected, sums, own, sent,
):
    width = taps.shape[1]
    input_gate, output_gate, values_part, mix_input, prior_one, prior_two, convolved = mixer_values(
        projected, flags, before, taps
    )
    grad_y = split_nt(grad_mixed, out_near, out_row)
    grad_conv = grad_y * output_gate
    for tap, values in enumerate((prior_two, prior_one, mix_input)):
        sums[0, tap : tap + 1] = jnp.sum(grad_conv * values, axis=0, keepdims=True)
    size = grad_conv.shape[0]
    place = lax.broadcasted_iota(jnp.int32, grad_conv.shape, 0)
    one, two = behind[0, 0:1], behind[0, 1:2]
    next_one = jnp.where(place == size - 1, one, pltpu.roll(grad_conv, size - 1, 0))
    next_two = jnp.where(place == size - 2, one, pltpu.roll(grad_conv, size - 2, 0))
    next_two = jnp.where(place == size - 1, two, next_two)
    grad_mix = (
        taps[2:3] * grad_conv
        + taps[1:2] * (flags[:, 2:3] * next_one)
        + taps[0:1] * (flags[:, 3:4] * next_two)
    )
    low = narrow(jnp.concatenate([grad_mix * values_part, grad_y * convolved, grad_mix * input_gate], axis=1))
    grad_projected[...] = low
    partial = narrow(jnp.concatenate([dot_nn(low, in_near[...]), dot_nn(low, in_row[...])], axis=1))
    own_or_sent(partial, own, sent)


def sequence_call(kernel, tiled, small, resident, outs, small_outs=()):
    size = tiled[0].shape[0] // 2

    def by_rows(array):
        return pl.BlockSpec((size, array.shape[1]), lambda i: (i, 0))

    def by_first(array):
        return pl.BlockSpec((1, *array.shape[1:]), lambda i: (i, 0, 0))

    shapes = [jax.ShapeDtypeStruct((2 * size, columns), dtype) for columns, dtype in outs]
    part = jax.ShapeDtypeStruct((size, 2 * resident[-1].shape[1]), jnp.bfloat16)
    small_shapes = [jax.ShapeDtypeStruct((2, *shape), jnp.float32) for shape in small_outs]
    return pl.pallas_call(
        kernel,
        grid=(2,),
        in_specs=[by_rows(one) for one in tiled] + [by_first(one) for one in small] + [whole(one) for one in resident],
        out_specs=[by_rows(one) for one in shapes] + [by_first(one) for one in small_shapes] + [whole(part)] * 2,
        out_shape=shapes + small_shapes + [part] * 2,
        compiler_params=pltpu.CompilerParams(vmem_limit_bytes=32 * 2**20),
        cost_estimate=COST,
    )(*tiled, *small, *resident)


def weight_kernel(left_near, left_far, right_near, right_far, own, sent):
    total = dot_tn(left_near[...], right_near[...]) + dot_tn(left_far[...], right_far[...])
    half = own.shape[1]
    own[...] = total[:, :half]
    sent[...] = narrow(total[:, half:])


def weight_grads(lefts, rights, tile):
    tokens, columns = lefts[0].shape
    half = rights[0].shape[1] // 2
    left_spec = pl.BlockSpec((tokens, tile), lambda i: (0, i))
    out_spec = pl.BlockSpec((tile, half), lambda i: (i, 0))
    return pl.pallas_call(
        weight_kernel,
        grid=(columns // tile,),
        in_specs=[left_spec, left_spec, whole(rights[0]), whole(rights[1])],
        out_specs=[out_spec, out_spec],
        out_shape=[
            jax.ShapeDtypeStruct((columns, half), jnp.float32),
            jax.ShapeDtypeStruct((columns, half), jnp.bfloat16),
        ],
        compiler_params=pltpu.CompilerParams(vmem_limit_bytes=28 * 2**20),
        cost_estimate=COST,
    )(*lefts, *rights)


def assemble_kernel(turned, place, own, far, pair, out, rows):
    count = own.shape[0]
    for distance, block in enumerate((own[...], pair[0], far[...], pair[1])):
        start = pl.multiple_of((place[0] ^ distance) * count, 16)
        rows[pl.ds(start, count), :] = wide(block)
    out[...] = rows[...].T if turned else rows[...]


def assemble(own, far, pair, turned):
    count, half = own.shape
    shape = (half, TEAM * count) if turned else (TEAM * count, half)
    place = (lax.axis_index("dp") % TEAM).astype(jnp.int32).reshape(1)
    vmem = pl.BlockSpec(memory_space=pltpu.VMEM)
    return pl.pallas_call(
        functools.partial(assemble_kernel, turned),
        in_specs=[pl.BlockSpec(memory_space=pltpu.SMEM), vmem, vmem, vmem],
        out_specs=vmem,
        out_shape=jax.ShapeDtypeStruct(shape, jnp.float32),
        scratch_shapes=[pltpu.VMEM((TEAM * count, half), jnp.float32)],
        compiler_params=pltpu.CompilerParams(vmem_limit_bytes=16 * 2**20),
        cost_estimate=COST,
    )(place, own, far, pair)


def body(
    tokens,
    segment_ids,
    cotangent,
    norm1_gain,
    in_weight,
    conv_weight,
    out_weight,
    norm2_gain,
    gate_weight,
    up_weight,
    down_weight,
):
    place = lax.axis_index("dp") % TEAM
    row = lax.axis_index("row")
    col = lax.axis_index("col")
    cols = lax.axis_size("col")
    sequence = tokens.shape[0]
    size = sequence // 2
    half = tokens.shape[1]

    tokens_other = lax.dynamic_slice_in_dim(tokens, (1 - row) * size, size, 0)
    tokens_own = lax.dynamic_slice_in_dim(tokens, row * size, size, 0)
    tokens_row = over_row(tokens_other)
    tokens_x0 = over_x(tokens_own)
    channels = in_weight.shape[2] // TEAM
    hidden = gate_weight.shape[1] // TEAM
    in_part = lax.dynamic_slice_in_dim(in_weight, place * channels, channels, 2)
    in_part = in_part.transpose(1, 2, 0).reshape(3 * channels, half)
    out_part = lax.dynamic_slice_in_dim(out_weight, place * channels, channels, 0)
    taps_part = lax.dynamic_slice_in_dim(conv_weight, place * channels, channels, 1)
    taps_part = jnp.pad(taps_part, ((0, 0), (0, half - channels)))
    gains_part = jnp.pad(jnp.stack([norm1_gain, norm2_gain]), ((0, 11), (0, 0)))
    in_pair = col_first(jnp.concatenate([in_part, taps_part, gains_part, out_part], axis=0))
    grads_other = lax.dynamic_slice_in_dim(cotangent, (1 - row) * size, size, 0)
    grads_own = lax.dynamic_slice_in_dim(cotangent, row * size, size, 0)
    gate_part = lax.dynamic_slice_in_dim(gate_weight, place * hidden, hidden, 1).T
    ids_row = over_row(segment_ids)
    in_pair, tokens_row, tokens_x0, ids_row, grads_other, gate_part = meet(
        in_pair, tokens_row, tokens_x0, ids_row, grads_other, gate_part
    )

    in_other = col_swap(in_pair, 1)
    tokens_x1 = over_x(tokens_row)
    grads_row = over_row(grads_other)
    gate_pair = col_first(gate_part)
    up_part = lax.dynamic_slice_in_dim(up_weight, place * hidden, hidden, 1).T
    down_part = lax.dynamic_slice_in_dim(down_weight, place * hidden, hidden, 0)
    ids = jnp.stack([segment_ids, ids_row])
    ids = lax.dynamic_index_in_dim(ids, (col // 2) ^ row, 0, keepdims=False)
    ids = lax.dynamic_slice_in_dim(ids, (col % 2) * sequence, sequence, 0)
    ids_far = over_x(ids)
    in_other, tokens_x1, grads_row, ids_far, gate_pair, grads_own, ids, up_part, down_part = meet(
        in_other, tokens_x1, grads_row, ids_far, gate_pair, grads_own, ids, up_part, down_part
    )
    in_rows = 3 * channels
    in_near = stacked(in_pair[:, :in_rows], in_other[:, :in_rows], 3)
    in_near = jnp.concatenate([in_near, in_pair[0, in_rows : in_rows + 16]], axis=0)
    out_near = stacked(in_pair[:, in_rows + 16 :], in_other[:, in_rows + 16 :], 1)
    grads_near = jnp.concatenate([grads_own, grads_row], axis=1)
    in_near, out_near, grads_near, up_part, tokens_x1, gate_pair, ids = meet(
        in_near, out_near, grads_near, up_part, tokens_x1, gate_pair, ids
    )

    near = jnp.concatenate([tokens_own, tokens_row], axis=1)
    far = jnp.concatenate([tokens_x0, tokens_x1], axis=1)
    pair, ids_pair = over_core(jnp.stack([near, far])), over_core(jnp.stack([ids, ids_far]))
    pair, ids_pair, in_near, out_near, in_other, grads_near, gate_pair, up_part = meet(
        pair, ids_pair, in_near, out_near, in_other, grads_near, gate_pair, up_part
    )
    in_row = over_row(in_near)
    out_row = over_row(out_near)
    gate_other = col_swap(gate_pair, 1)
    up_pair = col_first(up_part)
    grads_far = over_x(grads_near)
    ids = jnp.stack([ids, ids_pair[0], ids_far, ids_pair[1]])
    keeps = []
    for offset in (1, 2):
        equal = (ids[:, offset:] == ids[:, :-offset]).astype(jnp.float32)
        keeps.append(jnp.pad(equal, ((0, 0), (offset, offset))))
    flags = jnp.stack(
        [
            lax.dynamic_slice_in_dim(keeps[which], row * size + offset, size, 1)
            for which, offset in ((0, 0), (1, 0), (0, 1), (1, 2))
        ],
        axis=2,
    )
    flags = [flags[:2].reshape(2 * size, 4), flags[2:].reshape(2 * size, 4)]
    near_tokens, far_tokens = (near, pair[0]), (far, pair[1])
    inputs = [jnp.concatenate(both, axis=0) for both in (near_tokens, far_tokens)]
    taps = jnp.concatenate(
        [both[which, in_rows : in_rows + 3, :channels] for both in (in_pair, in_other) for which in (0, 1)], axis=1
    )
    taps = wide(taps)
    in_row, out_row, gate_other, up_pair, inputs, taps, flags, down_part = meet(
        in_row, out_row, gate_other, up_pair, inputs, taps, flags, down_part
    )

    width = cols * channels
    gains = jnp.stack([norm1_gain, norm2_gain])
    gains = wide(jnp.concatenate([gains, in_row[4 * in_rows + 3 : 4 * in_rows + 5]], axis=1))
    gain_one, gain_two = gains[0], gains[1]
    in_near, in_row = in_near[: 4 * in_rows], in_row[: 4 * in_rows]
    gate_near = stacked(gate_pair, gate_other, 1)
    gate_near, up_pair, down_part, inputs = meet(gate_near, up_pair, down_part, inputs)
    gate_row = over_row(gate_near)
    up_other = col_swap(up_pair, 1)
    down_pair = col_first(down_part)
    grads_pair = over_core(jnp.stack([grads_near, grads_far]))
    ends = wide(jnp.concatenate([one[at + size - 8 : at + size] for one in inputs for at in (0, size)], axis=0))
    ends = narrow(ends * norm_scale(ends) * gain_one)
    ends = dot_nt(ends[:, :half], in_near) + dot_nt(ends[:, half:], in_row)
    ends = (ends[:, :width] * ends[:, 2 * width :]).reshape(2, 2, 8, width)[:, :, 6:]
    before = over_row(ends)
    normed_one, projected = zip(
        *[
            token_call(
                project_kernel,
                [one],
                (gain_one[None], in_near, in_row),
                ((2 * half, jnp.bfloat16), (3 * width, jnp.float32)),
            )
            for one in inputs
        ]
    )

    def mix(which):
        return sequence_call(
            mix_kernel,
            [projected[which], flags[which]],
            [before[which]],
            (taps, out_near, out_row),
            ((width, jnp.bfloat16),),
        )

    mixed = [None, None]
    mixed[1], far_own, far_sent = mix(1)
    mixed[0], near_own, near_sent = mix(0)
    up_other, down_pair, gate_row, grads_pair, far_own, far_sent, near_own, near_sent = meet(
        up_other, down_pair, gate_row, grads_pair, far_own, far_sent, near_own, near_sent
    )
    up_near = stacked(up_pair, up_other, 1)
    near_grads, far_grads = (grads_near, grads_pair[0]), (grads_far, grads_pair[1])
    cotangents = [jnp.concatenate(both, axis=0) for both in (near_grads, far_grads)]
    far_moved, near_moved, far_own, near_own, up_near, down_pair, cotangents = meet(
        over_core(far_sent), over_core(near_sent), far_own, near_own, up_near, down_pair, cotangents
    )
    far_send = narrow(wide(far_own) + wide(far_moved))
    near_send = narrow(wide(near_own) + wide(near_moved))
    from_far, to_far = over_x(far_send), over_x(near_send)
    up_row = over_row(up_near)
    down_other = col_swap(down_pair, 1)
    from_far, down_other, up_row = meet(from_far, down_other, up_row)
    down_near = stacked(down_pair, down_other, 1)
    from_far, down_near = meet(from_far, down_near)
    down_row = over_row(down_near)
    hidden_near = wide(near_tokens[0]) + (wide(near_own) + wide(near_moved) + wide(from_far))
    scale_near = norm_scale(hidden_near)
    normed_own = narrow(hidden_near * scale_near * gain_two)
    to_far, normed_own = meet(to_far, normed_own)
    hidden_far = wide(far_tokens[0]) + (wide(far_own) + wide(far_moved) + wide(to_far))
    scale_far = norm_scale(hidden_far)
    normed_x = narrow(hidden_far * scale_far * gain_two)
    down_row, normed_own, normed_x = meet(down_row, normed_own, normed_x)
    (pair,) = hop(over_core, jnp.stack([normed_own, normed_x]))
    normed_near = jnp.concatenate([normed_own, pair[0]], axis=0)
    normed_far = jnp.concatenate([normed_x, pair[1]], axis=0)
    hiddens, scale_two, normed_two = (hidden_near, hidden_far), (scale_near, scale_far), (normed_near, normed_far)
    units = gate_near.shape[0]
    weights = (gate_near, gate_row, up_near, up_row, down_near, down_row)

    def exchange(partial):
        return partial[:, :half], narrow(partial[:, half:])

    act, grad_gate, grad_up = [None, None], [None, None], [None, None]
    act[0], grad_gate[0], grad_up[0], near_own, near_sent, near_out_own, near_out_sent = gated_call(
        normed_near, cotangents[0], weights
    )
    near_moved, near_own, normed_far = hop(over_core, near_sent, near_own, normed_far)
    near_send, normed_far = meet(narrow(wide(near_own) + wide(near_moved)), normed_far)
    back_to_far = over_x(near_send)
    act[1], grad_gate[1], grad_up[1], far_own, far_sent, far_out_own, far_out_sent = gated_call(
        normed_far, cotangents[1], weights
    )
    normed_two = [normed_near, normed_far]
    back_to_far, far_own, far_sent, grad_gate, grad_up, act = meet(
        back_to_far, far_own, far_sent, grad_gate, grad_up, act
    )
    far_moved, far_own, grad_gate, grad_up, act = hop(over_core, far_sent, far_own, grad_gate, grad_up, act)
    far_send, grad_gate, grad_up, act = meet(narrow(wide(far_own) + wide(far_moved)), grad_gate, grad_up, act)
    back_from_far = over_x(far_send)
    near_out_moved, far_out_moved = over_core(near_out_sent), over_core(far_out_sent)
    down_own, down_sent = weight_grads(act, cotangents, units // 3)
    down_sent, down_kept = col_send(jnp.concatenate([down_own, wide(down_sent)], axis=1), 1)
    down_moved = col_swap(down_sent, 1)
    down_sent, grad_gate, grad_up = meet(down_sent, grad_gate, grad_up)
    gate_own, gate_sent = weight_grads(grad_gate, normed_two, units // 3)
    gate_moved = over_row(gate_sent)
    gate_sent, grad_up = meet(gate_sent, grad_up)
    up_own, up_sent = weight_grads(grad_up, normed_two, units // 3)
    back_from_far, up_sent, near_out_moved, far_out_moved = meet(
        back_from_far, up_sent, near_out_moved, far_out_moved
    )

    back_sums = (
        wide(near_own) + wide(near_moved) + wide(back_from_far),
        wide(far_own) + wide(far_moved) + wide(back_to_far),
    )
    grad_hidden, low = [], []
    for which, cotangent_rows in ((0, near_grads[0]), (1, far_grads[0])):
        grads = wide(cotangent_rows) + norm_backward(
            back_sums[which], hiddens[which], scale_two[which], gain_two
        )
        grad_hidden.append(grads)
        low.append(narrow(grads))
    gain_two_grad = jnp.sum(back_sums[0] * hidden_near * scale_two[0], axis=0)
    gate_moved, down_moved, low = meet(gate_moved, down_moved, low)
    gate_sent, gate_kept = col_send(gate_own + wide(gate_moved), 1)
    down_sent, down_kept = col_add(down_kept, down_moved)
    low_moved = over_core(jnp.stack(low))
    low_moved, low, up_sent, gate_sent, down_sent = meet(low_moved, low, up_sent, gate_sent, down_sent)
    grad_mixed = [jnp.concatenate([low[which], low_moved[which]], axis=0) for which in (0, 1)]
    far_out = narrow(wide(far_out_own) + wide(far_out_moved))

    starts = jnp.concatenate([one[at : at + 8] for one in grad_mixed for at in (0, size)], axis=0)
    starts = dot_nt(starts[:, :half], out_near) + dot_nt(starts[:, half:], out_row)
    opened = jnp.concatenate([one[at : at + 8, width : 2 * width] for one in projected for at in (0, size)], axis=0)
    starts = (starts * opened).reshape(2, 2, 8, width)[:, :, :2]
    behind, grad_mixed, up_sent, gate_sent, down_sent, far_out = hop(
        over_row, starts, grad_mixed, up_sent, gate_sent, down_sent, far_out
    )
    up_moved = over_row(up_sent)
    gate_moved = col_swap(gate_sent, 1)
    down_moved = col_swap(down_sent, 2)
    out_from_far = over_x(far_out)

    def mix_back(which):
        return sequence_call(
            mix_back_kernel,
            [grad_mixed[which], projected[which], flags[which]],
            [before[which], behind[which]],
            (taps, out_near, out_row, in_near, in_row),
            ((3 * width, jnp.bfloat16),),
            ((3, width),),
        )

    grad_projected = [None, None]
    grad_projected[1], far_taps, far_one, far_one_sent = mix_back(1)
    far_one, grad_mixed = meet(far_one, grad_mixed)
    grad_projected[0], near_taps, near_one, near_one_sent = mix_back(0)
    in_own, in_sent = weight_grads(grad_projected, normed_one, width)
    out_own, out_sent = weight_grads(mixed, grad_mixed, width)
    mixer_own = jnp.concatenate([in_own, out_own], axis=0)
    mixer_sent = jnp.concatenate([in_sent, out_sent], axis=0)
    gain_one_grad = 0.0
    for rows, one in (
        (near_tokens[0], near_one), (near_tokens[1], near_one_sent), (far_tokens[0], far_one), (far_tokens[1], far_one_sent)
    ):
        rows = wide(rows)
        gain_one_grad = gain_one_grad + jnp.sum(wide(one) * (rows * norm_scale(rows)), axis=0)
    conv_local = jnp.sum(near_taps + far_taps, axis=0)
    gain_local = jnp.stack([gain_one_grad, gain_two_grad])
    conv_flat = conv_local.reshape(3, cols, channels).transpose(1, 0, 2).reshape(cols, 3 * channels)
    apart = jnp.arange(cols) ^ col
    conv_flat = jnp.take(conv_flat, apart // 2 + apart % 2 * 2, axis=0).reshape(-1)
    small = jnp.concatenate([gain_local[:, :half].reshape(-1), conv_flat, gain_local[:, half:].reshape(-1)])
    out_from_far, up_moved, gate_moved, down_moved, far_one, near_one, near_one_sent, mixer_sent, small = meet(
        out_from_far, up_moved, gate_moved, down_moved, far_one, near_one, near_one_sent, mixer_sent, small
    )
    far_one_moved, near_one_moved, small_moved, far_one, near_one, mixer_sent, up_moved, gate_moved, down_moved = meet(
        over_core(far_one_sent), over_core(near_one_sent), col_swap(small, 1),
        far_one, near_one, mixer_sent, up_moved, gate_moved, down_moved,
    )
    one_send = narrow(wide(far_one) + wide(far_one_moved))
    small = small + small_moved
    one_send, mixer_sent, small, up_moved, gate_moved, down_moved, near_one, far_one = meet(
        one_send, mixer_sent, small, up_moved, gate_moved, down_moved, near_one, far_one
    )
    one_from_far = over_x(one_send)
    mixer_moved = over_row(mixer_sent)
    small_moved = col_swap(small, 2)
    gate_sent, gate_kept = col_add(gate_kept, gate_moved)
    up_sent, up_kept = col_send(up_own + wide(up_moved), 1)
    down_own, down_sent = exchange(col_last(down_kept, down_moved))
    up_sent, gate_sent = meet(up_sent, gate_sent)
    up_moved = col_swap(up_sent, 1)
    gate_moved = col_swap(gate_sent, 2)
    result = narrow(hidden_near + (wide(near_out_own) + wide(near_out_moved) + wide(out_from_far)))
    small = small + small_moved
    one_from_far, mixer_moved, up_moved, gate_moved, near_one, result, down_sent, small = meet(
        one_from_far, mixer_moved, up_moved, gate_moved, near_one, result, down_sent, small
    )
    mixer_sent, mixer_kept = col_send(mixer_own + wide(mixer_moved), 4)
    up_sent, up_kept = col_add(up_kept, up_moved)
    gate_total = team_first(col_last(gate_kept, gate_moved))
    mixer_sent, up_sent, gate_total, one_from_far, near_one, down_sent = meet(
        mixer_sent, up_sent, gate_total, one_from_far, near_one, down_sent
    )
    mixer_moved = col_swap(mixer_sent, 1)
    up_moved = col_swap(up_sent, 2)
    gate_far = over_x(gate_total)
    kept = 2 * half + 3 * width
    sent = jnp.concatenate([small[kept:], small[2 * half : kept]])
    small = small[:kept] + over_row(sent)
    small, down_sent = meet(small, down_sent)
    down_from_row = over_row(down_sent)
    conv_own = lax.dynamic_slice_in_dim(small[2 * half :], col * 3 * channels, 3 * channels, 0)
    conv_wide = lax.dynamic_update_slice(
        jnp.zeros((TEAM * 3 * channels,), jnp.float32), conv_own, (place * 3 * channels,)
    )
    small = jnp.concatenate([small[: 2 * half], conv_wide])
    small = small + over_x(small)
    grad_normed_one = wide(near_one) + wide(near_one_moved) + wide(one_from_far)
    own_inputs = wide(near_tokens[0])
    own_scale = norm_scale(own_inputs)
    input_grad = grad_hidden[0] + norm_backward(grad_normed_one, own_inputs, own_scale, gain_one)
    mixer_moved, up_moved, gate_far, down_from_row, input_grad, small = meet(
        mixer_moved, up_moved, gate_far, down_from_row, input_grad, small
    )
    mixer_sent, mixer_kept = col_add(mixer_kept, mixer_moved)
    mixer_sent, up_moved, down_from_row, gate_far, input_grad, result, small = meet(
        mixer_sent, up_moved, down_from_row, gate_far, input_grad, result, small
    )
    mixer_moved = col_swap(mixer_sent, 2)
    up_total = team_first(col_last(up_kept, up_moved))
    down_total = team_first(down_own + wide(down_from_row))
    both = jnp.stack([up_total, down_total])
    both_far = over_x(both)
    input_row = over_row(narrow(input_grad[:, half:]))
    gate_pair = over_core(jnp.stack([gate_total, gate_far]))
    small_moved = over_core(small)
    gate_grad = assemble(gate_total, gate_far, gate_pair, True)
    small = other_teams(small + small_moved)
    conv_grad = small[2 * half :].reshape(TEAM, 3, channels).transpose(1, 0, 2).reshape(3, TEAM * channels)
    mixer_moved, both_far, gate_grad, result, conv_grad, input_row = meet(
        mixer_moved, both_far, gate_grad, result, conv_grad, input_row
    )
    mixer_total = team_first(col_last(mixer_kept, mixer_moved))
    mixer_total, both_far = meet(mixer_total, both_far)
    mixer_far = over_x(mixer_total)
    both_pair = over_core(jnp.stack([both, both_far]))
    up_grad = assemble(up_total, both_far[0], both_pair[:, 0], True)
    result_row = over_row(result[:, half:])
    mixer_far, up_grad, both_pair, input_grad = meet(
        mixer_far, up_grad, both_pair, to_blocks(input_grad[:, :half], input_row)
    )
    mixer_pair = over_core(jnp.stack([mixer_total, mixer_far]))
    down_grad = assemble(down_total, both_far[1], both_pair[:, 1], False)
    mixer_grads = team_rows(mixer_total, mixer_far, mixer_pair, 4)
    in_grad = wide(mixer_grads[:3].transpose(2, 0, 1))
    out_grad = wide(mixer_grads[3])
    return (
        to_blocks(result[:, :half], result_row),
        input_grad,
        small[:half],
        in_grad,
        conv_grad,
        out_grad,
        small[half : 2 * half],
        gate_grad,
        up_grad,
        down_grad,
    )


def solution(mesh):
    return jax.shard_map(
        body,
        mesh=mesh,
        in_specs=(
            P(("dp", "col"), "row"),
            P(("dp", "row")),
            P(("dp", "col"), "row"),
            P("row"),
            P("row", None, "col"),
            P(None, "col"),
            P("col", "row"),
            P("row"),
            P("row", "col"),
            P("row", "col"),
            P("col", "row"),
        ),
        out_specs=(
            P(("dp", "col"), "row"),
            P(("dp", "col"), "row"),
            P("row"),
            P("row", None, "col"),
            P(None, "col"),
            P("col", "row"),
            P("row"),
            P("row", "col"),
            P("row", "col"),
            P("col", "row"),
        ),
        check_vma=False,
    )
```

```python
import functools

import jax
import jax.numpy as jnp
from jax import lax
from jax.experimental import pallas as pl
from jax.experimental.pallas import tpu as pltpu
from jax.sharding import PartitionSpec as P

EPSILON = 1e-05
TEAM = 4


def dot_nt(left, right):
    return lax.dot_general(left, right, (((1,), (1,)), ((), ())), preferred_element_type=jnp.float32)


def dot_nn(left, right):
    return lax.dot_general(left, right, (((1,), (0,)), ((), ())), preferred_element_type=jnp.float32)


def dot_tn(left, right):
    return lax.dot_general(left, right, (((0,), (0,)), ((), ())), preferred_element_type=jnp.float32)


def over_dp(values, distance):
    size = lax.axis_size("dp")
    return lax.ppermute(values, "dp", [(i, i ^ distance) for i in range(size)])


def over_core(values):
    return over_dp(values, 1)


def over_x(values):
    return over_dp(values, 2)


def over_row(values):
    return lax.ppermute(values, "row", [(0, 1), (1, 0)])


def col_swap(values, distance):
    size = lax.axis_size("col")
    return lax.ppermute(values, "col", [(i, i ^ distance) for i in range(size)])


def narrow(values):
    return values.astype(jnp.bfloat16)


def wide(values):
    return values.astype(jnp.float32)


def halves(values):
    size = values.shape[0] // 2
    return values[:size], values[size:]


def other_teams(values):
    distance = TEAM
    while distance < lax.axis_size("dp"):
        values = values + over_dp(values, distance)
        distance *= 2
    return values


def after(value, *events):
    return lax.optimization_barrier((value, *events))[0]


def meet(*values):
    return lax.optimization_barrier(values)


def hop(move, value, *waiting):
    return meet(move(value), *waiting)


def stacked(pair, other, parts):
    pieces = jnp.concatenate([pair, other], axis=0)
    if parts > 1:
        pieces = pieces.reshape(4, parts, -1, pair.shape[2]).transpose(1, 0, 2, 3)
    return pieces.reshape(-1, pair.shape[2])


def col_first(piece):
    return jnp.stack([piece, col_swap(piece, 2)])


def col_send(values, parts):
    rows = values.shape[0] // (parts * 4)
    grid = values.reshape(parts, 2, 2 * rows, values.shape[1])
    return narrow(grid[:, 1]), grid[:, 0]


def col_add(kept, received):
    total = wide(kept) + wide(received)
    rows = total.shape[1] // 2
    return narrow(total[:, rows:]), total[:, :rows]


def col_last(kept, received):
    return (kept + wide(received)).reshape(-1, kept.shape[2])


def team_first(piece):
    return narrow(other_teams(piece))


def team_rows(own, far, pair, parts):
    rows, half = own.shape[0] // parts, own.shape[1]
    place = lax.axis_index("dp") % TEAM
    result = jnp.zeros((parts, TEAM * rows, half), jnp.bfloat16)
    for distance, block in enumerate((own, pair[0], far, pair[1])):
        block = block.reshape(parts, rows, half)
        result = lax.dynamic_update_slice(result, block, (0, (place ^ distance) * rows, 0))
    return result


def norm_scale(hidden):
    return lax.rsqrt(jnp.mean(hidden * hidden, axis=1, keepdims=True) + EPSILON)


def norm_backward(grad_normed, hidden, row_scale, gain_vector):
    inner_sum = jnp.sum(grad_normed * gain_vector * hidden, axis=1, keepdims=True)
    cubed = row_scale * row_scale * row_scale
    return grad_normed * gain_vector * row_scale - hidden * (cubed / hidden.shape[1]) * inner_sum


def to_blocks(values, received):
    size, half = values.shape
    row = lax.axis_index("row")
    result = jnp.zeros((2 * size, half), values.dtype)
    result = lax.dynamic_update_slice(result, values, (row * size, 0))
    return lax.dynamic_update_slice(result, received.astype(values.dtype), ((1 - row) * size, 0))


ROWS = 256
COST = pl.CostEstimate(flops=1, bytes_accessed=1, transcendentals=0)


def whole(array):
    return pl.BlockSpec(array.shape, lambda i: (0,) * array.ndim)


def row_tiles(array):
    return pl.BlockSpec((ROWS, array.shape[1]), lambda i: (i, 0))


def token_call(kernel, tiled, resident, outs):
    tokens = tiled[0].shape[0]
    shapes = [jax.ShapeDtypeStruct((tokens, columns), dtype) for columns, dtype in outs]
    return pl.pallas_call(
        kernel,
        grid=(tokens // ROWS,),
        in_specs=[row_tiles(one) for one in tiled] + [whole(one) for one in resident],
        out_specs=[row_tiles(one) for one in shapes],
        out_shape=shapes,
        compiler_params=pltpu.CompilerParams(vmem_limit_bytes=20 * 2**20),
        cost_estimate=COST,
    )(*tiled, *resident)


def split_nt(left, near, row):
    half = near.shape[1]
    return dot_nt(left[:, :half], near[...]) + dot_nt(left[:, half:], row[...])


def gated_kernel(
    normed, cotangent, gate_near, gate_row, up_near, up_row, down_near, down_row,
    act, grad_gate, grad_up, back_own, back_sent, out_own, out_sent,
):
    gate_value = split_nt(normed, gate_near, gate_row)
    up_value = split_nt(normed, up_near, up_row)
    grad_act = split_nt(cotangent, down_near, down_row)
    sigmoid_gate = jax.nn.sigmoid(gate_value)
    silu = gate_value * sigmoid_gate
    low_act = narrow(silu * up_value)
    low_gate = narrow(grad_act * up_value * (sigmoid_gate * (1.0 + gate_value * (1.0 - sigmoid_gate))))
    low_up = narrow(grad_act * silu)
    act[...] = low_act
    grad_gate[...] = low_gate
    grad_up[...] = low_up
    back = jnp.concatenate(
        [
            narrow(dot_nn(low_gate, gate_near[...]) + dot_nn(low_up, up_near[...])),
            narrow(dot_nn(low_gate, gate_row[...]) + dot_nn(low_up, up_row[...])),
        ],
        axis=1,
    )
    out = jnp.concatenate(
        [narrow(dot_nn(low_act, down_near[...])), narrow(dot_nn(low_act, down_row[...]))], axis=1
    )
    own_or_sent(back, back_own, back_sent)
    own_or_sent(out, out_own, out_sent)


def gated_call(normed, cotangent, weights):
    tokens, width = normed.shape
    units = weights[0].shape[0]
    steps = tokens // ROWS
    wide_out = jax.ShapeDtypeStruct((tokens, units), jnp.bfloat16)
    part_out = jax.ShapeDtypeStruct((tokens // 2, width), jnp.bfloat16)
    own = pl.BlockSpec((ROWS, width), lambda i: (jnp.minimum(i, steps // 2 - 1), 0))
    sent = pl.BlockSpec((ROWS, width), lambda i: (jnp.maximum(i - steps // 2, 0), 0))
    return pl.pallas_call(
        gated_kernel,
        grid=(steps,),
        in_specs=[row_tiles(normed), row_tiles(cotangent)] + [whole(one) for one in weights],
        out_specs=[row_tiles(wide_out)] * 3 + [own, sent] * 2,
        out_shape=[wide_out] * 3 + [part_out] * 4,
        compiler_params=pltpu.CompilerParams(vmem_limit_bytes=36 * 2**20),
        cost_estimate=COST,
    )(normed, cotangent, *weights)


def project_kernel(inputs, gain, in_near, in_row, normed, projected):
    values = wide(inputs[...])
    scale = lax.rsqrt(jnp.mean(values * values, axis=1, keepdims=True) + EPSILON)
    low = narrow(values * scale * gain[...])
    normed[...] = low
    projected[...] = split_nt(low, in_near, in_row)


def mixer_values(projected, flags, before, taps):
    width = taps.shape[1]
    input_gate, output_gate, values_part = (projected[:, part * width : (part + 1) * width] for part in range(3))
    mix_input = input_gate * values_part
    place = lax.broadcasted_iota(jnp.int32, mix_input.shape, 0)
    one, two = before[0, 1:2], before[0, 0:1]
    prior_one = flags[:, 0:1] * jnp.where(place == 0, one, pltpu.roll(mix_input, 1, 0))
    prior_two = jnp.where(place == 0, two, jnp.where(place == 1, one, pltpu.roll(mix_input, 2, 0)))
    prior_two = flags[:, 1:2] * prior_two
    convolved = taps[2:3] * mix_input + taps[1:2] * prior_one + taps[0:1] * prior_two
    return input_gate, output_gate, values_part, mix_input, prior_one, prior_two, convolved


def own_or_sent(partial, own, sent):
    first = pl.program_id(0) < pl.num_programs(0) // 2

    @pl.when(first)
    def _():
        own[...] = partial

    @pl.when(jnp.logical_not(first))
    def _():
        sent[...] = partial


def mix_kernel(projected, flags, before, taps, out_near, out_row, mixed, own, sent):
    _, output_gate, _, _, _, _, convolved = mixer_values(projected, flags, before, taps)
    low = narrow(output_gate * convolved)
    mixed[...] = low
    partial = narrow(jnp.concatenate([dot_nn(low, out_near[...]), dot_nn(low, out_row[...])], axis=1))
    own_or_sent(partial, own, sent)


def mix_back_kernel(
    grad_mixed, projected, flags, before, behind, taps, out_near, out_row, in_near, in_row,
    grad_projected, sums, own, sent,
):
    width = taps.shape[1]
    input_gate, output_gate, values_part, mix_input, prior_one, prior_two, convolved = mixer_values(
        projected, flags, before, taps
    )
    grad_y = split_nt(grad_mixed, out_near, out_row)
    grad_conv = grad_y * output_gate
    for tap, values in enumerate((prior_two, prior_one, mix_input)):
        sums[0, tap : tap + 1] = jnp.sum(grad_conv * values, axis=0, keepdims=True)
    size = grad_conv.shape[0]
    place = lax.broadcasted_iota(jnp.int32, grad_conv.shape, 0)
    one, two = behind[0, 0:1], behind[0, 1:2]
    next_one = jnp.where(place == size - 1, one, pltpu.roll(grad_conv, size - 1, 0))
    next_two = jnp.where(place == size - 2, one, pltpu.roll(grad_conv, size - 2, 0))
    next_two = jnp.where(place == size - 1, two, next_two)
    grad_mix = (
        taps[2:3] * grad_conv
        + taps[1:2] * (flags[:, 2:3] * next_one)
        + taps[0:1] * (flags[:, 3:4] * next_two)
    )
    low = narrow(jnp.concatenate([grad_mix * values_part, grad_y * convolved, grad_mix * input_gate], axis=1))
    grad_projected[...] = low
    partial = narrow(jnp.concatenate([dot_nn(low, in_near[...]), dot_nn(low, in_row[...])], axis=1))
    own_or_sent(partial, own, sent)


def sequence_call(kernel, tiled, small, resident, outs, small_outs=()):
    size = tiled[0].shape[0] // 2

    def by_rows(array):
        return pl.BlockSpec((size, array.shape[1]), lambda i: (i, 0))

    def by_first(array):
        return pl.BlockSpec((1, *array.shape[1:]), lambda i: (i, 0, 0))

    shapes = [jax.ShapeDtypeStruct((2 * size, columns), dtype) for columns, dtype in outs]
    part = jax.ShapeDtypeStruct((size, 2 * resident[-1].shape[1]), jnp.bfloat16)
    small_shapes = [jax.ShapeDtypeStruct((2, *shape), jnp.float32) for shape in small_outs]
    return pl.pallas_call(
        kernel,
        grid=(2,),
        in_specs=[by_rows(one) for one in tiled] + [by_first(one) for one in small] + [whole(one) for one in resident],
        out_specs=[by_rows(one) for one in shapes] + [by_first(one) for one in small_shapes] + [whole(part)] * 2,
        out_shape=shapes + small_shapes + [part] * 2,
        compiler_params=pltpu.CompilerParams(vmem_limit_bytes=32 * 2**20),
        cost_estimate=COST,
    )(*tiled, *small, *resident)


def weight_kernel(left_near, left_far, right_near, right_far, own, sent):
    total = dot_tn(left_near[...], right_near[...]) + dot_tn(left_far[...], right_far[...])
    half = own.shape[1]
    own[...] = total[:, :half]
    sent[...] = narrow(total[:, half:])


def whole_weight_kernel(left_near, left_far, right_near, right_far, out):
    out[...] = narrow(dot_tn(left_near[...], right_near[...]) + dot_tn(left_far[...], right_far[...]))


def whole_weight_grads(lefts, rights, tile):
    tokens, columns = lefts[0].shape
    width = rights[0].shape[1]
    left_spec = pl.BlockSpec((tokens, tile), lambda i: (0, i))
    return pl.pallas_call(
        whole_weight_kernel,
        grid=(columns // tile,),
        in_specs=[left_spec, left_spec, whole(rights[0]), whole(rights[1])],
        out_specs=pl.BlockSpec((tile, width), lambda i: (i, 0)),
        out_shape=jax.ShapeDtypeStruct((columns, width), jnp.bfloat16),
        compiler_params=pltpu.CompilerParams(vmem_limit_bytes=28 * 2**20),
        cost_estimate=COST,
    )(*lefts, *rights)


def weight_grads(lefts, rights, tile):
    tokens, columns = lefts[0].shape
    half = rights[0].shape[1] // 2
    left_spec = pl.BlockSpec((tokens, tile), lambda i: (0, i))
    out_spec = pl.BlockSpec((tile, half), lambda i: (i, 0))
    return pl.pallas_call(
        weight_kernel,
        grid=(columns // tile,),
        in_specs=[left_spec, left_spec, whole(rights[0]), whole(rights[1])],
        out_specs=[out_spec, out_spec],
        out_shape=[
            jax.ShapeDtypeStruct((columns, half), jnp.float32),
            jax.ShapeDtypeStruct((columns, half), jnp.bfloat16),
        ],
        compiler_params=pltpu.CompilerParams(vmem_limit_bytes=28 * 2**20),
        cost_estimate=COST,
    )(*lefts, *rights)


def assemble_kernel(turned, place, own, far, core_own, core_far, out, rows):
    count = own.shape[0]
    for distance, block in enumerate((own[...], core_own[...], far[...], core_far[...])):
        start = pl.multiple_of((place[0] ^ distance) * count, 16)
        rows[pl.ds(start, count), :] = wide(block)
    out[...] = rows[...].T if turned else rows[...]


def assemble(own, far, core_own, core_far, turned):
    count, half = own.shape
    shape = (half, TEAM * count) if turned else (TEAM * count, half)
    place = (lax.axis_index("dp") % TEAM).astype(jnp.int32).reshape(1)
    vmem = pl.BlockSpec(memory_space=pltpu.VMEM)
    return pl.pallas_call(
        functools.partial(assemble_kernel, turned),
        in_specs=[pl.BlockSpec(memory_space=pltpu.SMEM)] + [vmem] * 4,
        out_specs=vmem,
        out_shape=jax.ShapeDtypeStruct(shape, jnp.float32),
        scratch_shapes=[pltpu.VMEM((TEAM * count, half), jnp.float32)],
        compiler_params=pltpu.CompilerParams(vmem_limit_bytes=16 * 2**20),
        cost_estimate=COST,
    )(place, own, far, core_own, core_far)


def body(
    tokens,
    segment_ids,
    cotangent,
    norm1_gain,
    in_weight,
    conv_weight,
    out_weight,
    norm2_gain,
    gate_weight,
    up_weight,
    down_weight,
):
    place = lax.axis_index("dp") % TEAM
    row = lax.axis_index("row")
    col = lax.axis_index("col")
    cols = lax.axis_size("col")
    sequence = tokens.shape[0]
    size = sequence // 2
    half = tokens.shape[1]

    tokens_other = lax.dynamic_slice_in_dim(tokens, (1 - row) * size, size, 0)
    tokens_own = lax.dynamic_slice_in_dim(tokens, row * size, size, 0)
    tokens_row = over_row(tokens_other)
    tokens_x0 = over_x(tokens_own)
    channels = in_weight.shape[2] // TEAM
    hidden = gate_weight.shape[1] // TEAM
    in_part = lax.dynamic_slice_in_dim(in_weight, place * channels, channels, 2)
    in_part = in_part.transpose(1, 2, 0).reshape(3 * channels, half)
    out_part = lax.dynamic_slice_in_dim(out_weight, place * channels, channels, 0)
    taps_part = lax.dynamic_slice_in_dim(conv_weight, place * channels, channels, 1)
    taps_part = jnp.pad(taps_part, ((0, 0), (0, half - channels)))
    gains_part = jnp.pad(jnp.stack([norm1_gain, norm2_gain]), ((0, 11), (0, 0)))
    in_pair = col_first(jnp.concatenate([in_part, taps_part, gains_part, out_part], axis=0))
    grads_other = lax.dynamic_slice_in_dim(cotangent, (1 - row) * size, size, 0)
    grads_own = lax.dynamic_slice_in_dim(cotangent, row * size, size, 0)
    gate_part = lax.dynamic_slice_in_dim(gate_weight, place * hidden, hidden, 1).T
    ids_row = over_row(segment_ids)
    in_pair, tokens_row, tokens_x0, ids_row, grads_other, gate_part = meet(
        in_pair, tokens_row, tokens_x0, ids_row, grads_other, gate_part
    )

    in_other = col_swap(in_pair, 1)
    tokens_x1 = over_x(tokens_row)
    grads_row = over_row(grads_other)
    gate_pair = col_first(gate_part)
    up_part = lax.dynamic_slice_in_dim(up_weight, place * hidden, hidden, 1).T
    down_part = lax.dynamic_slice_in_dim(down_weight, place * hidden, hidden, 0)
    ids = jnp.stack([segment_ids, ids_row])
    ids = lax.dynamic_index_in_dim(ids, (col // 2) ^ row, 0, keepdims=False)
    ids = lax.dynamic_slice_in_dim(ids, (col % 2) * sequence, sequence, 0)
    ids_far = over_x(ids)
    in_other, tokens_x1, grads_row, ids_far, gate_pair, grads_own, ids, up_part, down_part = meet(
        in_other, tokens_x1, grads_row, ids_far, gate_pair, grads_own, ids, up_part, down_part
    )
    in_rows = 3 * channels
    in_near = stacked(in_pair[:, :in_rows], in_other[:, :in_rows], 3)
    in_near = jnp.concatenate([in_near, in_pair[0, in_rows : in_rows + 16]], axis=0)
    out_near = stacked(in_pair[:, in_rows + 16 :], in_other[:, in_rows + 16 :], 1)
    grads_near = jnp.concatenate([grads_own, grads_row], axis=1)
    in_near, out_near, grads_near, up_part, tokens_x1, gate_pair, ids = meet(
        in_near, out_near, grads_near, up_part, tokens_x1, gate_pair, ids
    )

    near = jnp.concatenate([tokens_own, tokens_row], axis=1)
    far = jnp.concatenate([tokens_x0, tokens_x1], axis=1)
    pair, ids_pair = over_core(jnp.stack([near, far])), over_core(jnp.stack([ids, ids_far]))
    pair, ids_pair, in_near, out_near, in_other, grads_near, gate_pair, up_part = meet(
        pair, ids_pair, in_near, out_near, in_other, grads_near, gate_pair, up_part
    )
    in_row = over_row(in_near)
    out_row = over_row(out_near)
    gate_other = col_swap(gate_pair, 1)
    up_pair = col_first(up_part)
    grads_far = over_x(grads_near)
    ids = jnp.stack([ids, ids_pair[0], ids_far, ids_pair[1]])
    keeps = []
    for offset in (1, 2):
        equal = (ids[:, offset:] == ids[:, :-offset]).astype(jnp.float32)
        keeps.append(jnp.pad(equal, ((0, 0), (offset, offset))))
    flags = jnp.stack(
        [
            lax.dynamic_slice_in_dim(keeps[which], row * size + offset, size, 1)
            for which, offset in ((0, 0), (1, 0), (0, 1), (1, 2))
        ],
        axis=2,
    )
    flags = [flags[:2].reshape(2 * size, 4), flags[2:].reshape(2 * size, 4)]
    near_tokens, far_tokens = (near, pair[0]), (far, pair[1])
    inputs = [jnp.concatenate(both, axis=0) for both in (near_tokens, far_tokens)]
    taps = jnp.concatenate(
        [both[which, in_rows : in_rows + 3, :channels] for both in (in_pair, in_other) for which in (0, 1)], axis=1
    )
    taps = wide(taps)
    in_row, out_row, gate_other, up_pair, inputs, taps, flags, down_part = meet(
        in_row, out_row, gate_other, up_pair, inputs, taps, flags, down_part
    )

    width = cols * channels
    gains = jnp.stack([norm1_gain, norm2_gain])
    gains = wide(jnp.concatenate([gains, in_row[4 * in_rows + 3 : 4 * in_rows + 5]], axis=1))
    gain_one, gain_two = gains[0], gains[1]
    in_near, in_row = in_near[: 4 * in_rows], in_row[: 4 * in_rows]
    gate_near = stacked(gate_pair, gate_other, 1)
    gate_near, up_pair, down_part, inputs = meet(gate_near, up_pair, down_part, inputs)
    gate_row = over_row(gate_near)
    up_other = col_swap(up_pair, 1)
    down_pair = col_first(down_part)
    grads_pair = over_core(jnp.stack([grads_near, grads_far]))
    ends = wide(jnp.concatenate([one[at + size - 8 : at + size] for one in inputs for at in (0, size)], axis=0))
    ends = narrow(ends * norm_scale(ends) * gain_one)
    ends = dot_nt(ends[:, :half], in_near) + dot_nt(ends[:, half:], in_row)
    ends = (ends[:, :width] * ends[:, 2 * width :]).reshape(2, 2, 8, width)[:, :, 6:]
    before = over_row(ends)
    normed_one, projected = zip(
        *[
            token_call(
                project_kernel,
                [one],
                (gain_one[None], in_near, in_row),
                ((2 * half, jnp.bfloat16), (3 * width, jnp.float32)),
            )
            for one in inputs
        ]
    )

    def mix(which):
        return sequence_call(
            mix_kernel,
            [projected[which], flags[which]],
            [before[which]],
            (taps, out_near, out_row),
            ((width, jnp.bfloat16),),
        )

    mixed = [None, None]
    mixed[1], far_own, far_sent = mix(1)
    mixed[0], near_own, near_sent = mix(0)
    up_other, down_pair, gate_row, grads_pair, far_own, far_sent, near_own, near_sent = meet(
        up_other, down_pair, gate_row, grads_pair, far_own, far_sent, near_own, near_sent
    )
    up_near = stacked(up_pair, up_other, 1)
    near_grads, far_grads = (grads_near, grads_pair[0]), (grads_far, grads_pair[1])
    cotangents = [jnp.concatenate(both, axis=0) for both in (near_grads, far_grads)]
    far_moved, near_moved, far_own, near_own, up_near, down_pair, cotangents = meet(
        over_core(far_sent), over_core(near_sent), far_own, near_own, up_near, down_pair, cotangents
    )
    far_send = narrow(wide(far_own) + wide(far_moved))
    near_send = narrow(wide(near_own) + wide(near_moved))
    from_far, to_far = over_x(far_send), over_x(near_send)
    up_row = over_row(up_near)
    down_other = col_swap(down_pair, 1)
    from_far, down_other, up_row = meet(from_far, down_other, up_row)
    down_near = stacked(down_pair, down_other, 1)
    from_far, down_near = meet(from_far, down_near)
    down_row = over_row(down_near)
    hidden_near = wide(near_tokens[0]) + (wide(near_own) + wide(near_moved) + wide(from_far))
    scale_near = norm_scale(hidden_near)
    normed_own = narrow(hidden_near * scale_near * gain_two)
    to_far, normed_own = meet(to_far, normed_own)
    hidden_far = wide(far_tokens[0]) + (wide(far_own) + wide(far_moved) + wide(to_far))
    scale_far = norm_scale(hidden_far)
    normed_x = narrow(hidden_far * scale_far * gain_two)
    down_row, normed_own, normed_x = meet(down_row, normed_own, normed_x)
    (pair,) = hop(over_core, jnp.stack([normed_own, normed_x]))
    normed_near = jnp.concatenate([normed_own, pair[0]], axis=0)
    normed_far = jnp.concatenate([normed_x, pair[1]], axis=0)
    hiddens, scale_two, normed_two = (hidden_near, hidden_far), (scale_near, scale_far), (normed_near, normed_far)
    units = gate_near.shape[0]
    weights = (gate_near, gate_row, up_near, up_row, down_near, down_row)

    def exchange(partial):
        return partial[:, :half], narrow(partial[:, half:])

    act, grad_gate, grad_up = [None, None], [None, None], [None, None]
    act[0], grad_gate[0], grad_up[0], near_own, near_sent, near_out_own, near_out_sent = gated_call(
        normed_near, cotangents[0], weights
    )
    near_moved, near_own, normed_far = hop(over_core, near_sent, near_own, normed_far)
    near_send, normed_far = meet(narrow(wide(near_own) + wide(near_moved)), normed_far)
    back_to_far = over_x(near_send)
    act[1], grad_gate[1], grad_up[1], far_own, far_sent, far_out_own, far_out_sent = gated_call(
        normed_far, cotangents[1], weights
    )
    normed_two = [normed_near, normed_far]
    back_to_far, far_own, far_sent, grad_gate, grad_up, act = meet(
        back_to_far, far_own, far_sent, grad_gate, grad_up, act
    )
    far_moved, far_own, grad_gate, grad_up, act = hop(over_core, far_sent, far_own, grad_gate, grad_up, act)
    far_send, grad_gate, grad_up, act = meet(narrow(wide(far_own) + wide(far_moved)), grad_gate, grad_up, act)
    back_from_far = over_x(far_send)
    near_out_moved, far_out_moved = over_core(near_out_sent), over_core(far_out_sent)
    down_sent, down_kept = col_send(whole_weight_grads(act, cotangents, units // 3), 1)
    down_moved = col_swap(down_sent, 1)
    down_sent, grad_gate, grad_up = meet(down_sent, grad_gate, grad_up)
    gate_own, gate_sent = weight_grads(grad_gate, normed_two, units // 3)
    gate_moved = over_row(gate_sent)
    gate_sent, grad_up = meet(gate_sent, grad_up)
    up_own, up_sent = weight_grads(grad_up, normed_two, units // 3)
    back_from_far, up_sent, near_out_moved, far_out_moved = meet(
        back_from_far, up_sent, near_out_moved, far_out_moved
    )

    back_sums = (
        wide(near_own) + wide(near_moved) + wide(back_from_far),
        wide(far_own) + wide(far_moved) + wide(back_to_far),
    )
    grad_hidden, low = [], []
    for which, cotangent_rows in ((0, near_grads[0]), (1, far_grads[0])):
        grads = wide(cotangent_rows) + norm_backward(
            back_sums[which], hiddens[which], scale_two[which], gain_two
        )
        grad_hidden.append(grads)
        low.append(narrow(grads))
    gain_two_grad = jnp.sum(back_sums[0] * hidden_near * scale_two[0], axis=0)
    gate_moved, down_moved, low = meet(gate_moved, down_moved, low)
    gate_sent, gate_kept = col_send(gate_own + wide(gate_moved), 1)
    down_sent, down_kept = col_add(down_kept, down_moved)
    low_moved = over_core(jnp.stack(low))
    low_moved, low, up_sent, gate_sent, down_sent = meet(low_moved, low, up_sent, gate_sent, down_sent)
    grad_mixed = [jnp.concatenate([low[which], low_moved[which]], axis=0) for which in (0, 1)]
    far_out = narrow(wide(far_out_own) + wide(far_out_moved))

    starts = jnp.concatenate([one[at : at + 8] for one in grad_mixed for at in (0, size)], axis=0)
    starts = dot_nt(starts[:, :half], out_near) + dot_nt(starts[:, half:], out_row)
    opened = jnp.concatenate([one[at : at + 8, width : 2 * width] for one in projected for at in (0, size)], axis=0)
    starts = (starts * opened).reshape(2, 2, 8, width)[:, :, :2]
    behind, grad_mixed, up_sent, gate_sent, down_sent, far_out = hop(
        over_row, starts, grad_mixed, up_sent, gate_sent, down_sent, far_out
    )
    up_moved = over_row(up_sent)
    gate_moved = col_swap(gate_sent, 1)
    down_moved = col_swap(down_sent, 2)
    out_from_far = over_x(far_out)

    def mix_back(which):
        return sequence_call(
            mix_back_kernel,
            [grad_mixed[which], projected[which], flags[which]],
            [before[which], behind[which]],
            (taps, out_near, out_row, in_near, in_row),
            ((3 * width, jnp.bfloat16),),
            ((3, width),),
        )

    grad_projected = [None, None]
    grad_projected[1], far_taps, far_one, far_one_sent = mix_back(1)
    far_one, grad_mixed = meet(far_one, grad_mixed)
    grad_projected[0], near_taps, near_one, near_one_sent = mix_back(0)
    in_own, in_sent = weight_grads(grad_projected, normed_one, width)
    out_own, out_sent = weight_grads(mixed, grad_mixed, width)
    mixer_own = jnp.concatenate([in_own, out_own], axis=0)
    mixer_sent = jnp.concatenate([in_sent, out_sent], axis=0)
    gain_one_grad = 0.0
    for rows, one in (
        (near_tokens[0], near_one), (near_tokens[1], near_one_sent), (far_tokens[0], far_one), (far_tokens[1], far_one_sent)
    ):
        rows = wide(rows)
        gain_one_grad = gain_one_grad + jnp.sum(wide(one) * (rows * norm_scale(rows)), axis=0)
    conv_local = jnp.sum(near_taps + far_taps, axis=0)
    gain_local = jnp.stack([gain_one_grad, gain_two_grad])
    conv_flat = conv_local.reshape(3, cols, channels).transpose(1, 0, 2).reshape(cols, 3 * channels)
    apart = jnp.arange(cols) ^ col
    conv_flat = jnp.take(conv_flat, apart // 2 + apart % 2 * 2, axis=0).reshape(-1)
    small = jnp.concatenate([gain_local[:, :half].reshape(-1), conv_flat, gain_local[:, half:].reshape(-1)])
    out_from_far, up_moved, gate_moved, down_moved, far_one, near_one, near_one_sent, mixer_sent, small = meet(
        out_from_far, up_moved, gate_moved, down_moved, far_one, near_one, near_one_sent, mixer_sent, small
    )
    far_one_moved, near_one_moved, small_moved, far_one, near_one, mixer_sent, up_moved, gate_moved, down_moved = meet(
        over_core(far_one_sent), over_core(near_one_sent), col_swap(small, 1),
        far_one, near_one, mixer_sent, up_moved, gate_moved, down_moved,
    )
    one_send = narrow(wide(far_one) + wide(far_one_moved))
    small = small + small_moved
    one_send, mixer_sent, small, up_moved, gate_moved, down_moved, near_one, far_one = meet(
        one_send, mixer_sent, small, up_moved, gate_moved, down_moved, near_one, far_one
    )
    one_from_far = over_x(one_send)
    mixer_moved = over_row(mixer_sent)
    small_moved = col_swap(small, 2)
    gate_sent, gate_kept = col_add(gate_kept, gate_moved)
    up_sent, up_kept = col_send(up_own + wide(up_moved), 1)
    down_own, down_sent = exchange(col_last(down_kept, down_moved))
    up_sent, gate_sent = meet(up_sent, gate_sent)
    up_moved = col_swap(up_sent, 1)
    gate_moved = col_swap(gate_sent, 2)
    result = narrow(hidden_near + (wide(near_out_own) + wide(near_out_moved) + wide(out_from_far)))
    small = small + small_moved
    one_from_far, mixer_moved, up_moved, gate_moved, near_one, result, down_sent, small = meet(
        one_from_far, mixer_moved, up_moved, gate_moved, near_one, result, down_sent, small
    )
    mixer_sent, mixer_kept = col_send(mixer_own + wide(mixer_moved), 4)
    up_sent, up_kept = col_add(up_kept, up_moved)
    gate_total = team_first(col_last(gate_kept, gate_moved))
    mixer_sent, up_sent, gate_total, one_from_far, near_one, down_sent = meet(
        mixer_sent, up_sent, gate_total, one_from_far, near_one, down_sent
    )
    mixer_moved = col_swap(mixer_sent, 1)
    up_moved = col_swap(up_sent, 2)
    gate_far = over_x(gate_total)
    kept = 2 * half + 3 * width
    sent = jnp.concatenate([small[kept:], small[2 * half : kept]])
    small = small[:kept] + over_row(sent)
    small, down_sent = meet(small, down_sent)
    down_from_row = over_row(down_sent)
    conv_own = lax.dynamic_slice_in_dim(small[2 * half :], col * 3 * channels, 3 * channels, 0)
    conv_wide = lax.dynamic_update_slice(
        jnp.zeros((TEAM * 3 * channels,), jnp.float32), conv_own, (place * 3 * channels,)
    )
    small = jnp.concatenate([small[: 2 * half], conv_wide])
    small = small + over_x(small)
    grad_normed_one = wide(near_one) + wide(near_one_moved) + wide(one_from_far)
    own_inputs = wide(near_tokens[0])
    own_scale = norm_scale(own_inputs)
    input_grad = grad_hidden[0] + norm_backward(grad_normed_one, own_inputs, own_scale, gain_one)
    mixer_moved, up_moved, gate_far, down_from_row, input_grad, small = meet(
        mixer_moved, up_moved, gate_far, down_from_row, input_grad, small
    )
    mixer_sent, mixer_kept = col_add(mixer_kept, mixer_moved)
    mixer_sent, up_moved, down_from_row, gate_far, input_grad, result, small = meet(
        mixer_sent, up_moved, down_from_row, gate_far, input_grad, result, small
    )
    mixer_moved = col_swap(mixer_sent, 2)
    up_total = team_first(col_last(up_kept, up_moved))
    down_total = team_first(down_own + wide(down_from_row))
    up_far, down_far = over_x(up_total), over_x(down_total)
    input_row = over_row(narrow(input_grad[:, half:]))
    small_moved = over_core(small)
    gate_grad = assemble(gate_total, gate_far, over_core(gate_total), over_core(gate_far), True)
    small = other_teams(small + small_moved)
    conv_grad = small[2 * half :].reshape(TEAM, 3, channels).transpose(1, 0, 2).reshape(3, TEAM * channels)
    mixer_moved, up_far, down_far, gate_grad, result, conv_grad, input_row = meet(
        mixer_moved, up_far, down_far, gate_grad, result, conv_grad, input_row
    )
    mixer_total = team_first(col_last(mixer_kept, mixer_moved))
    mixer_total, up_far, down_far, result = meet(mixer_total, up_far, down_far, result)
    mixer_far = over_x(mixer_total)
    mixer_core = over_core(mixer_total)
    result_row = over_row(result[:, half:])
    up_grad = assemble(up_total, up_far, over_core(up_total), over_core(up_far), True)
    mixer_far, mixer_core, up_grad, input_grad = meet(
        mixer_far, mixer_core, up_grad, to_blocks(input_grad[:, :half], input_row)
    )
    mixer_grads = team_rows(mixer_total, mixer_far, (mixer_core, over_core(mixer_far)), 4)
    down_grad = assemble(down_total, down_far, over_core(down_total), over_core(down_far), False)
    in_grad = wide(mixer_grads[:3].transpose(2, 0, 1))
    out_grad = wide(mixer_grads[3])
    return (
        to_blocks(result[:, :half], result_row),
        input_grad,
        small[:half],
        in_grad,
        conv_grad,
        out_grad,
        small[half : 2 * half],
        gate_grad,
        up_grad,
        down_grad,
    )


def solution(mesh):
    return jax.shard_map(
        body,
        mesh=mesh,
        in_specs=(
            P(("dp", "col"), "row"),
            P(("dp", "row")),
            P(("dp", "col"), "row"),
            P("row"),
            P("row", None, "col"),
            P(None, "col"),
            P("col", "row"),
            P("row"),
            P("row", "col"),
            P("row", "col"),
            P("col", "row"),
        ),
        out_specs=(
            P(("dp", "col"), "row"),
            P(("dp", "col"), "row"),
            P("row"),
            P("row", None, "col"),
            P(None, "col"),
            P("col", "row"),
            P("row"),
            P("row", "col"),
            P("row", "col"),
            P("col", "row"),
        ),
        check_vma=False,
    )
```

```python
import functools

import jax
import jax.numpy as jnp
from jax import lax
from jax.experimental import pallas as pl
from jax.experimental.pallas import tpu as pltpu
from jax.sharding import PartitionSpec as P

EPSILON = 1e-05
TEAM = 4


def dot_nt(left, right):
    return lax.dot_general(left, right, (((1,), (1,)), ((), ())), preferred_element_type=jnp.float32)


def dot_nn(left, right):
    return lax.dot_general(left, right, (((1,), (0,)), ((), ())), preferred_element_type=jnp.float32)


def dot_tn(left, right):
    return lax.dot_general(left, right, (((0,), (0,)), ((), ())), preferred_element_type=jnp.float32)


def over_dp(values, distance):
    size = lax.axis_size("dp")
    return lax.ppermute(values, "dp", [(i, i ^ distance) for i in range(size)])


def over_core(values):
    return over_dp(values, 1)


def over_x(values):
    return over_dp(values, 2)


def over_row(values):
    return lax.ppermute(values, "row", [(0, 1), (1, 0)])


def col_swap(values, distance):
    size = lax.axis_size("col")
    return lax.ppermute(values, "col", [(i, i ^ distance) for i in range(size)])


def narrow(values):
    return values.astype(jnp.bfloat16)


def wide(values):
    return values.astype(jnp.float32)


def halves(values):
    size = values.shape[0] // 2
    return values[:size], values[size:]


def other_teams(values):
    distance = TEAM
    while distance < lax.axis_size("dp"):
        values = values + over_dp(values, distance)
        distance *= 2
    return values


def after(value, *events):
    return lax.optimization_barrier((value, *events))[0]


def meet(*values):
    return lax.optimization_barrier(values)


def hop(move, value, *waiting):
    return meet(move(value), *waiting)


def stacked(pair, other, parts):
    pieces = jnp.concatenate([pair, other], axis=0)
    if parts > 1:
        pieces = pieces.reshape(4, parts, -1, pair.shape[2]).transpose(1, 0, 2, 3)
    return pieces.reshape(-1, pair.shape[2])


def col_first(piece):
    return jnp.stack([piece, col_swap(piece, 2)])


def col_send(values, parts):
    rows = values.shape[0] // (parts * 4)
    grid = values.reshape(parts, 2, 2 * rows, values.shape[1])
    return narrow(grid[:, 1]), grid[:, 0]


def col_add(kept, received):
    total = wide(kept) + wide(received)
    rows = total.shape[1] // 2
    return narrow(total[:, rows:]), total[:, :rows]


def col_last(kept, received):
    return (kept + wide(received)).reshape(-1, kept.shape[2])


def team_first(piece):
    return narrow(other_teams(piece))


def team_rows(own, far, pair, parts):
    rows, half = own.shape[0] // parts, own.shape[1]
    place = lax.axis_index("dp") % TEAM
    result = jnp.zeros((parts, TEAM * rows, half), jnp.bfloat16)
    for distance, block in enumerate((own, pair[0], far, pair[1])):
        block = block.reshape(parts, rows, half)
        result = lax.dynamic_update_slice(result, block, (0, (place ^ distance) * rows, 0))
    return result


def norm_scale(hidden):
    return lax.rsqrt(jnp.mean(hidden * hidden, axis=1, keepdims=True) + EPSILON)


def norm_backward(grad_normed, hidden, row_scale, gain_vector):
    inner_sum = jnp.sum(grad_normed * gain_vector * hidden, axis=1, keepdims=True)
    cubed = row_scale * row_scale * row_scale
    return grad_normed * gain_vector * row_scale - hidden * (cubed / hidden.shape[1]) * inner_sum


def to_blocks(values, received):
    size, half = values.shape
    row = lax.axis_index("row")
    result = jnp.zeros((2 * size, half), values.dtype)
    result = lax.dynamic_update_slice(result, values, (row * size, 0))
    return lax.dynamic_update_slice(result, received.astype(values.dtype), ((1 - row) * size, 0))


ROWS = 256
COST = pl.CostEstimate(flops=1, bytes_accessed=1, transcendentals=0)


def whole(array):
    return pl.BlockSpec(array.shape, lambda i: (0,) * array.ndim)


def row_tiles(array):
    return pl.BlockSpec((ROWS, array.shape[1]), lambda i: (i, 0))


def token_call(kernel, tiled, resident, outs):
    tokens = tiled[0].shape[0]
    shapes = [jax.ShapeDtypeStruct((tokens, columns), dtype) for columns, dtype in outs]
    return pl.pallas_call(
        kernel,
        grid=(tokens // ROWS,),
        in_specs=[row_tiles(one) for one in tiled] + [whole(one) for one in resident],
        out_specs=[row_tiles(one) for one in shapes],
        out_shape=shapes,
        compiler_params=pltpu.CompilerParams(vmem_limit_bytes=20 * 2**20),
        cost_estimate=COST,
    )(*tiled, *resident)


def split_nt(left, near, row):
    half = near.shape[1]
    return dot_nt(left[:, :half], near[...]) + dot_nt(left[:, half:], row[...])


def gated_kernel(
    normed, cotangent, gate_near, gate_row, up_near, up_row, down_near, down_row,
    act, grad_gate, grad_up, back_own, back_sent, out_own, out_sent,
):
    gate_value = split_nt(normed, gate_near, gate_row)
    up_value = split_nt(normed, up_near, up_row)
    grad_act = split_nt(cotangent, down_near, down_row)
    sigmoid_gate = jax.nn.sigmoid(gate_value)
    silu = gate_value * sigmoid_gate
    low_act = narrow(silu * up_value)
    low_gate = narrow(grad_act * up_value * (sigmoid_gate * (1.0 + gate_value * (1.0 - sigmoid_gate))))
    low_up = narrow(grad_act * silu)
    act[...] = low_act
    grad_gate[...] = low_gate
    grad_up[...] = low_up
    back = jnp.concatenate(
        [
            narrow(dot_nn(low_gate, gate_near[...]) + dot_nn(low_up, up_near[...])),
            narrow(dot_nn(low_gate, gate_row[...]) + dot_nn(low_up, up_row[...])),
        ],
        axis=1,
    )
    out = jnp.concatenate(
        [narrow(dot_nn(low_act, down_near[...])), narrow(dot_nn(low_act, down_row[...]))], axis=1
    )
    own_or_sent(back, back_own, back_sent)
    own_or_sent(out, out_own, out_sent)


def gated_call(normed, cotangent, weights):
    tokens, width = normed.shape
    units = weights[0].shape[0]
    steps = tokens // ROWS
    wide_out = jax.ShapeDtypeStruct((tokens, units), jnp.bfloat16)
    part_out = jax.ShapeDtypeStruct((tokens // 2, width), jnp.bfloat16)
    own = pl.BlockSpec((ROWS, width), lambda i: (jnp.minimum(i, steps // 2 - 1), 0))
    sent = pl.BlockSpec((ROWS, width), lambda i: (jnp.maximum(i - steps // 2, 0), 0))
    return pl.pallas_call(
        gated_kernel,
        grid=(steps,),
        in_specs=[row_tiles(normed), row_tiles(cotangent)] + [whole(one) for one in weights],
        out_specs=[row_tiles(wide_out)] * 3 + [own, sent] * 2,
        out_shape=[wide_out] * 3 + [part_out] * 4,
        compiler_params=pltpu.CompilerParams(vmem_limit_bytes=32 * 2**20),
        cost_estimate=COST,
    )(normed, cotangent, *weights)


def project_kernel(inputs, gain, in_near, in_row, normed, projected):
    values = wide(inputs[...])
    scale = lax.rsqrt(jnp.mean(values * values, axis=1, keepdims=True) + EPSILON)
    low = narrow(values * scale * gain[...])
    normed[...] = low
    projected[...] = split_nt(low, in_near, in_row)


def mixer_values(projected, flags, before, taps):
    width = taps.shape[1]
    input_gate, output_gate, values_part = (projected[:, part * width : (part + 1) * width] for part in range(3))
    mix_input = input_gate * values_part
    place = lax.broadcasted_iota(jnp.int32, mix_input.shape, 0)
    one, two = before[0, 1:2], before[0, 0:1]
    prior_one = flags[:, 0:1] * jnp.where(place == 0, one, pltpu.roll(mix_input, 1, 0))
    prior_two = jnp.where(place == 0, two, jnp.where(place == 1, one, pltpu.roll(mix_input, 2, 0)))
    prior_two = flags[:, 1:2] * prior_two
    convolved = taps[2:3] * mix_input + taps[1:2] * prior_one + taps[0:1] * prior_two
    return input_gate, output_gate, values_part, mix_input, prior_one, prior_two, convolved


def own_or_sent(partial, own, sent):
    first = pl.program_id(0) < pl.num_programs(0) // 2

    @pl.when(first)
    def _():
        own[...] = partial

    @pl.when(jnp.logical_not(first))
    def _():
        sent[...] = partial


def mix_kernel(projected, flags, before, taps, out_near, out_row, mixed, own, sent):
    _, output_gate, _, _, _, _, convolved = mixer_values(projected, flags, before, taps)
    low = narrow(output_gate * convolved)
    mixed[...] = low
    partial = narrow(jnp.concatenate([dot_nn(low, out_near[...]), dot_nn(low, out_row[...])], axis=1))
    own_or_sent(partial, own, sent)


def mix_back_kernel(
    grad_mixed, projected, flags, before, behind, taps, out_near, out_row, in_near, in_row,
    grad_projected, sums, own, sent,
):
    width = taps.shape[1]
    input_gate, output_gate, values_part, mix_input, prior_one, prior_two, convolved = mixer_values(
        projected, flags, before, taps
    )
    grad_y = split_nt(grad_mixed, out_near, out_row)
    grad_conv = grad_y * output_gate
    for tap, values in enumerate((prior_two, prior_one, mix_input)):
        sums[0, tap : tap + 1] = jnp.sum(grad_conv * values, axis=0, keepdims=True)
    size = grad_conv.shape[0]
    place = lax.broadcasted_iota(jnp.int32, grad_conv.shape, 0)
    one, two = behind[0, 0:1], behind[0, 1:2]
    next_one = jnp.where(place == size - 1, one, pltpu.roll(grad_conv, size - 1, 0))
    next_two = jnp.where(place == size - 2, one, pltpu.roll(grad_conv, size - 2, 0))
    next_two = jnp.where(place == size - 1, two, next_two)
    grad_mix = (
        taps[2:3] * grad_conv
        + taps[1:2] * (flags[:, 2:3] * next_one)
        + taps[0:1] * (flags[:, 3:4] * next_two)
    )
    low = narrow(jnp.concatenate([grad_mix * values_part, grad_y * convolved, grad_mix * input_gate], axis=1))
    grad_projected[...] = low
    partial = narrow(jnp.concatenate([dot_nn(low, in_near[...]), dot_nn(low, in_row[...])], axis=1))
    own_or_sent(partial, own, sent)


def sequence_call(kernel, tiled, small, resident, outs, small_outs=()):
    size = tiled[0].shape[0] // 2

    def by_rows(array):
        return pl.BlockSpec((size, array.shape[1]), lambda i: (i, 0))

    def by_first(array):
        return pl.BlockSpec((1, *array.shape[1:]), lambda i: (i, 0, 0))

    shapes = [jax.ShapeDtypeStruct((2 * size, columns), dtype) for columns, dtype in outs]
    part = jax.ShapeDtypeStruct((size, 2 * resident[-1].shape[1]), jnp.bfloat16)
    small_shapes = [jax.ShapeDtypeStruct((2, *shape), jnp.float32) for shape in small_outs]
    return pl.pallas_call(
        kernel,
        grid=(2,),
        in_specs=[by_rows(one) for one in tiled] + [by_first(one) for one in small] + [whole(one) for one in resident],
        out_specs=[by_rows(one) for one in shapes] + [by_first(one) for one in small_shapes] + [whole(part)] * 2,
        out_shape=shapes + small_shapes + [part] * 2,
        compiler_params=pltpu.CompilerParams(vmem_limit_bytes=32 * 2**20),
        cost_estimate=COST,
    )(*tiled, *small, *resident)


def weight_kernel(left_near, left_far, right_near, right_far, own, sent):
    total = dot_tn(left_near[...], right_near[...]) + dot_tn(left_far[...], right_far[...])
    half = own.shape[1]
    own[...] = total[:, :half]
    sent[...] = narrow(total[:, half:])


def whole_weight_kernel(left_near, left_far, right_near, right_far, out):
    out[...] = narrow(dot_tn(left_near[...], right_near[...]) + dot_tn(left_far[...], right_far[...]))


def whole_weight_grads(lefts, rights, tile):
    tokens, columns = lefts[0].shape
    width = rights[0].shape[1]
    left_spec = pl.BlockSpec((tokens, tile), lambda i: (0, i))
    return pl.pallas_call(
        whole_weight_kernel,
        grid=(columns // tile,),
        in_specs=[left_spec, left_spec, whole(rights[0]), whole(rights[1])],
        out_specs=pl.BlockSpec((tile, width), lambda i: (i, 0)),
        out_shape=jax.ShapeDtypeStruct((columns, width), jnp.bfloat16),
        compiler_params=pltpu.CompilerParams(vmem_limit_bytes=22 * 2**20),
        cost_estimate=COST,
    )(*lefts, *rights)


def weight_grads(lefts, rights, tile):
    tokens, columns = lefts[0].shape
    half = rights[0].shape[1] // 2
    left_spec = pl.BlockSpec((tokens, tile), lambda i: (0, i))
    out_spec = pl.BlockSpec((tile, half), lambda i: (i, 0))
    return pl.pallas_call(
        weight_kernel,
        grid=(columns // tile,),
        in_specs=[left_spec, left_spec, whole(rights[0]), whole(rights[1])],
        out_specs=[out_spec, out_spec],
        out_shape=[
            jax.ShapeDtypeStruct((columns, half), jnp.float32),
            jax.ShapeDtypeStruct((columns, half), jnp.bfloat16),
        ],
        compiler_params=pltpu.CompilerParams(vmem_limit_bytes=22 * 2**20),
        cost_estimate=COST,
    )(*lefts, *rights)


def assemble_kernel(turned, place, own, far, core_own, core_far, out, rows):
    count = own.shape[0]
    for distance, block in enumerate((own[...], core_own[...], far[...], core_far[...])):
        start = pl.multiple_of((place[0] ^ distance) * count, 16)
        rows[pl.ds(start, count), :] = wide(block)
    out[...] = rows[...].T if turned else rows[...]


def assemble(own, far, core_own, core_far, turned):
    count, half = own.shape
    shape = (half, TEAM * count) if turned else (TEAM * count, half)
    place = (lax.axis_index("dp") % TEAM).astype(jnp.int32).reshape(1)
    vmem = pl.BlockSpec(memory_space=pltpu.VMEM)
    return pl.pallas_call(
        functools.partial(assemble_kernel, turned),
        in_specs=[pl.BlockSpec(memory_space=pltpu.SMEM)] + [vmem] * 4,
        out_specs=vmem,
        out_shape=jax.ShapeDtypeStruct(shape, jnp.float32),
        scratch_shapes=[pltpu.VMEM((TEAM * count, half), jnp.float32)],
        compiler_params=pltpu.CompilerParams(vmem_limit_bytes=16 * 2**20),
        cost_estimate=COST,
    )(place, own, far, core_own, core_far)


def body(
    tokens,
    segment_ids,
    cotangent,
    norm1_gain,
    in_weight,
    conv_weight,
    out_weight,
    norm2_gain,
    gate_weight,
    up_weight,
    down_weight,
):
    place = lax.axis_index("dp") % TEAM
    row = lax.axis_index("row")
    col = lax.axis_index("col")
    cols = lax.axis_size("col")
    sequence = tokens.shape[0]
    size = sequence // 2
    half = tokens.shape[1]

    tokens_other = lax.dynamic_slice_in_dim(tokens, (1 - row) * size, size, 0)
    tokens_own = lax.dynamic_slice_in_dim(tokens, row * size, size, 0)
    tokens_row = over_row(tokens_other)
    tokens_x0 = over_x(tokens_own)
    channels = in_weight.shape[2] // TEAM
    hidden = gate_weight.shape[1] // TEAM
    in_part = lax.dynamic_slice_in_dim(in_weight, place * channels, channels, 2)
    in_part = in_part.transpose(1, 2, 0).reshape(3 * channels, half)
    out_part = lax.dynamic_slice_in_dim(out_weight, place * channels, channels, 0)
    taps_part = lax.dynamic_slice_in_dim(conv_weight, place * channels, channels, 1)
    taps_part = jnp.pad(taps_part, ((0, 0), (0, half - channels)))
    gains_part = jnp.pad(jnp.stack([norm1_gain, norm2_gain]), ((0, 11), (0, 0)))
    in_pair = col_first(jnp.concatenate([in_part, taps_part, gains_part, out_part], axis=0))
    grads_other = lax.dynamic_slice_in_dim(cotangent, (1 - row) * size, size, 0)
    grads_own = lax.dynamic_slice_in_dim(cotangent, row * size, size, 0)
    gate_part = lax.dynamic_slice_in_dim(gate_weight, place * hidden, hidden, 1).T
    ids_row = over_row(segment_ids)
    in_pair, tokens_row, tokens_x0, ids_row, grads_other, gate_part = meet(
        in_pair, tokens_row, tokens_x0, ids_row, grads_other, gate_part
    )

    in_other = col_swap(in_pair, 1)
    tokens_x1 = over_x(tokens_row)
    grads_row = over_row(grads_other)
    gate_pair = col_first(gate_part)
    up_part = lax.dynamic_slice_in_dim(up_weight, place * hidden, hidden, 1).T
    down_part = lax.dynamic_slice_in_dim(down_weight, place * hidden, hidden, 0)
    ids = jnp.stack([segment_ids, ids_row])
    ids = lax.dynamic_index_in_dim(ids, (col // 2) ^ row, 0, keepdims=False)
    ids = lax.dynamic_slice_in_dim(ids, (col % 2) * sequence, sequence, 0)
    ids_far = over_x(ids)
    in_other, tokens_x1, grads_row, ids_far, gate_pair, grads_own, ids, up_part, down_part = meet(
        in_other, tokens_x1, grads_row, ids_far, gate_pair, grads_own, ids, up_part, down_part
    )
    in_rows = 3 * channels
    in_near = stacked(in_pair[:, :in_rows], in_other[:, :in_rows], 3)
    in_near = jnp.concatenate([in_near, in_pair[0, in_rows : in_rows + 16]], axis=0)
    out_near = stacked(in_pair[:, in_rows + 16 :], in_other[:, in_rows + 16 :], 1)
    grads_near = jnp.concatenate([grads_own, grads_row], axis=1)
    in_near, out_near, grads_near, up_part, tokens_x1, gate_pair, ids = meet(
        in_near, out_near, grads_near, up_part, tokens_x1, gate_pair, ids
    )

    near = jnp.concatenate([tokens_own, tokens_row], axis=1)
    far = jnp.concatenate([tokens_x0, tokens_x1], axis=1)
    pair, ids_pair = over_core(jnp.stack([near, far])), over_core(jnp.stack([ids, ids_far]))
    pair, ids_pair, in_near, out_near, in_other, grads_near, gate_pair, up_part = meet(
        pair, ids_pair, in_near, out_near, in_other, grads_near, gate_pair, up_part
    )
    in_row = over_row(in_near)
    out_row = over_row(out_near)
    gate_other = col_swap(gate_pair, 1)
    up_pair = col_first(up_part)
    grads_far = over_x(grads_near)
    ids = jnp.stack([ids, ids_pair[0], ids_far, ids_pair[1]])
    keeps = []
    for offset in (1, 2):
        equal = (ids[:, offset:] == ids[:, :-offset]).astype(jnp.float32)
        keeps.append(jnp.pad(equal, ((0, 0), (offset, offset))))
    flags = jnp.stack(
        [
            lax.dynamic_slice_in_dim(keeps[which], row * size + offset, size, 1)
            for which, offset in ((0, 0), (1, 0), (0, 1), (1, 2))
        ],
        axis=2,
    )
    flags = [flags[:2].reshape(2 * size, 4), flags[2:].reshape(2 * size, 4)]
    near_tokens, far_tokens = (near, pair[0]), (far, pair[1])
    inputs = [jnp.concatenate(both, axis=0) for both in (near_tokens, far_tokens)]
    taps = jnp.concatenate(
        [both[which, in_rows : in_rows + 3, :channels] for both in (in_pair, in_other) for which in (0, 1)], axis=1
    )
    taps = wide(taps)
    in_row, out_row, gate_other, up_pair, inputs, taps, flags, down_part = meet(
        in_row, out_row, gate_other, up_pair, inputs, taps, flags, down_part
    )

    width = cols * channels
    gains = jnp.stack([norm1_gain, norm2_gain])
    gains = wide(jnp.concatenate([gains, in_row[4 * in_rows + 3 : 4 * in_rows + 5]], axis=1))
    gain_one, gain_two = gains[0], gains[1]
    in_near, in_row = in_near[: 4 * in_rows], in_row[: 4 * in_rows]
    gate_near = stacked(gate_pair, gate_other, 1)
    gate_near, up_pair, down_part, inputs = meet(gate_near, up_pair, down_part, inputs)
    gate_row = over_row(gate_near)
    up_other = col_swap(up_pair, 1)
    down_pair = col_first(down_part)
    grads_pair = over_core(jnp.stack([grads_near, grads_far]))
    ends = wide(jnp.concatenate([one[at + size - 8 : at + size] for one in inputs for at in (0, size)], axis=0))
    ends = narrow(ends * norm_scale(ends) * gain_one)
    ends = dot_nt(ends[:, :half], in_near) + dot_nt(ends[:, half:], in_row)
    ends = (ends[:, :width] * ends[:, 2 * width :]).reshape(2, 2, 8, width)[:, :, 6:]
    before = over_row(ends)
    normed_one, projected = zip(
        *[
            token_call(
                project_kernel,
                [one],
                (gain_one[None], in_near, in_row),
                ((2 * half, jnp.bfloat16), (3 * width, jnp.float32)),
            )
            for one in inputs
        ]
    )

    def mix(which):
        return sequence_call(
            mix_kernel,
            [projected[which], flags[which]],
            [before[which]],
            (taps, out_near, out_row),
            ((width, jnp.bfloat16),),
        )

    mixed = [None, None]
    mixed[1], far_own, far_sent = mix(1)
    mixed[0], near_own, near_sent = mix(0)
    up_other, down_pair, gate_row, grads_pair, far_own, far_sent, near_own, near_sent = meet(
        up_other, down_pair, gate_row, grads_pair, far_own, far_sent, near_own, near_sent
    )
    up_near = stacked(up_pair, up_other, 1)
    near_grads, far_grads = (grads_near, grads_pair[0]), (grads_far, grads_pair[1])
    cotangents = [jnp.concatenate(both, axis=0) for both in (near_grads, far_grads)]
    far_moved, near_moved, far_own, near_own, up_near, down_pair, cotangents = meet(
        over_core(far_sent), over_core(near_sent), far_own, near_own, up_near, down_pair, cotangents
    )
    far_send = narrow(wide(far_own) + wide(far_moved))
    near_send = narrow(wide(near_own) + wide(near_moved))
    from_far, to_far = over_x(far_send), over_x(near_send)
    up_row = over_row(up_near)
    down_other = col_swap(down_pair, 1)
    from_far, down_other, up_row = meet(from_far, down_other, up_row)
    down_near = stacked(down_pair, down_other, 1)
    from_far, down_near = meet(from_far, down_near)
    down_row = over_row(down_near)
    hidden_near = wide(near_tokens[0]) + (wide(near_own) + wide(near_moved) + wide(from_far))
    scale_near = norm_scale(hidden_near)
    normed_own = narrow(hidden_near * scale_near * gain_two)
    to_far, normed_own = meet(to_far, normed_own)
    hidden_far = wide(far_tokens[0]) + (wide(far_own) + wide(far_moved) + wide(to_far))
    scale_far = norm_scale(hidden_far)
    normed_x = narrow(hidden_far * scale_far * gain_two)
    down_row, normed_own, normed_x = meet(down_row, normed_own, normed_x)
    (pair,) = hop(over_core, jnp.stack([normed_own, normed_x]))
    normed_near = jnp.concatenate([normed_own, pair[0]], axis=0)
    normed_far = jnp.concatenate([normed_x, pair[1]], axis=0)
    hiddens, scale_two, normed_two = (hidden_near, hidden_far), (scale_near, scale_far), (normed_near, normed_far)
    units = gate_near.shape[0]
    weights = (gate_near, gate_row, up_near, up_row, down_near, down_row)

    def exchange(partial):
        return partial[:, :half], narrow(partial[:, half:])

    act, grad_gate, grad_up = [None, None], [None, None], [None, None]
    act[0], grad_gate[0], grad_up[0], near_own, near_sent, near_out_own, near_out_sent = gated_call(
        normed_near, cotangents[0], weights
    )
    near_moved, near_own, normed_far = hop(over_core, near_sent, near_own, normed_far)
    near_send, normed_far = meet(narrow(wide(near_own) + wide(near_moved)), normed_far)
    back_to_far = over_x(near_send)
    act[1], grad_gate[1], grad_up[1], far_own, far_sent, far_out_own, far_out_sent = gated_call(
        normed_far, cotangents[1], weights
    )
    normed_two = [normed_near, normed_far]
    back_to_far, far_own, far_sent, grad_gate, grad_up, act = meet(
        back_to_far, far_own, far_sent, grad_gate, grad_up, act
    )
    far_moved, far_own, grad_gate, grad_up, act = hop(over_core, far_sent, far_own, grad_gate, grad_up, act)
    far_send, grad_gate, grad_up, act = meet(narrow(wide(far_own) + wide(far_moved)), grad_gate, grad_up, act)
    back_from_far = over_x(far_send)
    near_out_moved, far_out_moved = over_core(near_out_sent), over_core(far_out_sent)
    down_sent, down_kept = col_send(whole_weight_grads(act, cotangents, units // 3), 1)
    down_moved = col_swap(down_sent, 1)
    down_sent, grad_gate, grad_up = meet(down_sent, grad_gate, grad_up)
    gate_own, gate_sent = weight_grads(grad_gate, normed_two, units // 3)
    gate_moved = over_row(gate_sent)
    gate_sent, grad_up = meet(gate_sent, grad_up)
    up_own, up_sent = weight_grads(grad_up, normed_two, units // 3)
    back_from_far, up_sent, near_out_moved, far_out_moved = meet(
        back_from_far, up_sent, near_out_moved, far_out_moved
    )

    back_sums = (
        wide(near_own) + wide(near_moved) + wide(back_from_far),
        wide(far_own) + wide(far_moved) + wide(back_to_far),
    )
    grad_hidden, low = [], []
    for which, cotangent_rows in ((0, near_grads[0]), (1, far_grads[0])):
        grads = wide(cotangent_rows) + norm_backward(
            back_sums[which], hiddens[which], scale_two[which], gain_two
        )
        grad_hidden.append(grads)
        low.append(narrow(grads))
    gain_two_grad = jnp.sum(back_sums[0] * hidden_near * scale_two[0], axis=0)
    gate_moved, down_moved, low = meet(gate_moved, down_moved, low)
    gate_sent, gate_kept = col_send(gate_own + wide(gate_moved), 1)
    down_sent, down_kept = col_add(down_kept, down_moved)
    low_moved = over_core(jnp.stack(low))
    low_moved, low, up_sent, gate_sent, down_sent = meet(low_moved, low, up_sent, gate_sent, down_sent)
    grad_mixed = [jnp.concatenate([low[which], low_moved[which]], axis=0) for which in (0, 1)]
    far_out = narrow(wide(far_out_own) + wide(far_out_moved))

    starts = jnp.concatenate([one[at : at + 8] for one in grad_mixed for at in (0, size)], axis=0)
    starts = dot_nt(starts[:, :half], out_near) + dot_nt(starts[:, half:], out_row)
    opened = jnp.concatenate([one[at : at + 8, width : 2 * width] for one in projected for at in (0, size)], axis=0)
    starts = (starts * opened).reshape(2, 2, 8, width)[:, :, :2]
    behind, grad_mixed, up_sent, gate_sent, down_sent, far_out = hop(
        over_row, starts, grad_mixed, up_sent, gate_sent, down_sent, far_out
    )
    up_moved = over_row(up_sent)
    gate_moved = col_swap(gate_sent, 1)
    down_moved = col_swap(down_sent, 2)
    out_from_far = over_x(far_out)

    def mix_back(which):
        return sequence_call(
            mix_back_kernel,
            [grad_mixed[which], projected[which], flags[which]],
            [before[which], behind[which]],
            (taps, out_near, out_row, in_near, in_row),
            ((3 * width, jnp.bfloat16),),
            ((3, width),),
        )

    grad_projected = [None, None]
    grad_projected[1], far_taps, far_one, far_one_sent = mix_back(1)
    far_one, grad_mixed = meet(far_one, grad_mixed)
    grad_projected[0], near_taps, near_one, near_one_sent = mix_back(0)
    in_own, in_sent = weight_grads(grad_projected, normed_one, width)
    out_own, out_sent = weight_grads(mixed, grad_mixed, width)
    mixer_own = jnp.concatenate([in_own, out_own], axis=0)
    mixer_sent = jnp.concatenate([in_sent, out_sent], axis=0)
    gain_one_grad = 0.0
    for rows, one in (
        (near_tokens[0], near_one), (near_tokens[1], near_one_sent), (far_tokens[0], far_one), (far_tokens[1], far_one_sent)
    ):
        rows = wide(rows)
        gain_one_grad = gain_one_grad + jnp.sum(wide(one) * (rows * norm_scale(rows)), axis=0)
    conv_local = jnp.sum(near_taps + far_taps, axis=0)
    gain_local = jnp.stack([gain_one_grad, gain_two_grad])
    conv_flat = conv_local.reshape(3, cols, channels).transpose(1, 0, 2).reshape(cols, 3 * channels)
    apart = jnp.arange(cols) ^ col
    conv_flat = jnp.take(conv_flat, apart // 2 + apart % 2 * 2, axis=0).reshape(-1)
    small = jnp.concatenate([gain_local[:, :half].reshape(-1), conv_flat, gain_local[:, half:].reshape(-1)])
    out_from_far, up_moved, gate_moved, down_moved, far_one, near_one, near_one_sent, mixer_sent, small = meet(
        out_from_far, up_moved, gate_moved, down_moved, far_one, near_one, near_one_sent, mixer_sent, small
    )
    far_one_moved, near_one_moved, small_moved, far_one, near_one, mixer_sent, up_moved, gate_moved, down_moved = meet(
        over_core(far_one_sent), over_core(near_one_sent), col_swap(small, 1),
        far_one, near_one, mixer_sent, up_moved, gate_moved, down_moved,
    )
    one_send = narrow(wide(far_one) + wide(far_one_moved))
    small = small + small_moved
    one_send, mixer_sent, small, up_moved, gate_moved, down_moved, near_one, far_one = meet(
        one_send, mixer_sent, small, up_moved, gate_moved, down_moved, near_one, far_one
    )
    one_from_far = over_x(one_send)
    mixer_moved = over_row(mixer_sent)
    small_moved = col_swap(small, 2)
    gate_sent, gate_kept = col_add(gate_kept, gate_moved)
    up_sent, up_kept = col_send(up_own + wide(up_moved), 1)
    down_own, down_sent = exchange(col_last(down_kept, down_moved))
    up_sent, gate_sent = meet(up_sent, gate_sent)
    up_moved = col_swap(up_sent, 1)
    gate_moved = col_swap(gate_sent, 2)
    result = narrow(hidden_near + (wide(near_out_own) + wide(near_out_moved) + wide(out_from_far)))
    small = small + small_moved
    one_from_far, mixer_moved, up_moved, gate_moved, near_one, result, down_sent, small = meet(
        one_from_far, mixer_moved, up_moved, gate_moved, near_one, result, down_sent, small
    )
    mixer_sent, mixer_kept = col_send(mixer_own + wide(mixer_moved), 4)
    up_sent, up_kept = col_add(up_kept, up_moved)
    gate_total = team_first(col_last(gate_kept, gate_moved))
    mixer_sent, up_sent, gate_total, one_from_far, near_one, down_sent = meet(
        mixer_sent, up_sent, gate_total, one_from_far, near_one, down_sent
    )
    mixer_moved = col_swap(mixer_sent, 1)
    up_moved = col_swap(up_sent, 2)
    gate_far = over_x(gate_total)
    kept = 2 * half + 3 * width
    sent = jnp.concatenate([small[kept:], small[2 * half : kept]])
    small = small[:kept] + over_row(sent)
    small, down_sent = meet(small, down_sent)
    down_from_row = over_row(down_sent)
    conv_own = lax.dynamic_slice_in_dim(small[2 * half :], col * 3 * channels, 3 * channels, 0)
    conv_wide = lax.dynamic_update_slice(
        jnp.zeros((TEAM * 3 * channels,), jnp.float32), conv_own, (place * 3 * channels,)
    )
    small = jnp.concatenate([small[: 2 * half], conv_wide])
    small = small + over_x(small)
    grad_normed_one = wide(near_one) + wide(near_one_moved) + wide(one_from_far)
    own_inputs = wide(near_tokens[0])
    own_scale = norm_scale(own_inputs)
    input_grad = grad_hidden[0] + norm_backward(grad_normed_one, own_inputs, own_scale, gain_one)
    mixer_moved, up_moved, gate_far, down_from_row, input_grad, small = meet(
        mixer_moved, up_moved, gate_far, down_from_row, input_grad, small
    )
    mixer_sent, mixer_kept = col_add(mixer_kept, mixer_moved)
    mixer_sent, up_moved, down_from_row, gate_far, input_grad, result, small = meet(
        mixer_sent, up_moved, down_from_row, gate_far, input_grad, result, small
    )
    mixer_moved = col_swap(mixer_sent, 2)
    up_total = team_first(col_last(up_kept, up_moved))
    down_total = team_first(down_own + wide(down_from_row))
    up_far, down_far = over_x(up_total), over_x(down_total)
    input_row = over_row(narrow(input_grad[:, half:]))
    small_moved = over_core(small)
    gate_grad = assemble(gate_total, gate_far, over_core(gate_total), over_core(gate_far), True)
    small = other_teams(small + small_moved)
    conv_grad = small[2 * half :].reshape(TEAM, 3, channels).transpose(1, 0, 2).reshape(3, TEAM * channels)
    mixer_moved, up_far, down_far, gate_grad, result, conv_grad, input_row = meet(
        mixer_moved, up_far, down_far, gate_grad, result, conv_grad, input_row
    )
    mixer_total = team_first(col_last(mixer_kept, mixer_moved))
    mixer_total, up_far, down_far, result = meet(mixer_total, up_far, down_far, result)
    mixer_far = over_x(mixer_total)
    mixer_core = over_core(mixer_total)
    result_row = over_row(result[:, half:])
    up_grad = assemble(up_total, up_far, over_core(up_total), over_core(up_far), True)
    mixer_far, mixer_core, up_grad, input_grad = meet(
        mixer_far, mixer_core, up_grad, to_blocks(input_grad[:, :half], input_row)
    )
    mixer_grads = team_rows(mixer_total, mixer_far, (mixer_core, over_core(mixer_far)), 4)
    down_grad = assemble(down_total, down_far, over_core(down_total), over_core(down_far), False)
    in_grad = wide(mixer_grads[:3].transpose(2, 0, 1))
    out_grad = wide(mixer_grads[3])
    return (
        to_blocks(result[:, :half], result_row),
        input_grad,
        small[:half],
        in_grad,
        conv_grad,
        out_grad,
        small[half : 2 * half],
        gate_grad,
        up_grad,
        down_grad,
    )


def solution(mesh):
    return jax.shard_map(
        body,
        mesh=mesh,
        in_specs=(
            P(("dp", "col"), "row"),
            P(("dp", "row")),
            P(("dp", "col"), "row"),
            P("row"),
            P("row", None, "col"),
            P(None, "col"),
            P("col", "row"),
            P("row"),
            P("row", "col"),
            P("row", "col"),
            P("col", "row"),
        ),
        out_specs=(
            P(("dp", "col"), "row"),
            P(("dp", "col"), "row"),
            P("row"),
            P("row", None, "col"),
            P(None, "col"),
            P("col", "row"),
            P("row"),
            P("row", "col"),
            P("row", "col"),
            P("col", "row"),
        ),
        check_vma=False,
    )
```
